32 devices in a mesh: gx: 4 (over y, core), gy: 8 (over z, x).
Axes of the slice: x: 2, y: 2, z: 4, core: 2. Of those that a mesh axis runs over, the one named last changes fastest.
Arguments:
- right_side: float32 [32, 128, 256], P('gx', 'gy'), may hold values from -8 to 8
- velocity: float32 [3, 32, 128, 256], P(None, 'gx', 'gy'), may hold values from 0.1 to 3
- deflation: bfloat16 [32, 32, 128, 256], P(None, 'gx', 'gy'), may hold values from -0.1875 to 0.1875
- inverse_rows: float32 [1024, 1024], P(('gx', 'gy')), may hold values from -0.1875 to 0.1875
Outputs:
- solution_field: float32 [32, 128, 256], P('gx', 'gy')
- residual: float32 [32, 128, 256], P('gx', 'gy')
The draws below stay inside these ranges and needn't reach their ends.
All inputs are finite; a program needn't handle non-finite values.
Results may differ from the reference program's by a relative error of at most 0.005.
Values sent between devices are 32-bit elements; how exact they have to be, the bound alone decides.
No kernel may reach another device: no remote copies, remote signals or barrier semaphores. Data moves between devices by JAX's collectives and lax.ppermute only.
A program may use at most 64 MiB of HBM per device.

```python
import math
import jax
import jax.numpy as jnp
from jax import lax

CX = 8
CY = 16
NZ = 256
KD = 32
DEPTH = 2
CHEB = 4
NX = 32
NY = 128
KC = 1024
N_GX = 4
N_GY = 8


def level_of(key, extent, split, low, top_value):
    def one(position, parts):
        steps = jax.random.uniform(jax.random.fold_in(jax.random.fold_in(key, 6), position), (parts,), jnp.float32, low / len(split), top_value / len(split))
        return jnp.repeat(jnp.exp(steps), extent[position] // parts).reshape((-1,) + (1,) * (len(extent) - position - 1))

    level = one(*split[0])
    for cut in split[1:]:
        level = level * one(*cut)
    return level


def gaussian(key, extent, width, most, split=(), kind=jnp.bfloat16):
    array = width * jax.random.normal(key, extent, jnp.float32)
    if split:
        array = array * level_of(key, extent, split, -0.22, 0.18)
    return jnp.clip(array, -most, most).astype(kind)


def setup_inputs(seed: int = 0) -> dict:
    arg_keys = jax.random.split(jax.random.key(seed), 5)
    right_side = gaussian(arg_keys[0], (NX, NY, NZ), 1.0, 8.0, ((0, 4), (1, 8)), jnp.float32)
    velocity = jnp.clip(jnp.exp(math.log(3.0) - 3.4011974 * jax.random.uniform(arg_keys[1], (3, NX, NY, NZ), jnp.float32) ** level_of(arg_keys[1], (3, NX, NY, NZ), ((1, 4), (2, 8)), -0.2, 0.2)), 0.1, 3.0)
    deflation = gaussian(arg_keys[2], (KD, NX, NY, NZ), ((KD * CX * CY * NZ) ** -0.25), 0.1875, ((1, 4), (2, 8)))
    inverse_rows = gaussian(arg_keys[3], (KC, KC), KC ** -0.5, 0.1875, ((0, 32),), jnp.float32)
    return dict(right_side=right_side, velocity=velocity, deflation=deflation, inverse_rows=inverse_rows)


cheb_center = 1.0
cheb_radius = 0.9


def upwind(padded, velocity):
    centre = padded[1:-1, 1:-1, 1:-1]
    diagonal = 6.0 + velocity[0] + velocity[1] + velocity[2]
    beside = padded[2:, 1:-1, 1:-1] + (1.0 + velocity[0]) * padded[:-2, 1:-1, 1:-1]
    beside = beside + padded[1:-1, 2:, 1:-1] + (1.0 + velocity[1]) * padded[1:-1, :-2, 1:-1]
    beside = beside + padded[1:-1, 1:-1, 2:] + (1.0 + velocity[2]) * padded[1:-1, 1:-1, :-2]
    return diagonal * centre - beside


def box_apply(field, velocity):
    return upwind(jnp.pad(field, 1), velocity)


def chebyshev(source, velocity, inside):
    inverse_diag = 1.0 / (6.0 + velocity[0] + velocity[1] + velocity[2])
    sigma_ratio = cheb_center / cheb_radius
    rho_now = 1.0 / sigma_ratio
    update = inverse_diag * source / cheb_center * inside
    estimate = update
    remainder = source
    for sweep_index in range(CHEB - 1):
        remainder = remainder - box_apply(update, velocity)
        rho_next = 1.0 / (2.0 * sigma_ratio - rho_now)
        update = (rho_next * rho_now * update + (2.0 * rho_next / cheb_radius) * inverse_diag * remainder) * inside
        estimate = estimate + update
        rho_now = rho_next
    return estimate


def assemble(blocks):
    return blocks.reshape(N_GX, N_GY, CX, CY, NZ).transpose(0, 2, 1, 3, 4).reshape(CX * N_GX, CY * N_GY, NZ)


def precondition(residual, velocity, deflation, inverse_rows):
    count = N_GX * N_GY
    numbers = jnp.arange(count, dtype=jnp.int32)
    rounded = residual.astype(jnp.bfloat16)
    zero = jnp.zeros((), jnp.int32)

    def local_vectors(number):
        start_x = (number // N_GY * CX).astype(jnp.int32)
        start_y = (number % N_GY * CY).astype(jnp.int32)
        local = lax.dynamic_slice(deflation, (zero, start_x, start_y, zero), (KD, CX, CY, NZ))
        return local.reshape(KD, CX * CY * NZ), start_x, start_y

    def restrict_one(number):
        local, start_x, start_y = local_vectors(number)
        piece = lax.dynamic_slice(rounded, (start_x, start_y, zero), (CX, CY, NZ)).reshape(CX * CY * NZ)
        return jnp.dot(local, piece, preferred_element_type=jnp.float32)

    coarse = lax.map(restrict_one, numbers).reshape(count * KD)
    solved = jnp.dot(inverse_rows, coarse, precision=lax.Precision.HIGHEST).astype(jnp.bfloat16)
    solved = solved.reshape(count, KD)

    def prolong_one(item):
        number, weights = item
        local, start_x, start_y = local_vectors(number)
        return jnp.dot(weights, local, preferred_element_type=jnp.float32).reshape(CX, CY, NZ)

    correction = assemble(lax.map(prolong_one, (numbers, solved)))
    remaining = residual - box_apply(correction, velocity)
    padded_rest = jnp.pad(remaining, ((DEPTH, DEPTH), (DEPTH, DEPTH), (0, 0)))
    padded_vel = jnp.pad(velocity, ((0, 0), (DEPTH, DEPTH), (DEPTH, DEPTH), (0, 0)))
    padded_in = jnp.pad(jnp.ones((CX * N_GX, CY * N_GY, 1), residual.dtype), ((DEPTH, DEPTH), (DEPTH, DEPTH), (0, 0)))
    wide_x = CX + 2 * DEPTH
    wide_y = CY + 2 * DEPTH

    def smooth_one(number):
        start_x = (number // N_GY * CX).astype(jnp.int32)
        start_y = (number % N_GY * CY).astype(jnp.int32)
        source = lax.dynamic_slice(padded_rest, (start_x, start_y, zero), (wide_x, wide_y, NZ))
        vel_box = lax.dynamic_slice(padded_vel, (zero, start_x, start_y, zero), (3, wide_x, wide_y, NZ))
        inside = lax.dynamic_slice(padded_in, (start_x, start_y, zero), (wide_x, wide_y, 1))
        estimate = chebyshev(source, vel_box, inside)
        return estimate[DEPTH:DEPTH + CX, DEPTH:DEPTH + CY]

    return correction + assemble(lax.map(smooth_one, numbers))


def reference(right_side, velocity, deflation, inverse_rows):
    residual = right_side
    rho_now = jnp.sum(residual * residual)
    search = precondition(residual, velocity, deflation, inverse_rows)
    image = box_apply(search, velocity)
    alpha_step = rho_now / jnp.sum(residual * image)
    middle = residual - alpha_step * image
    smoothed = precondition(middle, velocity, deflation, inverse_rows)
    turned = box_apply(smoothed, velocity)
    omega_step = jnp.sum(turned * middle) / jnp.sum(turned * turned)
    solution_field = alpha_step * search + omega_step * smoothed
    return solution_field, middle - omega_step * turned
```

```python
import functools

import jax
import jax.numpy as jnp
from jax import lax
from jax.experimental import pallas as pl
from jax.experimental.pallas import tpu as pltpu
from jax.sharding import PartitionSpec as P

DEPTH = 2
CHEB = 4
WIDE = 4
LANES = 128
AXES = ("gx", "gy")
F32 = jnp.float32
HIGHEST = lax.Precision.HIGHEST
PARAMS = pltpu.CompilerParams(vmem_limit_bytes=24 * 1024 * 1024)

cheb_center = 1.0
cheb_radius = 0.9

ODD_X, ODD_Y, LOW_X, HIGH_X, LOW_Y, HIGH_Y, SLOT = range(7)
OWN_LOW, PAST_LOW, PAST_HIGH, OWN_HIGH = 3, 4, 5, 6


def pair_permutations(count_x, count_y):
    def number(i, j):
        return i * count_y + j

    even_x, odd_x, even_y, odd_y = [], [], [], []
    for i in range(count_x):
        for j in range(count_y):
            here = number(i, j)
            even_x.append((here, number(i ^ 1, j)))
            even_y.append((here, number(i, j ^ 1)))
            other = ((i - 1) ^ 1) + 1
            odd_x.append((here, number(other, j) if 0 <= other < count_x else number(i, j ^ 1)))
            other = ((j - 1) ^ 1) + 1
            odd_y.append((here, number(i, other) if 0 <= other < count_y else number(i ^ 1, j)))
    return (even_x, odd_x), (even_y, odd_y)


def call(body, outs, scratch, *args):
    specs = [pl.BlockSpec(memory_space=pltpu.SMEM)] + [pl.BlockSpec(memory_space=pltpu.VMEM)] * (len(args) - 1)
    return pl.pallas_call(
        body,
        out_shape=[jax.ShapeDtypeStruct(shape, F32) for shape in outs],
        in_specs=specs,
        out_specs=[pl.BlockSpec(memory_space=pltpu.VMEM)] * len(outs),
        scratch_shapes=[pltpu.VMEM(shape, F32) for shape in scratch],
        compiler_params=PARAMS,
    )(*args)


def rows_of(plane):
    return lax.broadcasted_iota(jnp.int32, plane.shape, 0)


def z_before(plane):
    return pltpu.roll(plane, 1, 1)


def z_after(plane, keep_last):
    return jnp.where(keep_last, pltpu.roll(plane, plane.shape[1] - 1, 1), 0.0)


def stencil(before, here, after, diagonal, c0, c1, c2, keep_last):
    rows = here.shape[0]
    out = diagonal * here
    if after is not None:
        out = out - after
    if before is not None:
        out = out - c0 * before
    out = out - pltpu.roll(here, rows - 1, 0) - c1 * pltpu.roll(here, 1, 0)
    return out - z_after(here, keep_last) - c2 * z_before(here)


def lane_masks(shape):
    lanes = lax.broadcasted_iota(jnp.int32, shape, 1)
    return lanes > 0, lanes < shape[1] - 1


def restrict(vectors, field, sums, flags, send):
    count, size_x, size_y, size_z = vectors.shape
    stage = send[1]
    stage[...] = jnp.zeros_like(stage)

    def lanes_of(total):
        total = jnp.sum(total, axis=0, keepdims=True)
        return functools.reduce(jnp.add, [total[:, k : k + LANES] for k in range(0, size_z, LANES)])

    offset = pl.multiple_of(flags[SLOT] * count, count)
    for j in range(count):
        total = vectors[j, 0].astype(F32) * field[0]
        for x in range(1, size_x):
            total = total + vectors[j, x].astype(F32) * field[x]
        stage[pl.ds(offset + j, 1), :] = lanes_of(total)
    for k, total in enumerate(sums):
        stage[LANES + k : LANES + k + 1, :] = lanes_of(total)
    write_row(stage, send[0])


def write_row(stage, out):
    row = lax.dot_general(
        jnp.ones((8, LANES), F32), stage[...], (((1,), (1,)), ((), ())), precision=HIGHEST, preferred_element_type=F32
    )
    for k in range(0, out.shape[0], 8):
        out[k : k + 8, :] = row


def gathered(received):
    count = received.shape[0]
    return received[:, :LANES], jnp.sum(received[:, LANES:], axis=0, keepdims=True)


def solve(coarse, inverse, vectors):
    count = coarse.shape[0]
    share = LANES // vectors.shape[0]
    groups = count // share
    pick = (
        lax.broadcasted_iota(jnp.int32, (groups, count), 1) // share
        == lax.broadcasted_iota(jnp.int32, (groups, count), 0)
    ).astype(F32)
    packed = jnp.dot(pick, coarse, precision=HIGHEST, preferred_element_type=F32)
    total = inverse[:, :LANES] * packed[0:1]
    for k in range(1, groups):
        total = total + inverse[:, k * LANES : (k + 1) * LANES] * packed[k : k + 1]
    return jnp.sum(total, axis=1, keepdims=True).astype(jnp.bfloat16).astype(F32)


def prolong(solved, vectors, corr):
    count, size_x, size_y, size_z = vectors.shape
    totals = [jnp.zeros((size_y, size_z), F32) for _ in range(size_x)]
    for j in range(count):
        weight = jnp.broadcast_to(solved[j : j + 1], (size_y, size_z))
        for x in range(size_x):
            totals[x] = totals[x] + vectors[j, x].astype(F32) * weight
    for x in range(size_x):
        corr[x] = totals[x]


def subtract_own(field, corr, velocity, out):
    size_x, size_y, size_z = corr.shape
    keep_first, keep_last = lane_masks((size_y, size_z))
    rows = lax.broadcasted_iota(jnp.int32, (size_y, size_z), 0)
    for x in range(size_x):
        v0, v1, v2 = velocity[0, x], velocity[1, x], velocity[2, x]
        here = corr[x]
        image = (6.0 + v0 + v1 + v2) * here
        if x + 1 < size_x:
            image = image - corr[x + 1]
        if x > 0:
            image = image - (1.0 + v0) * corr[x - 1]
        image = image - jnp.where(rows < size_y - 1, pltpu.roll(here, size_y - 1, 0), 0.0)
        image = image - (1.0 + v1) * jnp.where(rows > 0, pltpu.roll(here, 1, 0), 0.0)
        image = image - z_after(here, keep_last) - (1.0 + v2) * jnp.where(keep_first, z_before(here), 0.0)
        out[x] = field[x] - image


def write_y_message(out, field, corr, high):
    size_x, size_y, _ = corr.shape
    start = size_y - WIDE if high else 0
    for k in range(WIDE):
        for x in range(size_x):
            out[k, x : x + 1, :] = field[x, start + k : start + k + 1, :]
    edge = size_y - 1 if high else 0
    for x in range(size_x):
        out[WIDE, x : x + 1, :] = corr[x, edge : edge + 1, :]
    out[WIDE + 1, 0:WIDE, :] = corr[0, start : start + WIDE, :]
    out[WIDE + 1, WIDE : 2 * WIDE, :] = corr[size_x - 1, start : start + WIDE, :]


def by_parity(odd, write, even_out, odd_out):
    @pl.when(odd == 0)
    def _():
        write(even_out, True)
        write(odd_out, False)

    @pl.when(odd != 0)
    def _():
        write(even_out, False)
        write(odd_out, True)


def first_kernel(flags, field, vectors, out, stage):
    square = field[0] * field[0]
    for x in range(1, field.shape[0]):
        square = square + field[x] * field[x]
    rounded = [field[x].astype(jnp.bfloat16).astype(F32) for x in range(field.shape[0])]
    restrict(vectors, rounded, [square], flags, (out, stage))


def velocity_faces_kernel(flags, velocity, even_out, odd_out):
    _, size_x, size_y, _ = velocity.shape

    def write(out, high):
        start = size_y - WIDE if high else 0
        for d in range(3):
            for k in range(WIDE):
                for x in range(size_x):
                    out[d * WIDE + k, x : x + 1, :] = velocity[d, x, start + k : start + k + 1, :]

    by_parity(flags[ODD_Y], write, even_out, odd_out)


def velocity_wide_kernel(flags, velocity, even_in, odd_in, wide, even_out, odd_out):
    _, size_x, size_y, _ = velocity.shape

    def place(low, high):
        for d in range(3):
            for x in range(size_x):
                wide[d, x, WIDE : WIDE + size_y, :] = velocity[d, x]
                for k in range(WIDE):
                    wide[d, x, k : k + 1, :] = low[d * WIDE + k, x : x + 1, :]
                    row = WIDE + size_y + k
                    wide[d, x, row : row + 1, :] = high[d * WIDE + k, x : x + 1, :]

    @pl.when(flags[ODD_Y] == 0)
    def _():
        place(odd_in, even_in)

    @pl.when(flags[ODD_Y] != 0)
    def _():
        place(even_in, odd_in)

    def write(out, high):
        start = size_x - WIDE if high else 0
        for d in range(3):
            for k in range(WIDE):
                out[d * WIDE + k] = wide[d, start + k]

    by_parity(flags[ODD_X], write, even_out, odd_out)


def coarse_kernel(flags, received, inverse, vectors, field, velocity, corr, rest, even_out, odd_out):
    coarse, _ = gathered(received)
    prolong(solve(coarse, inverse, vectors), vectors, corr)
    subtract_own(field, corr, velocity, rest)
    by_parity(flags[ODD_Y], lambda out, high: write_y_message(out, rest, corr, high), even_out, odd_out)


def second_coarse_kernel(
    flags, received, second, inverse, vectors, field, image, velocity, corr, rest, middle, alpha, even_out, odd_out
):
    coarse, squares = gathered(received)
    coarse_image, products = gathered(second)
    step = jnp.broadcast_to(squares[:, 0:1] / products[:, 0:1], alpha.shape)
    alpha[...] = step
    step = step[0:1, 0:1]
    for x in range(field.shape[0]):
        middle[x] = field[x] - step * image[x]
    prolong(solve(coarse - step * coarse_image, inverse, vectors), vectors, corr)
    subtract_own(middle, corr, velocity, rest)
    by_parity(flags[ODD_Y], lambda out, high: write_y_message(out, rest, corr, high), even_out, odd_out)


def extend_kernel(flags, rest, corr, even_in, odd_in, wide, sides, even_out, odd_out):
    size_x, size_y, size_z = rest.shape
    rows = size_y + 2 * WIDE

    def place(low, high):
        has_low, has_high = flags[LOW_Y] != 0, flags[HIGH_Y] != 0
        past_low = jnp.where(has_low, low[WIDE], 0.0)
        past_high = jnp.where(has_high, high[WIDE], 0.0)
        for x in range(size_x):
            wide[x, WIDE : WIDE + size_y, :] = rest[x]
            for k in range(WIDE):
                wide[x, k : k + 1, :] = low[k, x : x + 1, :]
                wide[x, WIDE + size_y + k : WIDE + size_y + k + 1, :] = high[k, x : x + 1, :]
            wide[x, rows : rows + 8, :] = jnp.zeros((8, size_z), F32)
            wide[x, rows + OWN_LOW : rows + OWN_LOW + 1, :] = corr[x, 0:1, :]
            wide[x, rows + PAST_LOW : rows + PAST_LOW + 1, :] = past_low[x : x + 1]
            wide[x, rows + PAST_HIGH : rows + PAST_HIGH + 1, :] = past_high[x : x + 1]
            wide[x, rows + OWN_HIGH : rows + OWN_HIGH + 1, :] = corr[x, size_y - 1 : size_y, :]
        for side, x in enumerate((0, size_x - 1)):
            first = side * WIDE
            sides[side, 0:WIDE, :] = low[WIDE + 1, first : first + WIDE, :]
            sides[side, WIDE : WIDE + size_y, :] = corr[x]
            sides[side, WIDE + size_y : rows, :] = high[WIDE + 1, first : first + WIDE, :]
            sides[side, rows : rows + 8, :] = jnp.zeros((8, size_z), F32)

    @pl.when(flags[ODD_Y] == 0)
    def _():
        place(odd_in, even_in)

    @pl.when(flags[ODD_Y] != 0)
    def _():
        place(even_in, odd_in)

    def write(out, high):
        start = size_x - WIDE if high else 0
        for k in range(WIDE):
            out[k] = wide[start + k]
        out[WIDE] = sides[1 if high else 0]

    by_parity(flags[ODD_X], write, even_out, odd_out)


def chebyshev(planes, tile, weight_of, source, left, update, coefs, keep_last, wanted):
    c0, c1, c2, diagonal = coefs
    sigma = cheb_center / cheb_radius
    rho = 1.0 / sigma
    first, last = planes[0], planes[-1]
    estimate = {}
    for x in planes:
        left[x, tile] = source[x, tile]
        value = weight_of(x) * source[x, tile]
        update[0, x, tile] = value
        if x in wanted:
            estimate[x] = value
    for sweep in range(1, CHEB):
        rest = CHEB - 1 - sweep
        low, high = max(first, wanted[0] - rest), min(last, wanted[-1] + rest)
        rho_next = 1.0 / (2.0 * sigma - rho)
        now, later = (sweep + 1) % 2, sweep % 2
        for x in range(low, high + 1):
            here = update[now, x, tile]
            before = update[now, x - 1, tile] if x > first else None
            after = update[now, x + 1, tile] if x < last else None
            remainder = left[x, tile] - stencil(
                before, here, after, diagonal[x, tile], c0[x, tile], c1[x, tile], c2[x, tile], keep_last
            )
            if rest:
                left[x, tile] = remainder
            value = rho_next * rho * here + (2.0 * rho_next / cheb_radius) * (weight_of(x) * remainder)
            if rest:
                update[later, x, tile] = value
            if x in wanted:
                estimate[x] = estimate[x] + value
        rho = rho_next
    return estimate


def smooth(flags, wide, sides, even_in, odd_in, velocity, even_vel, odd_vel, corr, field_out, image_out, scratch):
    c0, c1, c2, diagonal, inverse, source, left, update, whole = scratch
    size_x, size_y, size_z = corr.shape
    rows = size_y + 2 * WIDE
    span = size_x + 2 * WIDE
    shape = (rows, size_z)
    row = lax.broadcasted_iota(jnp.int32, shape, 0)
    keep_first, keep_last = lane_masks(shape)
    has_low_x, has_high_x = flags[LOW_X] != 0, flags[HIGH_X] != 0
    has_low_y, has_high_y = flags[LOW_Y] != 0, flags[HIGH_Y] != 0
    lowest, highest = slice(0, 8), slice(rows - 8, rows)
    tile_row = lax.broadcasted_iota(jnp.int32, (8, size_z), 0)
    last_tile = slice(rows, rows + 8)

    def coefficients(x, v0, v1, v2):
        c0[x] = 1.0 + v0
        c1[x] = 1.0 + v1
        c2[x] = jnp.where(keep_first, 1.0 + v2, 0.0)
        total = 6.0 + v0 + v1 + v2
        diagonal[x] = total
        inverse[x] = 1.0 / total

    def source_plane(x, plane):
        source[x] = plane[0:rows]
        lines = plane[last_tile]
        kept = (tile_row == OWN_LOW) | (tile_row == PAST_LOW)
        source[x, lowest] = source[x, lowest] + jnp.where(
            kept, lines * jnp.where(tile_row == PAST_LOW, c1[x, lowest], 1.0), 0.0
        )
        lines = pltpu.roll(lines, 8 - (PAST_HIGH - OWN_LOW), 0)
        source[x, highest] = source[x, highest] + jnp.where(
            kept, lines * jnp.where(tile_row == PAST_LOW, c1[x, highest], 1.0), 0.0
        )

    def halo(low, high, low_vel, high_vel):
        for k in range(WIDE):
            coefficients(k, *[low_vel[d * WIDE + k] for d in range(3)])
            source_plane(k, low[k])
            x = WIDE + size_x + k
            coefficients(x, *[high_vel[d * WIDE + k] for d in range(3)])
            source_plane(x, high[k])
        whole[0] = jnp.where(has_low_x, low[WIDE, 0:rows], 0.0)
        whole[size_x + 1] = jnp.where(has_high_x, high[WIDE, 0:rows], 0.0)

    @pl.when(flags[ODD_X] == 0)
    def _():
        halo(odd_in, even_in, odd_vel, even_vel)

    @pl.when(flags[ODD_X] != 0)
    def _():
        halo(even_in, odd_in, even_vel, odd_vel)

    for k in range(size_x):
        coefficients(WIDE + k, velocity[0, k], velocity[1, k], velocity[2, k])
        source_plane(WIDE + k, wide[k])

    low_in, high_in = WIDE, WIDE + size_x - 1
    source[low_in - 1] = source[low_in - 1] + sides[0, 0:rows]
    source[low_in] = source[low_in] + c0[low_in] * whole[0]
    source[high_in] = source[high_in] + whole[size_x + 1]
    source[high_in + 1] = source[high_in + 1] + c0[high_in + 1] * sides[1, 0:rows]

    first_row = jnp.where(has_low_y, WIDE - DEPTH, WIDE)
    end_row = jnp.where(has_high_y, WIDE + size_y + DEPTH, WIDE + size_y)
    box_rows = (row >= first_row) & (row < end_row)
    everything = slice(0, rows)

    def plane_weight(x, tile, kept):
        value = jnp.where(kept, inverse[x, tile], 0.0)
        if x < WIDE:
            value = jnp.where(has_low_x, value, 0.0)
        if x >= WIDE + size_x:
            value = jnp.where(has_high_x, value, 0.0)
        return value

    run = functools.partial(
        chebyshev, source=source, left=left, update=update, coefs=(c0, c1, c2, diagonal)
    )
    box_planes = range(WIDE - DEPTH, WIDE + size_x + DEPTH)
    own_planes = range(WIDE, WIDE + size_x)

    low_planes, high_planes = range(0, WIDE + DEPTH), range(span - WIDE - DEPTH, span)
    own_weight = lambda x: plane_weight(x, everything, box_rows)
    beside = run(low_planes, everything, own_weight, keep_last=keep_last, wanted=(WIDE - 1,))[WIDE - 1]
    inner = (row >= WIDE) & (row < WIDE + size_y)
    whole[0] = jnp.where(has_low_x & inner, whole[0] + beside, 0.0)
    x = WIDE + size_x
    beside = run(high_planes, everything, own_weight, keep_last=keep_last, wanted=(x,))[x]
    whole[size_x + 1] = jnp.where(has_high_x & inner, whole[size_x + 1] + beside, 0.0)

    own = run(box_planes, everything, own_weight, keep_last=keep_last, wanted=tuple(own_planes))
    zeros = jnp.zeros((rows - size_y, size_z), F32)
    for k in range(size_x):
        placed = pltpu.roll(jnp.concatenate([corr[k], zeros], axis=0), WIDE, 0)
        whole[k + 1] = jnp.where(inner, placed + own[WIDE + k], 0.0)

    keep_tile = lane_masks((8, size_z))[1]
    low_weight = lambda x: plane_weight(x, lowest, tile_row < WIDE + DEPTH)
    beside = run(box_planes, lowest, low_weight, keep_last=keep_tile, wanted=tuple(own_planes))
    for k in range(size_x):
        line = pltpu.roll(wide[k, last_tile], 8 + WIDE - 1 - PAST_LOW, 0) + beside[WIDE + k]
        kept = has_low_y & (tile_row == WIDE - 1)
        whole[k + 1, lowest] = jnp.where(kept, line, whole[k + 1, lowest])
    high_weight = lambda x: plane_weight(x, highest, tile_row >= 8 - WIDE - DEPTH)
    beside = run(box_planes, highest, high_weight, keep_last=keep_tile, wanted=tuple(own_planes))
    for k in range(size_x):
        line = pltpu.roll(wide[k, last_tile], (8 + 8 - WIDE - PAST_HIGH) % 8, 0) + beside[WIDE + k]
        kept = has_high_y & (tile_row == 8 - WIDE)
        whole[k + 1, highest] = jnp.where(kept, line, whole[k + 1, highest])

    for k in range(size_x):
        x = WIDE + k
        image = stencil(
            whole[k], whole[k + 1], whole[k + 2], diagonal[x], c0[x], c1[x], c2[x], keep_last
        )
        image_out[k] = pltpu.roll(image, rows - WIDE, 0)[0:size_y]
        field_out[k] = pltpu.roll(whole[k + 1], rows - WIDE, 0)[0:size_y]


def dot_planes(left, right):
    total = left[0] * right[0]
    for x in range(1, left.shape[0]):
        total = total + left[x] * right[x]
    return total


def search_kernel(
    flags, wide, sides, even_in, odd_in, velocity, even_vel, odd_vel, corr, vectors, right_side, search, image, out,
    stage, *scratch
):
    smooth(flags, wide, sides, even_in, odd_in, velocity, even_vel, odd_vel, corr, search, image, scratch)
    restrict(vectors, image, [dot_planes(right_side, image)], flags, (out, stage))


def smoothed_kernel(
    flags, wide, sides, even_in, odd_in, velocity, even_vel, odd_vel, corr, middle, smoothed, turned, out, stage, *scratch
):
    smooth(flags, wide, sides, even_in, odd_in, velocity, even_vel, odd_vel, corr, smoothed, turned, scratch)
    stage[...] = jnp.zeros_like(stage)
    for k, total in enumerate((dot_planes(turned, middle), dot_planes(turned, turned))):
        total = jnp.sum(total, axis=0, keepdims=True)
        parts = [total[:, i : i + LANES] for i in range(0, total.shape[1], LANES)]
        stage[LANES + k : LANES + k + 1, :] = functools.reduce(jnp.add, parts)
    write_row(stage, out)


def last_kernel(flags, received, alpha, search, smoothed, middle, turned, solution_field, residual):
    _, sums = gathered(received)
    omega = sums[:, 0:1] / sums[:, 1:2]
    step = alpha[0:1, 0:1]
    for x in range(search.shape[0]):
        solution_field[x] = step * search[x] + omega * smoothed[x]
        residual[x] = middle[x] - omega * turned[x]


def local(right_side, velocity, deflation, inverse_rows):
    size_x, size_y, size_z = right_side.shape
    vectors_count = deflation.shape[0]
    count_x, count_y = lax.axis_size("gx"), lax.axis_size("gy")
    count = count_x * count_y
    at_x, at_y = lax.axis_index("gx"), lax.axis_index("gy")
    flags = jnp.stack(
        [
            at_x % 2,
            at_y % 2,
            (at_x > 0).astype(jnp.int32),
            (at_x < count_x - 1).astype(jnp.int32),
            (at_y > 0).astype(jnp.int32),
            (at_y < count_y - 1).astype(jnp.int32),
            (at_x * count_y + at_y) % (LANES // vectors_count),
            at_x,
        ]
    ).astype(jnp.int32)
    x_pairs, y_pairs = pair_permutations(count_x, count_y)

    def swap(messages, pairs):
        return [lax.ppermute(message, AXES, pair) for message, pair in zip(messages, pairs)]

    def share(row):
        return lax.all_to_all(row, AXES, 0, 0, tiled=True)

    rows = size_y + 2 * WIDE
    span = size_x + 2 * WIDE
    block = (size_x, size_y, size_z)
    row = (count, 2 * LANES)
    stage = (2 * LANES, LANES)
    y_message = (WIDE + 2, size_x, size_z)
    x_message = (WIDE + 1, rows + 8, size_z)
    region = (span, rows, size_z)
    smooth_scratch = [region] * 7 + [(2,) + region, (size_x + 2, rows, size_z)]

    faces = (3 * WIDE, size_x, size_z)
    velocity_y = swap(call(velocity_faces_kernel, [faces] * 2, [], flags, velocity), y_pairs)
    (first_row,) = call(first_kernel, [row], [stage], flags, right_side, deflation)
    wide_faces = (3 * WIDE, rows, size_z)
    wide_velocity, *velocity_x = call(
        velocity_wide_kernel,
        [(3, size_x, rows, size_z), wide_faces, wide_faces],
        [],
        flags,
        velocity,
        *velocity_y,
    )
    velocity_x = swap(velocity_x, x_pairs)
    first = share(first_row)

    def exchange(corr, rest, messages):
        messages = swap(messages, y_pairs)
        wide, sides, *messages = call(
            extend_kernel,
            [(size_x, rows + 8, size_z), (2, rows + 8, size_z), x_message, x_message],
            [],
            flags,
            rest,
            corr,
            *messages,
        )
        return (wide, sides, *swap(messages, x_pairs), wide_velocity, *velocity_x, corr)

    corr, rest, *messages = call(
        coarse_kernel,
        [block, block, y_message, y_message],
        [],
        flags,
        first,
        inverse_rows,
        deflation,
        right_side,
        velocity,
    )
    search, image, second_row = call(
        search_kernel,
        [block, block, row],
        [stage] + smooth_scratch,
        flags,
        *exchange(corr, rest, messages),
        deflation,
        right_side,
    )
    second = share(second_row)
    corr, rest, middle, alpha, *messages = call(
        second_coarse_kernel,
        [block, block, block, (8, LANES), y_message, y_message],
        [],
        flags,
        first,
        second,
        inverse_rows,
        deflation,
        right_side,
        image,
        velocity,
    )
    smoothed, turned, third_row = call(
        smoothed_kernel,
        [block, block, row],
        [stage] + smooth_scratch,
        flags,
        *exchange(corr, rest, messages),
        middle,
    )
    third = share(third_row)
    return tuple(
        call(last_kernel, [block, block], [], flags, third, alpha, search, smoothed, middle, turned)
    )


def solution(mesh):
    return jax.shard_map(
        local,
        mesh=mesh,
        in_specs=(
            P("gx", "gy", None),
            P(None, "gx", "gy", None),
            P(None, "gx", "gy", None),
            P(("gx", "gy"), None),
        ),
        out_specs=(P("gx", "gy", None), P("gx", "gy", None)),
        check_vma=False,
    )
```

```python
import functools

import jax
import jax.numpy as jnp
from jax import lax
from jax.experimental import pallas as pl
from jax.experimental.pallas import tpu as pltpu
from jax.sharding import PartitionSpec as P

DEPTH = 2
CHEB = 4
WIDE = 4
LANES = 128
AXES = ("gx", "gy")
F32 = jnp.float32
HIGHEST = lax.Precision.HIGHEST

cheb_center = 1.0
cheb_radius = 0.9

ODD_X, ODD_Y, LOW_X, HIGH_X, LOW_Y, HIGH_Y, SLOT = range(7)
OWN_LOW, PAST_LOW, PAST_HIGH, OWN_HIGH = 3, 4, 5, 6


def pair_permutations(count_x, count_y):
    def number(i, j):
        return i * count_y + j

    even_x, odd_x, even_y, odd_y = [], [], [], []
    for i in range(count_x):
        for j in range(count_y):
            here = number(i, j)
            even_x.append((here, number(i ^ 1, j)))
            even_y.append((here, number(i, j ^ 1)))
            other = ((i - 1) ^ 1) + 1
            odd_x.append((here, number(other, j) if 0 <= other < count_x else number(i, j ^ 1)))
            other = ((j - 1) ^ 1) + 1
            odd_y.append((here, number(i, other) if 0 <= other < count_y else number(i ^ 1, j)))
    return (even_x, odd_x), (even_y, odd_y)


def call(body, outs, scratch, *args, micros):
    specs = [pl.BlockSpec(memory_space=pltpu.SMEM)] + [pl.BlockSpec(memory_space=pltpu.VMEM)] * (len(args) - 1)
    return pl.pallas_call(
        body,
        out_shape=[jax.ShapeDtypeStruct(shape, F32) for shape in outs],
        in_specs=specs,
        out_specs=[pl.BlockSpec(memory_space=pltpu.VMEM)] * len(outs),
        scratch_shapes=[pltpu.VMEM(kind, F32) if isinstance(kind, tuple) else kind for kind in scratch],
        compiler_params=pltpu.CompilerParams(vmem_limit_bytes=24 * 1024 * 1024),
        cost_estimate=pl.CostEstimate(flops=0, bytes_accessed=int(micros * 3.6e6), transcendentals=0),
    )(*args)


def z_before(plane):
    return pltpu.roll(plane, 1, 1)


def z_after(plane, keep_last):
    return jnp.where(keep_last, pltpu.roll(plane, plane.shape[1] - 1, 1), 0.0)


def lane_masks(shape):
    lanes = lax.broadcasted_iota(jnp.int32, shape, 1)
    return lanes > 0, lanes < shape[1] - 1


def restrict(vectors, field, sums, flags, send, copies=()):
    count, size_x, size_y, size_z = vectors.shape
    stage = send[1]
    stage[...] = jnp.zeros_like(stage)

    def lanes_of(total):
        total = jnp.sum(total, axis=0, keepdims=True)
        return functools.reduce(jnp.add, [total[:, k : k + LANES] for k in range(0, size_z, LANES)])

    offset = pl.multiple_of(flags[SLOT] * count, count)
    for j in range(count):
        if copies and j % (count // len(copies)) == 0:
            copies[j // (count // len(copies))].wait()
        total = vectors[j, 0].astype(F32) * field[0]
        for x in range(1, size_x):
            total = total + vectors[j, x].astype(F32) * field[x]
        stage[pl.ds(offset + j, 1), :] = lanes_of(total)
    for k, total in enumerate(sums):
        stage[LANES + k : LANES + k + 1, :] = lanes_of(total)
    write_row(stage, send[0])


def write_row(stage, out):
    row = lax.dot_general(
        jnp.ones((8, LANES), F32), stage[...], (((1,), (1,)), ((), ())), precision=HIGHEST, preferred_element_type=F32
    )
    for k in range(0, out.shape[0], 8):
        out[k : k + 8, :] = row


def gathered(received):
    count = received.shape[0]
    return received[:, :LANES], jnp.sum(received[:, LANES:], axis=0, keepdims=True)


def solve(coarse, inverse, vectors):
    count = coarse.shape[0]
    share = LANES // vectors.shape[0]
    groups = count // share
    pick = (
        lax.broadcasted_iota(jnp.int32, (groups, count), 1) // share
        == lax.broadcasted_iota(jnp.int32, (groups, count), 0)
    ).astype(F32)
    packed = jnp.dot(pick, coarse, precision=HIGHEST, preferred_element_type=F32)
    total = inverse[:, :LANES] * packed[0:1]
    for k in range(1, groups):
        total = total + inverse[:, k * LANES : (k + 1) * LANES] * packed[k : k + 1]
    return jnp.sum(total, axis=1, keepdims=True).astype(jnp.bfloat16).astype(F32)


def prolong(solved, vectors, corr):
    count, size_x, size_y, size_z = vectors.shape
    totals = [jnp.zeros((size_y, size_z), F32) for _ in range(size_x)]
    for j in range(count):
        weight = jnp.broadcast_to(solved[j : j + 1], (size_y, size_z))
        for x in range(size_x):
            totals[x] = totals[x] + vectors[j, x].astype(F32) * weight
    for x in range(size_x):
        corr[x] = totals[x]


def subtract_own(field, corr, velocity, out):
    size_x, size_y, size_z = corr.shape
    keep_first, keep_last = lane_masks((size_y, size_z))
    rows = lax.broadcasted_iota(jnp.int32, (size_y, size_z), 0)
    for x in range(size_x):
        v0, v1, v2 = velocity[0, x], velocity[1, x], velocity[2, x]
        here = corr[x]
        image = (6.0 + v0 + v1 + v2) * here
        if x + 1 < size_x:
            image = image - corr[x + 1]
        if x > 0:
            image = image - (1.0 + v0) * corr[x - 1]
        image = image - jnp.where(rows < size_y - 1, pltpu.roll(here, size_y - 1, 0), 0.0)
        image = image - (1.0 + v1) * jnp.where(rows > 0, pltpu.roll(here, 1, 0), 0.0)
        image = image - z_after(here, keep_last) - (1.0 + v2) * jnp.where(keep_first, z_before(here), 0.0)
        out[x] = field[x] - image


def write_y_message(out, field, corr, high):
    size_x, size_y, _ = corr.shape
    start = size_y - WIDE if high else 0
    edge = size_y - 1 if high else 0
    for x in range(size_x):
        out[x] = field[x, start : start + WIDE, :]
        out[size_x + x // WIDE, x % WIDE : x % WIDE + 1, :] = corr[x, edge : edge + 1, :]
    last = size_x + size_x // WIDE
    out[last] = corr[0, start : start + WIDE, :]
    out[last + 1] = corr[size_x - 1, start : start + WIDE, :]


def by_parity(odd, write, even_out, odd_out):
    @pl.when(odd == 0)
    def _():
        write(even_out, True)
        write(odd_out, False)

    @pl.when(odd != 0)
    def _():
        write(even_out, False)
        write(odd_out, True)


def velocity_faces_kernel(flags, velocity, after, even_y, odd_y, even_x, odd_x):
    _, size_x, size_y, _ = velocity.shape

    def write_y(out, high):
        start = size_y - WIDE if high else 0
        for d in range(3):
            for x in range(size_x):
                out[d, x] = velocity[d, x, start : start + WIDE, :]

    def write_x(out, high):
        start = size_x - WIDE if high else 0
        for d in range(3):
            for k in range(WIDE):
                out[d, k, 0:size_y, :] = velocity[d, start + k]
                out[d, k, size_y:, :] = jnp.zeros((2 * WIDE, velocity.shape[3]), F32)

    by_parity(flags[ODD_Y], write_y, even_y, odd_y)
    by_parity(flags[ODD_X], write_x, even_x, odd_x)


def coefficients(x, v0, v1, v2, kept, keep_first, outs):
    inverse, b0, b1, b2 = outs
    total = 6.0 + v0 + v1 + v2
    value = jnp.where(kept, 1.0 / total, 0.0)
    inverse[x] = value
    b0[x] = value * (1.0 + v0)
    b1[x] = value * (1.0 + v1)
    b2[x] = jnp.where(keep_first, value * (1.0 + v2), 0.0)
    return total


def rows_in_grid(flags, shape):
    row = lax.broadcasted_iota(jnp.int32, shape, 0)
    first_row = jnp.where(flags[LOW_Y] != 0, 0, WIDE)
    end_row = jnp.where(flags[HIGH_Y] != 0, shape[0], shape[0] - WIDE)
    return (row >= first_row) & (row < end_row)


def coefficients_kernel(flags, velocity, even_in, odd_in, diagonal, inverse, b0, b1, b2, wide):
    _, size_x, size_y, size_z = velocity.shape
    rows = size_y + 2 * WIDE

    def place(low, high):
        for d in range(3):
            for x in range(size_x):
                wide[d, x, 0:WIDE, :] = low[d, x]
                wide[d, x, WIDE : WIDE + size_y, :] = velocity[d, x]
                wide[d, x, WIDE + size_y : rows, :] = high[d, x]

    @pl.when(flags[ODD_Y] == 0)
    def _():
        place(odd_in, even_in)

    @pl.when(flags[ODD_Y] != 0)
    def _():
        place(even_in, odd_in)

    kept = rows_in_grid(flags, (rows, size_z))
    keep_first, _ = lane_masks((rows, size_z))
    for x in range(size_x):
        diagonal[x] = coefficients(x, wide[0, x], wide[1, x], wide[2, x], kept, keep_first, (inverse, b0, b1, b2))


def halo_coefficients(flags, even_in, odd_in, even_vel, odd_vel, outs, wide):
    rows, size_z = even_vel.shape[2:]
    size_y = rows - 2 * WIDE
    kept = rows_in_grid(flags, (rows, size_z))
    keep_first, _ = lane_masks((rows, size_z))

    def side(start, message, faces, present):
        for k in range(WIDE):
            for d in range(3):
                wide[d, 0:WIDE, :] = message[WIDE + 1 + d, 8 * k : 8 * k + WIDE, :]
                wide[d, WIDE : WIDE + size_y, :] = faces[d, k, 0:size_y, :]
                wide[d, WIDE + size_y : rows, :] = message[WIDE + 1 + d, 8 * k + WIDE : 8 * k + 2 * WIDE, :]
            coefficients(start + k, wide[0], wide[1], wide[2], kept & (flags[present] != 0), keep_first, outs)

    @pl.when(flags[ODD_X] == 0)
    def _():
        side(0, odd_in, odd_vel, LOW_X)
        side(WIDE, even_in, even_vel, HIGH_X)

    @pl.when(flags[ODD_X] != 0)
    def _():
        side(0, even_in, even_vel, LOW_X)
        side(WIDE, odd_in, odd_vel, HIGH_X)


class Region:
    def __init__(self, own, halo):
        self.own, self.halo = own, halo

    def __getitem__(self, index):
        x, tile = index if isinstance(index, tuple) else (index, slice(None))
        size_x = self.own.shape[0]
        if x < WIDE:
            return self.halo[x, tile]
        return self.own[x - WIDE, tile] if x < WIDE + size_x else self.halo[x - size_x, tile]


def coarse_kernel(flags, received, inverse, vectors, field, velocity, after, corr, rest, even_out, odd_out):
    coarse, _ = gathered(received)
    prolong(solve(coarse, inverse, vectors), vectors, corr)
    subtract_own(field, corr, velocity, rest)
    by_parity(flags[ODD_Y], lambda out, high: write_y_message(out, rest, corr, high), even_out, odd_out)


def second_coarse_kernel(
    flags, received, second, inverse, vectors, field, image, velocity, corr, rest, middle, alpha, even_out, odd_out
):
    coarse, _ = gathered(received)
    coarse_image, products = gathered(second)
    step = jnp.broadcast_to(products[:, 0:1] / products[:, 1:2], alpha.shape)
    alpha[...] = step
    step = step[0:1, 0:1]
    for x in range(field.shape[0]):
        middle[x] = field[x] - step * image[x]
    prolong(solve(coarse - step * coarse_image, inverse, vectors), vectors, corr)
    subtract_own(middle, corr, velocity, rest)
    by_parity(flags[ODD_Y], lambda out, high: write_y_message(out, rest, corr, high), even_out, odd_out)


def extend_kernel(flags, rest, corr, even_in, odd_in, even_vel, odd_vel, wide, sides, even_out, odd_out):
    size_x, size_y, size_z = rest.shape
    rows = size_y + 2 * WIDE

    def place(low, high):
        has_low, has_high = flags[LOW_Y] != 0, flags[HIGH_Y] != 0
        for x in range(size_x):
            at, line = size_x + x // WIDE, slice(x % WIDE, x % WIDE + 1)
            wide[x, 0:WIDE, :] = low[x]
            wide[x, WIDE : WIDE + size_y, :] = rest[x]
            wide[x, WIDE + size_y : rows, :] = high[x]
            wide[x, rows : rows + 8, :] = jnp.zeros((8, size_z), F32)
            wide[x, rows + OWN_LOW : rows + OWN_LOW + 1, :] = corr[x, 0:1, :]
            wide[x, rows + PAST_LOW : rows + PAST_LOW + 1, :] = jnp.where(has_low, low[at, line, :], 0.0)
            wide[x, rows + PAST_HIGH : rows + PAST_HIGH + 1, :] = jnp.where(has_high, high[at, line, :], 0.0)
            wide[x, rows + OWN_HIGH : rows + OWN_HIGH + 1, :] = corr[x, size_y - 1 : size_y, :]
        last = size_x + size_x // WIDE
        for side, x in enumerate((0, size_x - 1)):
            sides[side, 0:WIDE, :] = low[last + side]
            sides[side, WIDE : WIDE + size_y, :] = corr[x]
            sides[side, WIDE + size_y : rows, :] = high[last + side]
            sides[side, rows : rows + 8, :] = jnp.zeros((8, size_z), F32)

    @pl.when(flags[ODD_Y] == 0)
    def _():
        place(odd_in, even_in)

    @pl.when(flags[ODD_Y] != 0)
    def _():
        place(even_in, odd_in)

    def write(out, high):
        start = size_x - WIDE if high else 0
        for k in range(WIDE):
            out[k] = wide[start + k]
        out[WIDE] = sides[1 if high else 0]

    by_parity(flags[ODD_X], write, even_out, odd_out)
    if even_vel is None:
        return

    def corners(low, high):
        def write(out, upper):
            start = size_x - WIDE if upper else 0
            for d in range(3):
                for k in range(WIDE):
                    out[WIDE + 1 + d, 8 * k : 8 * k + WIDE, :] = low[d, start + k]
                    out[WIDE + 1 + d, 8 * k + WIDE : 8 * k + 2 * WIDE, :] = high[d, start + k]

        by_parity(flags[ODD_X], write, even_out, odd_out)

    @pl.when(flags[ODD_Y] == 0)
    def _():
        corners(odd_vel, even_vel)

    @pl.when(flags[ODD_Y] != 0)
    def _():
        corners(even_vel, odd_vel)


def extend_again_kernel(flags, rest, corr, even_in, odd_in, wide, sides, even_out, odd_out):
    extend_kernel(flags, rest, corr, even_in, odd_in, None, None, wide, sides, even_out, odd_out)


def beside_terms(before, here, after, x, tile, coefs, keep_last):
    inverse, b0, b1, b2 = coefs
    rows = here.shape[0]
    ahead = pltpu.roll(here, rows - 1, 0) + z_after(here, keep_last)
    if after is not None:
        ahead = ahead + after
    total = inverse[x, tile] * ahead + b1[x, tile] * pltpu.roll(here, 1, 0) + b2[x, tile] * z_before(here)
    if before is not None:
        total = total + b0[x, tile] * before
    return total


def chebyshev(planes, tile, inside, source, left, update, coefs, keep_last, wanted):
    sigma = cheb_center / cheb_radius
    rho = 1.0 / sigma
    first, last = planes[0], planes[-1]
    for x in planes:
        update[0, x, tile] = jnp.where(inside, source(x), 0.0)
    estimate = {}
    for sweep in range(1, CHEB):
        rest = CHEB - 1 - sweep
        low, high = max(first, wanted[0] - rest), min(last, wanted[-1] + rest)
        rho_next = 1.0 / (2.0 * sigma - rho)
        for x in range(low, high + 1):
            here = update[sweep - 1, x, tile]
            before = update[sweep - 1, x - 1, tile] if x > first else None
            after = update[sweep - 1, x + 1, tile] if x < last else None
            remainder = (here if sweep == 1 else left[x, tile]) - here
            remainder = remainder + beside_terms(before, here, after, x, tile, coefs, keep_last)
            if rest:
                left[x, tile] = remainder
            value = rho_next * rho * here + (2.0 * rho_next / cheb_radius) * jnp.where(inside, remainder, 0.0)
            if rest:
                update[sweep, x, tile] = value
            else:
                for k in range(CHEB - 1):
                    value = value + update[k, x, tile]
                estimate[x] = value
        rho = rho_next
    return estimate


def smooth(
    flags, wide, sides, even_in, odd_in, diagonal, coefs, corr, field_out, image_out, scratch
):
    source, left, update, whole = scratch
    inverse, b0, b1, _ = coefs
    size_x, size_y, size_z = corr.shape
    rows = size_y + 2 * WIDE
    span = size_x + 2 * WIDE
    row = lax.broadcasted_iota(jnp.int32, (rows, size_z), 0)
    keep_last = lane_masks((rows, size_z))[1]
    has_low_x, has_high_x = flags[LOW_X] != 0, flags[HIGH_X] != 0
    has_low_y, has_high_y = flags[LOW_Y] != 0, flags[HIGH_Y] != 0
    lowest, highest = slice(0, 8), slice(rows - 8, rows)
    tile_row = lax.broadcasted_iota(jnp.int32, (8, size_z), 0)
    last_tile = slice(rows, rows + 8)
    kept = (tile_row == OWN_LOW) | (tile_row == PAST_LOW)

    def source_plane(x, plane):
        source[x] = inverse[x] * plane[0:rows]
        lines = plane[last_tile]
        for tile, shift in ((lowest, 0), (highest, 8 - (PAST_HIGH - OWN_LOW))):
            moved = pltpu.roll(lines, shift, 0) if shift else lines
            factor = jnp.where(tile_row == PAST_LOW, b1[x, tile], inverse[x, tile])
            source[x, tile] = source[x, tile] + jnp.where(kept, moved * factor, 0.0)

    def halo(low, high):
        for k in range(WIDE):
            source_plane(k, low.at[k])
            source_plane(WIDE + size_x + k, high.at[k])
        whole[0] = jnp.where(has_low_x, low[WIDE, 0:rows], 0.0)
        whole[size_x + 1] = jnp.where(has_high_x, high[WIDE, 0:rows], 0.0)

    @pl.when(flags[ODD_X] == 0)
    def _():
        halo(odd_in, even_in)

    @pl.when(flags[ODD_X] != 0)
    def _():
        halo(even_in, odd_in)

    for k in range(size_x):
        source_plane(WIDE + k, wide.at[k])

    low_in, high_in = WIDE, WIDE + size_x - 1
    source[low_in - 1] = source[low_in - 1] + inverse[low_in - 1] * sides[0, 0:rows]
    source[low_in] = source[low_in] + b0[low_in] * whole[0]
    source[high_in] = source[high_in] + inverse[high_in] * whole[size_x + 1]
    source[high_in + 1] = source[high_in + 1] + b0[high_in + 1] * sides[1, 0:rows]

    def run(planes, tile, inside, wanted):
        return chebyshev(
            planes,
            tile,
            inside,
            lambda x: source[x, tile],
            left,
            update,
            coefs,
            lane_masks(inside.shape)[1],
            wanted,
        )

    everything = slice(0, rows)
    box_rows = (row >= WIDE - DEPTH) & (row < WIDE + size_y + DEPTH)
    box_planes = range(WIDE - DEPTH, WIDE + size_x + DEPTH)
    own_planes = range(WIDE, WIDE + size_x)
    inner = (row >= WIDE) & (row < WIDE + size_y)

    beside = run(range(0, WIDE + DEPTH), everything, box_rows, (WIDE - 1,))[WIDE - 1]
    whole[0] = jnp.where(has_low_x & inner, whole[0] + beside, 0.0)
    x = WIDE + size_x
    beside = run(range(span - WIDE - DEPTH, span), everything, box_rows, (x,))[x]
    whole[size_x + 1] = jnp.where(has_high_x & inner, whole[size_x + 1] + beside, 0.0)

    own = run(box_planes, everything, box_rows, tuple(own_planes))
    zeros = jnp.zeros((rows - size_y, size_z), F32)
    for k in range(size_x):
        placed = pltpu.roll(jnp.concatenate([corr[k], zeros], axis=0), WIDE, 0)
        whole[k + 1] = jnp.where(inner, placed + own[WIDE + k], 0.0)

    beside = run(box_planes, lowest, tile_row < WIDE + DEPTH, tuple(own_planes))
    for k in range(size_x):
        line = pltpu.roll(wide[k, last_tile], 8 + WIDE - 1 - PAST_LOW, 0) + beside[WIDE + k]
        here = has_low_y & (tile_row == WIDE - 1)
        whole[k + 1, lowest] = jnp.where(here, line, whole[k + 1, lowest])
    beside = run(box_planes, highest, tile_row >= 8 - WIDE - DEPTH, tuple(own_planes))
    for k in range(size_x):
        line = pltpu.roll(wide[k, last_tile], (8 + 8 - WIDE - PAST_HIGH) % 8, 0) + beside[WIDE + k]
        here = has_high_y & (tile_row == 8 - WIDE)
        whole[k + 1, highest] = jnp.where(here, line, whole[k + 1, highest])

    for k in range(size_x):
        x = WIDE + k
        terms = beside_terms(whole[k], whole[k + 1], whole[k + 2], x, everything, coefs, keep_last)
        image = diagonal[k] * (whole[k + 1] - terms)
        image_out[k] = pltpu.roll(image, rows - WIDE, 0)[0:size_y]
        field_out[k] = pltpu.roll(whole[k + 1], rows - WIDE, 0)[0:size_y]


def dot_planes(left, right):
    total = left[0] * right[0]
    for x in range(1, left.shape[0]):
        total = total + left[x] * right[x]
    return total


def search_kernel(
    flags, wide, sides, even_in, odd_in, diagonal, own0, own1, own2, own3, corr, even_vel, odd_vel, vectors, right_side,
    search, image, out, halo0, halo1, halo2, halo3, stage, wide_vel, *scratch
):
    halos = (halo0, halo1, halo2, halo3)
    halo_coefficients(flags, even_in, odd_in, even_vel, odd_vel, halos, wide_vel)
    coefs = [Region(*pair) for pair in zip((own0, own1, own2, own3), halos)]
    smooth(flags, wide, sides, even_in, odd_in, diagonal, coefs, corr, search, image, scratch)
    products = [dot_planes(right_side, right_side), dot_planes(right_side, image)]
    restrict(vectors, image, products, flags, (out, stage))


def smoothed_kernel(
    flags, wide, sides, even_in, odd_in, diagonal, own0, own1, own2, own3, corr, halo0, halo1, halo2, halo3, middle,
    smoothed, turned, out, stage, *scratch
):
    coefs = [Region(*pair) for pair in zip((own0, own1, own2, own3), (halo0, halo1, halo2, halo3))]
    smooth(flags, wide, sides, even_in, odd_in, diagonal, coefs, corr, smoothed, turned, scratch)
    stage[...] = jnp.zeros_like(stage)
    for k, total in enumerate((dot_planes(turned, middle), dot_planes(turned, turned))):
        total = jnp.sum(total, axis=0, keepdims=True)
        parts = [total[:, i : i + LANES] for i in range(0, total.shape[1], LANES)]
        stage[LANES + k : LANES + k + 1, :] = functools.reduce(jnp.add, parts)
    write_row(stage, out)


def last_kernel(flags, received, alpha, search, smoothed, middle, turned, solution_field, residual):
    _, sums = gathered(received)
    omega = sums[:, 0:1] / sums[:, 1:2]
    step = alpha[0:1, 0:1]
    for x in range(search.shape[0]):
        solution_field[x] = step * search[x] + omega * smoothed[x]
        residual[x] = middle[x] - omega * turned[x]


def local(right_side, velocity, deflation, inverse_rows):
    size_x, size_y, size_z = right_side.shape
    vectors_count = deflation.shape[0]
    count_x, count_y = lax.axis_size("gx"), lax.axis_size("gy")
    count = count_x * count_y
    at_x, at_y = lax.axis_index("gx"), lax.axis_index("gy")
    flags = jnp.stack(
        [
            at_x % 2,
            at_y % 2,
            (at_x > 0).astype(jnp.int32),
            (at_x < count_x - 1).astype(jnp.int32),
            (at_y > 0).astype(jnp.int32),
            (at_y < count_y - 1).astype(jnp.int32),
            (at_x * count_y + at_y) % (LANES // vectors_count),
            at_x,
        ]
    ).astype(jnp.int32)
    x_pairs, y_pairs = pair_permutations(count_x, count_y)

    def swap(messages, pairs):
        return [lax.ppermute(message, AXES, pair) for message, pair in zip(messages, pairs)]

    def share(row):
        return lax.all_to_all(row, AXES, 0, 0, tiled=True)

    rows = size_y + 2 * WIDE
    span = size_x + 2 * WIDE
    block = (size_x, size_y, size_z)
    row = (count, 2 * LANES)
    stage = (2 * LANES, LANES)
    y_message = (size_x + size_x // WIDE + 2, WIDE, size_z)
    region = (span, rows, size_z)
    smooth_scratch = [region, region, (CHEB - 1,) + region, (size_x + 2, rows, size_z)]

    rounded = lax.reduce_precision(right_side, 8, 7)
    partial = lax.optimization_barrier(jnp.sum(deflation.astype(F32) * rounded, axis=(1, 2)))
    share_count = LANES // vectors_count
    first_row = jnp.where(jnp.arange(2 * share_count)[:, None] == flags[SLOT], jnp.sum(partial, axis=1)[None, :], 0.0)
    first_row = jnp.broadcast_to(first_row.reshape(1, 2 * LANES), row)

    first = share(first_row)
    faces_y, faces_x = (3, size_x, WIDE, size_z), (3, WIDE, rows, size_z)
    faces = call(
        velocity_faces_kernel, [faces_y] * 2 + [faces_x] * 2, [], flags, velocity, first_row[0, :8], micros=0.01
    )
    after = faces[0]
    velocity_y, velocity_x = swap(faces[:2], y_pairs), swap(faces[2:], x_pairs)

    def exchange(corr, rest, messages, extend, message, *vel):
        wide, sides, *messages = call(
            extend,
            [(size_x, rows + 8, size_z), (2, rows + 8, size_z), message, message],
            [],
            flags,
            rest,
            corr,
            *swap(messages, y_pairs),
            *vel,
            micros=0.01,
        )
        return (wide, sides, *swap(messages, x_pairs), *coefs, corr)

    corr, rest, *messages = call(
        coarse_kernel,
        [block, block, y_message, y_message],
        [],
        flags,
        first,
        inverse_rows,
        deflation,
        right_side,
        velocity,
        after,
        micros=1.4,
    )
    wide_own, wide_halo = (size_x, rows, size_z), (2 * WIDE, rows, size_z)
    coefs = call(
        coefficients_kernel,
        [wide_own] * 5,
        [(3, size_x, rows, size_z)],
        flags,
        velocity,
        *velocity_y,
        micros=0.01,
    )
    search, image, second_row, *halo_coefs = call(
        search_kernel,
        [block, block, row] + [wide_halo] * 4,
        [stage, (3, rows, size_z)] + smooth_scratch,
        flags,
        *exchange(corr, rest, messages, extend_kernel, (WIDE + 4, rows + 8, size_z), *velocity_y),
        *velocity_x,
        deflation,
        right_side,
        micros=3.0,
    )
    second = share(second_row)
    corr, rest, middle, alpha, *messages = call(
        second_coarse_kernel,
        [block, block, block, (8, LANES), y_message, y_message],
        [],
        flags,
        first,
        second,
        inverse_rows,
        deflation,
        right_side,
        image,
        velocity,
        micros=1.4,
    )
    smoothed, turned, third_row = call(
        smoothed_kernel,
        [block, block, row],
        [stage] + smooth_scratch,
        flags,
        *exchange(corr, rest, messages, extend_again_kernel, (WIDE + 1, rows + 8, size_z)),
        *halo_coefs,
        middle,
        micros=2.5,
    )
    third = share(third_row)
    return tuple(
        call(last_kernel, [block, block], [], flags, third, alpha, search, smoothed, middle, turned, micros=1.4)
    )


def solution(mesh):
    return jax.shard_map(
        local,
        mesh=mesh,
        in_specs=(
            P("gx", "gy", None),
            P(None, "gx", "gy", None),
            P(None, "gx", "gy", None),
            P(("gx", "gy"), None),
        ),
        out_specs=(P("gx", "gy", None), P("gx", "gy", None)),
        check_vma=False,
    )
```

```python
import functools

import jax
import jax.numpy as jnp
from jax import lax
from jax.experimental import pallas as pl
from jax.experimental.pallas import tpu as pltpu
from jax.sharding import PartitionSpec as P

DEPTH = 2
CHEB = 4
WIDE = 4
LANES = 128
AXES = ("gx", "gy")
F32 = jnp.float32
HIGHEST = lax.Precision.HIGHEST

cheb_center = 1.0
cheb_radius = 0.9

ODD_X, ODD_Y, LOW_X, HIGH_X, LOW_Y, HIGH_Y, SLOT = range(7)

def pair_permutations(count_x, count_y):
    def number(i, j):
        return i * count_y + j

    even_x, odd_x, even_y, odd_y = [], [], [], []
    for i in range(count_x):
        for j in range(count_y):
            here = number(i, j)
            even_x.append((here, number(i ^ 1, j)))
            even_y.append((here, number(i, j ^ 1)))
            other = ((i - 1) ^ 1) + 1
            odd_x.append((here, number(other, j) if 0 <= other < count_x else number(i, j ^ 1)))
            other = ((j - 1) ^ 1) + 1
            odd_y.append((here, number(i, other) if 0 <= other < count_y else number(i ^ 1, j)))
    return (even_x, odd_x), (even_y, odd_y)


def call(body, outs, scratch, *args, micros):
    specs = [pl.BlockSpec(memory_space=pltpu.SMEM)] + [pl.BlockSpec(memory_space=pltpu.VMEM)] * (len(args) - 1)
    return pl.pallas_call(
        body,
        out_shape=[jax.ShapeDtypeStruct(shape, F32) for shape in outs],
        in_specs=specs,
        out_specs=[pl.BlockSpec(memory_space=pltpu.VMEM)] * len(outs),
        scratch_shapes=[pltpu.VMEM(kind, F32) if isinstance(kind, tuple) else kind for kind in scratch],
        compiler_params=pltpu.CompilerParams(vmem_limit_bytes=24 * 1024 * 1024),
        cost_estimate=pl.CostEstimate(flops=0, bytes_accessed=int(micros * 3.6e6), transcendentals=0),
    )(*args)


def z_before(plane):
    return pltpu.roll(plane, 1, 1)


def z_after(plane, keep_last):
    return jnp.where(keep_last, pltpu.roll(plane, plane.shape[1] - 1, 1), 0.0)


def lane_masks(shape):
    lanes = lax.broadcasted_iota(jnp.int32, shape, 1)
    return lanes > 0, lanes < shape[1] - 1


def restrict(vectors, field, sums, flags, send, copies=()):
    count, size_x, size_y, size_z = vectors.shape
    stage = send[1]
    stage[...] = jnp.zeros_like(stage)

    def lanes_of(total):
        total = jnp.sum(total, axis=0, keepdims=True)
        return functools.reduce(jnp.add, [total[:, k : k + LANES] for k in range(0, size_z, LANES)])

    offset = pl.multiple_of(flags[SLOT] * count, count)
    for j in range(count):
        if copies and j % (count // len(copies)) == 0:
            copies[j // (count // len(copies))].wait()
        total = vectors[j, 0].astype(F32) * field[0]
        for x in range(1, size_x):
            total = total + vectors[j, x].astype(F32) * field[x]
        stage[pl.ds(offset + j, 1), :] = lanes_of(total)
    for k, total in enumerate(sums):
        stage[LANES + k : LANES + k + 1, :] = lanes_of(total)
    write_row(stage, send[0])


def write_row(stage, out):
    row = lax.dot_general(
        jnp.ones((8, LANES), F32), stage[...], (((1,), (1,)), ((), ())), precision=HIGHEST, preferred_element_type=F32
    )
    for k in range(0, out.shape[0], 8):
        out[k : k + 8, :] = row


def gathered(received):
    count = received.shape[0]
    return received[:, :LANES], jnp.sum(received[:, LANES:], axis=0, keepdims=True)


def solve(coarse, inverse, vectors):
    count = coarse.shape[0]
    share = LANES // vectors.shape[0]
    groups = count // share
    pick = (
        lax.broadcasted_iota(jnp.int32, (groups, count), 1) // share
        == lax.broadcasted_iota(jnp.int32, (groups, count), 0)
    ).astype(F32)
    packed = jnp.dot(pick, coarse, precision=HIGHEST, preferred_element_type=F32)
    total = inverse[:, :LANES] * packed[0:1]
    for k in range(1, groups):
        total = total + inverse[:, k * LANES : (k + 1) * LANES] * packed[k : k + 1]
    return jnp.sum(total, axis=1, keepdims=True).astype(jnp.bfloat16).astype(F32)


def prolong(solved, vectors, corr):
    count, size_x, size_y, size_z = vectors.shape
    totals = [jnp.zeros((size_y, size_z), F32) for _ in range(size_x)]
    for j in range(count):
        weight = jnp.broadcast_to(solved[j : j + 1], (size_y, size_z))
        for x in range(size_x):
            totals[x] = totals[x] + vectors[j, x].astype(F32) * weight
    for x in range(size_x):
        corr[x] = totals[x]


def subtract_own(field, corr, velocity, out):
    size_x, size_y, size_z = corr.shape
    keep_first, keep_last = lane_masks((size_y, size_z))
    rows = lax.broadcasted_iota(jnp.int32, (size_y, size_z), 0)
    for x in range(size_x):
        v0, v1, v2 = velocity[0, x], velocity[1, x], velocity[2, x]
        here = corr[x]
        image = (6.0 + v0 + v1 + v2) * here
        if x + 1 < size_x:
            image = image - corr[x + 1]
        if x > 0:
            image = image - (1.0 + v0) * corr[x - 1]
        image = image - jnp.where(rows < size_y - 1, pltpu.roll(here, size_y - 1, 0), 0.0)
        image = image - (1.0 + v1) * jnp.where(rows > 0, pltpu.roll(here, 1, 0), 0.0)
        image = image - z_after(here, keep_last) - (1.0 + v2) * jnp.where(keep_first, z_before(here), 0.0)
        out[x] = field[x] - image


def write_y_message(out, field, corr, high):
    size_x, size_y, _ = corr.shape
    start = size_y - WIDE if high else 0
    edge = size_y - 1 if high else 0
    for x in range(size_x):
        out[x] = field[x, start : start + WIDE, :]
        out[size_x + x // WIDE, x % WIDE : x % WIDE + 1, :] = corr[x, edge : edge + 1, :]
    last = size_x + size_x // WIDE
    out[last] = corr[0, start : start + WIDE, :]
    out[last + 1] = corr[size_x - 1, start : start + WIDE, :]


def by_parity(odd, write, even_out, odd_out):
    @pl.when(odd == 0)
    def _():
        write(even_out, True)
        write(odd_out, False)

    @pl.when(odd != 0)
    def _():
        write(even_out, False)
        write(odd_out, True)


def velocity_y_kernel(flags, velocity, after, even_out, odd_out):
    _, size_x, size_y, _ = velocity.shape

    def write_y(out, high):
        start = size_y - WIDE if high else 0
        for d in range(3):
            for x in range(size_x):
                out[d, x] = velocity[d, x, start : start + WIDE, :]

    by_parity(flags[ODD_Y], write_y, even_out, odd_out)


def write_velocity_x(flags, velocity, even_out, odd_out):
    size_x = velocity.shape[1]

    def write(out, high):
        start = size_x - WIDE if high else 0
        for d in range(3):
            for k in range(WIDE):
                out[d * WIDE + k] = velocity[d, start + k]
        for k in range(3 * WIDE, out.shape[0]):
            out[k] = jnp.zeros(out.shape[1:], F32)

    by_parity(flags[ODD_X], write, even_out, odd_out)


def coefficients(x, v0, v1, v2, kept, keep_first, outs):
    inverse, b0, b1, b2 = outs
    total = 6.0 + v0 + v1 + v2
    value = jnp.where(kept, 1.0 / total, 0.0)
    inverse[x] = value
    b0[x] = value * (1.0 + v0)
    b1[x] = value * (1.0 + v1)
    b2[x] = jnp.where(keep_first, value * (1.0 + v2), 0.0)
    return total


def rows_in_grid(flags, shape):
    row = lax.broadcasted_iota(jnp.int32, shape, 0)
    first_row = jnp.where(flags[LOW_Y] != 0, 0, WIDE)
    end_row = jnp.where(flags[HIGH_Y] != 0, shape[0], shape[0] - WIDE)
    return (row >= first_row) & (row < end_row)


def coefficients_kernel(flags, velocity, even_in, odd_in, diagonal, inverse, b0, b1, b2, wide):
    _, size_x, size_y, size_z = velocity.shape
    rows = size_y + 2 * WIDE

    def place(low, high):
        for d in range(3):
            for x in range(size_x):
                wide[d, x, 0:WIDE, :] = low[d, x]
                wide[d, x, WIDE : WIDE + size_y, :] = velocity[d, x]
                wide[d, x, WIDE + size_y : rows, :] = high[d, x]

    @pl.when(flags[ODD_Y] == 0)
    def _():
        place(odd_in, even_in)

    @pl.when(flags[ODD_Y] != 0)
    def _():
        place(even_in, odd_in)

    kept = rows_in_grid(flags, (rows, size_z))
    keep_first, _ = lane_masks((rows, size_z))
    for x in range(size_x):
        diagonal[x] = coefficients(x, wide[0, x], wide[1, x], wide[2, x], kept, keep_first, (inverse, b0, b1, b2))


def halo_coefficients(flags, even_in, odd_in, even_vel, odd_vel, outs, wide):
    size_y, size_z = even_vel.shape[1:]
    rows = size_y + 2 * WIDE
    kept = rows_in_grid(flags, (rows, size_z))
    keep_first, _ = lane_masks((rows, size_z))

    def side(start, message, faces, present):
        for k in range(WIDE):
            for d in range(3):
                wide[d, 0:WIDE, :] = message[WIDE + 1 + k, 8 * d : 8 * d + WIDE, :]
                wide[d, WIDE : WIDE + size_y, :] = faces[d * WIDE + k]
                wide[d, WIDE + size_y : rows, :] = message[WIDE + 1 + k, 8 * d + WIDE : 8 * d + 2 * WIDE, :]
            coefficients(start + k, wide[0], wide[1], wide[2], kept & (flags[present] != 0), keep_first, outs)

    @pl.when(flags[ODD_X] == 0)
    def _():
        side(0, odd_in, odd_vel, LOW_X)
        side(WIDE, even_in, even_vel, HIGH_X)

    @pl.when(flags[ODD_X] != 0)
    def _():
        side(0, even_in, even_vel, LOW_X)
        side(WIDE, odd_in, odd_vel, HIGH_X)


class Region:
    def __init__(self, own, halo):
        self.own, self.halo = own, halo

    def __getitem__(self, index):
        x, tile = index if isinstance(index, tuple) else (index, slice(None))
        size_x = self.own.shape[0]
        if x < WIDE:
            return self.halo[x, tile]
        return self.own[x - WIDE, tile] if x < WIDE + size_x else self.halo[x - size_x, tile]


def coarse_kernel(
    flags, received, inverse, vectors, field, velocity, after, corr, rest, even_out, odd_out, even_vel, odd_vel
):
    coarse, _ = gathered(received)
    prolong(solve(coarse, inverse, vectors), vectors, corr)
    subtract_own(field, corr, velocity, rest)
    by_parity(flags[ODD_Y], lambda out, high: write_y_message(out, rest, corr, high), even_out, odd_out)
    write_velocity_x(flags, velocity, even_vel, odd_vel)


def second_coarse_kernel(
    flags, received, second, inverse, vectors, field, image, velocity, corr, rest, middle, alpha, even_out, odd_out
):
    coarse, _ = gathered(received)
    coarse_image, products = gathered(second)
    step = jnp.broadcast_to(products[:, 0:1] / products[:, 1:2], alpha.shape)
    alpha[...] = step
    step = step[0:1, 0:1]
    for x in range(field.shape[0]):
        middle[x] = field[x] - step * image[x]
    prolong(solve(coarse - step * coarse_image, inverse, vectors), vectors, corr)
    subtract_own(middle, corr, velocity, rest)
    by_parity(flags[ODD_Y], lambda out, high: write_y_message(out, rest, corr, high), even_out, odd_out)


def extend_kernel(
    flags, rest, corr, even_in, odd_in, velocity, even_vel, odd_vel, wide, sides, past, even_out, odd_out, corners=True
):
    size_x, size_y, size_z = rest.shape
    rows = size_y + 2 * WIDE
    end = WIDE + size_y

    def place(low, high, high_vel):
        has_low, has_high = flags[LOW_Y] != 0, flags[HIGH_Y] != 0
        for x in range(size_x):
            at, line = size_x + x // WIDE, slice(x % WIDE, x % WIDE + 1)
            past_low = jnp.where(has_low, low[at, line, :], 0.0)
            past_high = jnp.where(has_high, high[at, line, :], 0.0)
            past[0, x : x + 1, :] = past_low
            past[1, x : x + 1, :] = past_high
            wide[x, 0 : WIDE - 1, :] = low[x, 0 : WIDE - 1, :]
            wide[x, WIDE - 1 : WIDE, :] = low[x, WIDE - 1 : WIDE, :] + corr[x, 0:1, :]
            wide[x, WIDE:end, :] = rest[x]
            wide[x, WIDE : WIDE + 1, :] = rest[x, 0:1, :] + (1.0 + velocity[1, x, 0:1, :]) * past_low
            wide[x, end - 1 : end, :] = rest[x, size_y - 1 : size_y, :] + past_high
            weight = 1.0 + high_vel[1, x, 0:1, :]
            wide[x, end : end + 1, :] = high[x, 0:1, :] + weight * corr[x, size_y - 1 : size_y, :]
            wide[x, end + 1 : rows, :] = high[x, 1:WIDE, :]
        last = size_x + size_x // WIDE
        for side, x in enumerate((0, size_x - 1)):
            sides[side, 0:WIDE, :] = low[last + side]
            sides[side, WIDE:end, :] = corr[x]
            sides[side, end:rows, :] = high[last + side]

    @pl.when(flags[ODD_Y] == 0)
    def _():
        place(odd_in, even_in, even_vel)

    @pl.when(flags[ODD_Y] != 0)
    def _():
        place(even_in, odd_in, odd_vel)

    def write(out, high):
        start = size_x - WIDE if high else 0
        for k in range(WIDE):
            out[k] = wide[start + k]
        out[WIDE] = sides[1 if high else 0]

    by_parity(flags[ODD_X], write, even_out, odd_out)
    if not corners:
        return

    def write_corners(low, high):
        def write(out, upper):
            start = size_x - WIDE if upper else 0
            for k in range(WIDE):
                for d in range(3):
                    out[WIDE + 1 + k, 8 * d : 8 * d + WIDE, :] = low[d, start + k]
                    out[WIDE + 1 + k, 8 * d + WIDE : 8 * d + 2 * WIDE, :] = high[d, start + k]

        by_parity(flags[ODD_X], write, even_out, odd_out)

    @pl.when(flags[ODD_Y] == 0)
    def _():
        write_corners(odd_vel, even_vel)

    @pl.when(flags[ODD_Y] != 0)
    def _():
        write_corners(even_vel, odd_vel)


def beside_terms(before, here, after, x, tile, coefs, keep_last):
    inverse, b0, b1, b2 = coefs
    rows = here.shape[0]
    ahead = pltpu.roll(here, rows - 1, 0) + z_after(here, keep_last)
    if after is not None:
        ahead = ahead + after
    total = inverse[x, tile] * ahead + b1[x, tile] * pltpu.roll(here, 1, 0) + b2[x, tile] * z_before(here)
    if before is not None:
        total = total + b0[x, tile] * before
    return total


def chebyshev(planes, tile, inside, source, left, update, coefs, keep_last, wanted):
    sigma = cheb_center / cheb_radius
    rho = 1.0 / sigma
    first, last = planes[0], planes[-1]
    for x in planes:
        update[0, x, tile] = jnp.where(inside, source(x), 0.0)
    estimate = {}
    for sweep in range(1, CHEB):
        rest = CHEB - 1 - sweep
        low, high = max(first, wanted[0] - rest), min(last, wanted[-1] + rest)
        rho_next = 1.0 / (2.0 * sigma - rho)
        for x in range(low, high + 1):
            here = update[sweep - 1, x, tile]
            before = update[sweep - 1, x - 1, tile] if x > first else None
            after = update[sweep - 1, x + 1, tile] if x < last else None
            remainder = (here if sweep == 1 else left[x, tile]) - here
            remainder = remainder + beside_terms(before, here, after, x, tile, coefs, keep_last)
            if rest:
                left[x, tile] = remainder
            value = rho_next * rho * here + (2.0 * rho_next / cheb_radius) * jnp.where(inside, remainder, 0.0)
            if rest:
                update[sweep, x, tile] = value
            else:
                for k in range(CHEB - 1):
                    value = value + update[k, x, tile]
                estimate[x] = value
        rho = rho_next
    return estimate


def smooth(
    flags, wide, sides, past, even_in, odd_in, diagonal, coefs, corr, field_out, image_out, scratch
):
    source, left, update, whole = scratch
    inverse, b0, _, _ = coefs
    size_x, size_y, size_z = corr.shape
    rows = size_y + 2 * WIDE
    span = size_x + 2 * WIDE
    row = lax.broadcasted_iota(jnp.int32, (rows, size_z), 0)
    keep_last = lane_masks((rows, size_z))[1]
    has_low_x, has_high_x = flags[LOW_X] != 0, flags[HIGH_X] != 0
    has_low_y, has_high_y = flags[LOW_Y] != 0, flags[HIGH_Y] != 0
    lowest, highest = slice(0, 8), slice(rows - 8, rows)
    tile_row = lax.broadcasted_iota(jnp.int32, (8, size_z), 0)
    def halo(low, high):
        for k in range(WIDE):
            source[k] = inverse[k] * low[k]
            source[WIDE + size_x + k] = inverse[WIDE + size_x + k] * high[k]
        whole[0] = jnp.where(has_low_x, low[WIDE], 0.0)
        whole[size_x + 1] = jnp.where(has_high_x, high[WIDE], 0.0)

    @pl.when(flags[ODD_X] == 0)
    def _():
        halo(odd_in, even_in)

    @pl.when(flags[ODD_X] != 0)
    def _():
        halo(even_in, odd_in)

    for k in range(size_x):
        source[WIDE + k] = inverse[WIDE + k] * wide[k]

    low_in, high_in = WIDE, WIDE + size_x - 1
    source[low_in - 1] = source[low_in - 1] + inverse[low_in - 1] * sides[0]
    source[low_in] = source[low_in] + b0[low_in] * whole[0]
    source[high_in] = source[high_in] + inverse[high_in] * whole[size_x + 1]
    source[high_in + 1] = source[high_in + 1] + b0[high_in + 1] * sides[1]

    def run(planes, tile, inside, wanted):
        return chebyshev(
            planes,
            tile,
            inside,
            lambda x: source[x, tile],
            left,
            update,
            coefs,
            lane_masks(inside.shape)[1],
            wanted,
        )

    everything = slice(0, rows)
    box_rows = (row >= WIDE - DEPTH) & (row < WIDE + size_y + DEPTH)
    box_planes = range(WIDE - DEPTH, WIDE + size_x + DEPTH)
    own_planes = range(WIDE, WIDE + size_x)
    inner = (row >= WIDE) & (row < WIDE + size_y)

    beside = run(range(0, WIDE + DEPTH), everything, box_rows, (WIDE - 1,))[WIDE - 1]
    whole[0] = jnp.where(has_low_x & inner, whole[0] + beside, 0.0)
    x = WIDE + size_x
    beside = run(range(span - WIDE - DEPTH, span), everything, box_rows, (x,))[x]
    whole[size_x + 1] = jnp.where(has_high_x & inner, whole[size_x + 1] + beside, 0.0)

    own = run(box_planes, everything, box_rows, tuple(own_planes))
    zeros = jnp.zeros((rows - size_y, size_z), F32)
    for k in range(size_x):
        placed = pltpu.roll(jnp.concatenate([corr[k], zeros], axis=0), WIDE, 0)
        whole[k + 1] = jnp.where(inner, placed + own[WIDE + k], 0.0)

    beside = run(box_planes, lowest, tile_row < WIDE + DEPTH, tuple(own_planes))
    for k in range(size_x):
        line = past[0, k : k + 1, :] + beside[WIDE + k]
        here = has_low_y & (tile_row == WIDE - 1)
        whole[k + 1, lowest] = jnp.where(here, line, whole[k + 1, lowest])
    beside = run(box_planes, highest, tile_row >= 8 - WIDE - DEPTH, tuple(own_planes))
    for k in range(size_x):
        line = past[1, k : k + 1, :] + beside[WIDE + k]
        here = has_high_y & (tile_row == 8 - WIDE)
        whole[k + 1, highest] = jnp.where(here, line, whole[k + 1, highest])

    for k in range(size_x):
        x = WIDE + k
        terms = beside_terms(whole[k], whole[k + 1], whole[k + 2], x, everything, coefs, keep_last)
        image = diagonal[k] * (whole[k + 1] - terms)
        image_out[k] = pltpu.roll(image, rows - WIDE, 0)[0:size_y]
        field_out[k] = pltpu.roll(whole[k + 1], rows - WIDE, 0)[0:size_y]


def dot_planes(left, right):
    total = left[0] * right[0]
    for x in range(1, left.shape[0]):
        total = total + left[x] * right[x]
    return total


def search_kernel(
    flags, wide, sides, past, even_in, odd_in, diagonal, own0, own1, own2, own3, corr, even_vel, odd_vel, vectors, right_side,
    search, image, out, halo0, halo1, halo2, halo3, stage, wide_vel, *scratch
):
    halos = (halo0, halo1, halo2, halo3)
    halo_coefficients(flags, even_in, odd_in, even_vel, odd_vel, halos, wide_vel)
    coefs = [Region(*pair) for pair in zip((own0, own1, own2, own3), halos)]
    smooth(flags, wide, sides, past, even_in, odd_in, diagonal, coefs, corr, search, image, scratch)
    products = [dot_planes(right_side, right_side), dot_planes(right_side, image)]
    restrict(vectors, image, products, flags, (out, stage))


def smoothed_kernel(
    flags, wide, sides, past, even_in, odd_in, diagonal, own0, own1, own2, own3, corr, halo0, halo1, halo2, halo3, middle,
    smoothed, turned, out, stage, *scratch
):
    coefs = [Region(*pair) for pair in zip((own0, own1, own2, own3), (halo0, halo1, halo2, halo3))]
    smooth(flags, wide, sides, past, even_in, odd_in, diagonal, coefs, corr, smoothed, turned, scratch)
    stage[...] = jnp.zeros_like(stage)
    for k, total in enumerate((dot_planes(turned, middle), dot_planes(turned, turned))):
        total = jnp.sum(total, axis=0, keepdims=True)
        parts = [total[:, i : i + LANES] for i in range(0, total.shape[1], LANES)]
        stage[LANES + k : LANES + k + 1, :] = functools.reduce(jnp.add, parts)
    write_row(stage, out)


def last_kernel(flags, received, alpha, search, smoothed, middle, turned, solution_field, residual):
    _, sums = gathered(received)
    omega = sums[:, 0:1] / sums[:, 1:2]
    step = alpha[0:1, 0:1]
    for x in range(search.shape[0]):
        solution_field[x] = step * search[x] + omega * smoothed[x]
        residual[x] = middle[x] - omega * turned[x]


def local(right_side, velocity, deflation, inverse_rows):
    size_x, size_y, size_z = right_side.shape
    vectors_count = deflation.shape[0]
    count_x, count_y = lax.axis_size("gx"), lax.axis_size("gy")
    count = count_x * count_y
    at_x, at_y = lax.axis_index("gx"), lax.axis_index("gy")
    flags = jnp.stack(
        [
            at_x % 2,
            at_y % 2,
            (at_x > 0).astype(jnp.int32),
            (at_x < count_x - 1).astype(jnp.int32),
            (at_y > 0).astype(jnp.int32),
            (at_y < count_y - 1).astype(jnp.int32),
            (at_x * count_y + at_y) % (LANES // vectors_count),
            at_x,
        ]
    ).astype(jnp.int32)
    x_pairs, y_pairs = pair_permutations(count_x, count_y)

    def swap(messages, pairs):
        return [lax.ppermute(message, AXES, pair) for message, pair in zip(messages, pairs)]

    def share(row):
        return lax.all_to_all(row, AXES, 0, 0, tiled=True)

    rows = size_y + 2 * WIDE
    span = size_x + 2 * WIDE
    block = (size_x, size_y, size_z)
    row = (count, 2 * LANES)
    stage = (2 * LANES, LANES)
    y_message = (size_x + size_x // WIDE + 2, WIDE, size_z)
    region = (span, rows, size_z)
    smooth_scratch = [region, region, (CHEB - 1,) + region, (size_x + 2, rows, size_z)]

    rounded = lax.reduce_precision(right_side, 8, 7)
    partial = lax.optimization_barrier(jnp.sum(deflation.astype(F32) * rounded, axis=(1, 2)))
    share_count = LANES // vectors_count
    first_row = jnp.where(jnp.arange(2 * share_count)[:, None] == flags[SLOT], jnp.sum(partial, axis=1)[None, :], 0.0)
    first_row = jnp.broadcast_to(first_row.reshape(1, 2 * LANES), row)

    first = share(first_row)
    faces_y, faces_x = (3, size_x, WIDE, size_z), (3 * WIDE + 2, size_y, size_z)
    velocity_y = call(velocity_y_kernel, [faces_y] * 2, [], flags, velocity, first_row[0, :8], micros=0.01)
    after = velocity_y[0]
    velocity_y = swap(velocity_y, y_pairs)

    wide_own, wide_halo = (size_x, rows, size_z), (2 * WIDE, rows, size_z)

    def exchange(corr, rest, messages, corners):
        message = (WIDE + 1 + (WIDE if corners else 0), rows, size_z)
        *own, even, odd = call(
            functools.partial(extend_kernel, corners=corners),
            [wide_own, (2, rows, size_z), (2, size_x, size_z), message, message],
            [],
            flags,
            rest,
            corr,
            *swap(messages, y_pairs),
            velocity,
            *velocity_y,
            micros=0.01,
        )
        return (*own, *swap((even, odd), x_pairs), *coefs, corr)

    corr, rest, *messages, even_vel, odd_vel = call(
        coarse_kernel,
        [block, block, y_message, y_message, faces_x, faces_x],
        [],
        flags,
        first,
        inverse_rows,
        deflation,
        right_side,
        velocity,
        after,
        micros=1.4,
    )
    velocity_x = swap((even_vel, odd_vel), x_pairs)
    coefs = call(
        coefficients_kernel,
        [wide_own] * 5,
        [(3, size_x, rows, size_z)],
        flags,
        velocity,
        *velocity_y,
        micros=0.01,
    )
    search, image, second_row, *halo_coefs = call(
        search_kernel,
        [block, block, row] + [wide_halo] * 4,
        [stage, (3, rows, size_z)] + smooth_scratch,
        flags,
        *exchange(corr, rest, messages, True),
        *velocity_x,
        deflation,
        right_side,
        micros=3.0,
    )
    second = share(second_row)
    corr, rest, middle, alpha, *messages = call(
        second_coarse_kernel,
        [block, block, block, (8, LANES), y_message, y_message],
        [],
        flags,
        first,
        second,
        inverse_rows,
        deflation,
        right_side,
        image,
        velocity,
        micros=1.4,
    )
    smoothed, turned, third_row = call(
        smoothed_kernel,
        [block, block, row],
        [stage] + smooth_scratch,
        flags,
        *exchange(corr, rest, messages, False),
        *halo_coefs,
        middle,
        micros=2.5,
    )
    third = share(third_row)
    return tuple(
        call(last_kernel, [block, block], [], flags, third, alpha, search, smoothed, middle, turned, micros=1.4)
    )


def solution(mesh):
    return jax.shard_map(
        local,
        mesh=mesh,
        in_specs=(
            P("gx", "gy", None),
            P(None, "gx", "gy", None),
            P(None, "gx", "gy", None),
            P(("gx", "gy"), None),
        ),
        out_specs=(P("gx", "gy", None), P("gx", "gy", None)),
        check_vma=False,
    )
```

```python
import functools

import jax
import jax.numpy as jnp
from jax import lax
from jax.experimental import pallas as pl
from jax.experimental.pallas import tpu as pltpu
from jax.sharding import PartitionSpec as P

DEPTH = 2
CHEB = 4
WIDE = 4
LANES = 128
AXES = ("gx", "gy")
F32 = jnp.float32
HIGHEST = lax.Precision.HIGHEST

cheb_center = 1.0
cheb_radius = 0.9

ODD_X, ODD_Y, LOW_X, HIGH_X, LOW_Y, HIGH_Y, SLOT = range(7)

def pair_permutations(count_x, count_y):
    def number(i, j):
        return i * count_y + j

    even_x, odd_x, even_y, odd_y = [], [], [], []
    for i in range(count_x):
        for j in range(count_y):
            here = number(i, j)
            even_x.append((here, number(i ^ 1, j)))
            even_y.append((here, number(i, j ^ 1)))
            other = ((i - 1) ^ 1) + 1
            odd_x.append((here, number(other, j) if 0 <= other < count_x else number(i, j ^ 1)))
            other = ((j - 1) ^ 1) + 1
            odd_y.append((here, number(i, other) if 0 <= other < count_y else number(i ^ 1, j)))
    return (even_x, odd_x), (even_y, odd_y)


def place_flags(vectors_count):
    count_x, count_y = lax.axis_size("gx"), lax.axis_size("gy")
    at_x, at_y = lax.axis_index("gx"), lax.axis_index("gy")
    return (
        lax.rem(at_x, 2),
        lax.rem(at_y, 2),
        (at_x > 0).astype(jnp.int32),
        (at_x < count_x - 1).astype(jnp.int32),
        (at_y > 0).astype(jnp.int32),
        (at_y < count_y - 1).astype(jnp.int32),
        lax.rem(at_x * count_y + at_y, LANES // vectors_count),
    )


def call(vectors, body, outs, scratch, *args, micros):
    def kernel(*refs):
        body(place_flags(vectors), *refs)

    return pl.pallas_call(
        kernel,
        out_shape=[jax.ShapeDtypeStruct(shape, F32) for shape in outs],
        in_specs=[pl.BlockSpec(memory_space=pltpu.VMEM)] * len(args),
        out_specs=[pl.BlockSpec(memory_space=pltpu.VMEM)] * len(outs),
        scratch_shapes=[pltpu.VMEM(shape, F32) for shape in scratch],
        compiler_params=pltpu.CompilerParams(vmem_limit_bytes=24 * 1024 * 1024),
        cost_estimate=pl.CostEstimate(flops=0, bytes_accessed=int(micros * 3.6e6), transcendentals=0),
    )(*args)


def z_before(plane):
    return pltpu.roll(plane, 1, 1)


def z_after(plane, keep_last):
    return jnp.where(keep_last, pltpu.roll(plane, plane.shape[1] - 1, 1), 0.0)


def lane_masks(shape):
    lanes = lax.broadcasted_iota(jnp.int32, shape, 1)
    return lanes > 0, lanes < shape[1] - 1


def restrict(vectors, field, sums, flags, send, copies=()):
    count, size_x, size_y, size_z = vectors.shape
    stage = send[1]
    stage[...] = jnp.zeros_like(stage)

    def lanes_of(total):
        total = jnp.sum(total, axis=0, keepdims=True)
        return functools.reduce(jnp.add, [total[:, k : k + LANES] for k in range(0, size_z, LANES)])

    offset = pl.multiple_of(flags[SLOT] * count, count)
    for j in range(count):
        if copies and j % (count // len(copies)) == 0:
            copies[j // (count // len(copies))].wait()
        total = vectors[j, 0].astype(F32) * field[0]
        for x in range(1, size_x):
            total = total + vectors[j, x].astype(F32) * field[x]
        stage[pl.ds(offset + j, 1), :] = lanes_of(total)
    for k, total in enumerate(sums):
        stage[LANES + k : LANES + k + 1, :] = lanes_of(total)
    write_row(stage, send[0])


def write_row(stage, out):
    row = lax.dot_general(
        jnp.ones((8, LANES), F32), stage[...], (((1,), (1,)), ((), ())), precision=HIGHEST, preferred_element_type=F32
    )
    for k in range(0, out.shape[0], 8):
        out[k : k + 8, :] = row


def gathered(received):
    count = received.shape[0]
    return received[:, :LANES], jnp.sum(received[:, LANES:], axis=0, keepdims=True)


def solve(coarse, inverse, vectors):
    count = coarse.shape[0]
    share = LANES // vectors.shape[0]
    groups = count // share
    pick = (
        lax.broadcasted_iota(jnp.int32, (groups, count), 1) // share
        == lax.broadcasted_iota(jnp.int32, (groups, count), 0)
    ).astype(F32)
    packed = jnp.dot(pick, coarse, precision=HIGHEST, preferred_element_type=F32)
    total = inverse[:, :LANES] * packed[0:1]
    for k in range(1, groups):
        total = total + inverse[:, k * LANES : (k + 1) * LANES] * packed[k : k + 1]
    return jnp.sum(total, axis=1, keepdims=True).astype(jnp.bfloat16).astype(F32)


def prolong(solved, vectors, corr):
    count, size_x, size_y, size_z = vectors.shape
    totals = [jnp.zeros((size_y, size_z), F32) for _ in range(size_x)]
    for j in range(count):
        weight = jnp.broadcast_to(solved[j : j + 1], (size_y, size_z))
        for x in range(size_x):
            totals[x] = totals[x] + vectors[j, x].astype(F32) * weight
    for x in range(size_x):
        corr[x] = totals[x]


def subtract_own(field, corr, velocity, out):
    size_x, size_y, size_z = corr.shape
    keep_first, keep_last = lane_masks((size_y, size_z))
    rows = lax.broadcasted_iota(jnp.int32, (size_y, size_z), 0)
    for x in range(size_x):
        v0, v1, v2 = velocity[0, x], velocity[1, x], velocity[2, x]
        here = corr[x]
        image = (6.0 + v0 + v1 + v2) * here
        if x + 1 < size_x:
            image = image - corr[x + 1]
        if x > 0:
            image = image - (1.0 + v0) * corr[x - 1]
        image = image - jnp.where(rows < size_y - 1, pltpu.roll(here, size_y - 1, 0), 0.0)
        image = image - (1.0 + v1) * jnp.where(rows > 0, pltpu.roll(here, 1, 0), 0.0)
        image = image - z_after(here, keep_last) - (1.0 + v2) * jnp.where(keep_first, z_before(here), 0.0)
        out[x] = field[x] - image


def write_y_message(out, field, corr, high):
    size_x, size_y, _ = corr.shape
    start = size_y - WIDE if high else 0
    edge = size_y - 1 if high else 0
    for x in range(size_x):
        out[x] = field[x, start : start + WIDE, :]
        out[size_x + x // WIDE, x % WIDE : x % WIDE + 1, :] = corr[x, edge : edge + 1, :]
    last = size_x + size_x // WIDE
    out[last] = corr[0, start : start + WIDE, :]
    out[last + 1] = corr[size_x - 1, start : start + WIDE, :]


def by_parity(odd, write, even_out, odd_out):
    @pl.when(odd == 0)
    def _():
        write(even_out, True)
        write(odd_out, False)

    @pl.when(odd != 0)
    def _():
        write(even_out, False)
        write(odd_out, True)


def velocity_y_kernel(flags, velocity, after, even_out, odd_out):
    _, size_x, size_y, _ = velocity.shape

    def write_y(out, high):
        start = size_y - WIDE if high else 0
        for d in range(3):
            for x in range(size_x):
                out[d, x] = velocity[d, x, start : start + WIDE, :]

    by_parity(flags[ODD_Y], write_y, even_out, odd_out)


def write_velocity_x(flags, velocity, even_out, odd_out):
    size_x = velocity.shape[1]

    def write(out, high):
        start = size_x - WIDE if high else 0
        for d in range(3):
            for k in range(WIDE):
                out[d * WIDE + k] = velocity[d, start + k]
        for k in range(3 * WIDE, out.shape[0]):
            out[k] = jnp.zeros(out.shape[1:], F32)

    by_parity(flags[ODD_X], write, even_out, odd_out)


def coefficients(x, v0, v1, v2, kept, keep_first, outs):
    inverse, b0, b1, b2 = outs
    total = 6.0 + v0 + v1 + v2
    value = jnp.where(kept, 1.0 / total, 0.0)
    inverse[x] = value
    b0[x] = value * (1.0 + v0)
    b1[x] = value * (1.0 + v1)
    b2[x] = jnp.where(keep_first, value * (1.0 + v2), 0.0)
    return total


def rows_in_grid(flags, shape):
    row = lax.broadcasted_iota(jnp.int32, shape, 0)
    first_row = jnp.where(flags[LOW_Y] != 0, 0, WIDE)
    end_row = jnp.where(flags[HIGH_Y] != 0, shape[0], shape[0] - WIDE)
    return (row >= first_row) & (row < end_row)


def coefficients_kernel(flags, velocity, even_in, odd_in, diagonal, inverse, b0, b1, b2, wide):
    _, size_x, size_y, size_z = velocity.shape
    rows = size_y + 2 * WIDE

    def place(low, high):
        for d in range(3):
            for x in range(size_x):
                wide[d, x, 0:WIDE, :] = low[d, x]
                wide[d, x, WIDE : WIDE + size_y, :] = velocity[d, x]
                wide[d, x, WIDE + size_y : rows, :] = high[d, x]

    @pl.when(flags[ODD_Y] == 0)
    def _():
        place(odd_in, even_in)

    @pl.when(flags[ODD_Y] != 0)
    def _():
        place(even_in, odd_in)

    kept = rows_in_grid(flags, (rows, size_z))
    keep_first, _ = lane_masks((rows, size_z))
    for x in range(size_x):
        diagonal[x] = coefficients(x, wide[0, x], wide[1, x], wide[2, x], kept, keep_first, (inverse, b0, b1, b2))


def halo_coefficients(flags, even_in, odd_in, even_vel, odd_vel, outs, wide):
    size_y, size_z = even_vel.shape[1:]
    rows = size_y + 2 * WIDE
    kept = rows_in_grid(flags, (rows, size_z))
    keep_first, _ = lane_masks((rows, size_z))

    def side(start, message, faces, present):
        for k in range(WIDE):
            for d in range(3):
                wide[d, 0:WIDE, :] = message[WIDE + 1 + k, 8 * d : 8 * d + WIDE, :]
                wide[d, WIDE : WIDE + size_y, :] = faces[d * WIDE + k]
                wide[d, WIDE + size_y : rows, :] = message[WIDE + 1 + k, 8 * d + WIDE : 8 * d + 2 * WIDE, :]
            coefficients(start + k, wide[0], wide[1], wide[2], kept & (flags[present] != 0), keep_first, outs)

    @pl.when(flags[ODD_X] == 0)
    def _():
        side(0, odd_in, odd_vel, LOW_X)
        side(WIDE, even_in, even_vel, HIGH_X)

    @pl.when(flags[ODD_X] != 0)
    def _():
        side(0, even_in, even_vel, LOW_X)
        side(WIDE, odd_in, odd_vel, HIGH_X)


class Region:
    def __init__(self, own, halo):
        self.own, self.halo = own, halo

    def __getitem__(self, index):
        x, tile = index if isinstance(index, tuple) else (index, slice(None))
        size_x = self.own.shape[0]
        if x < WIDE:
            return self.halo[x, tile]
        return self.own[x - WIDE, tile] if x < WIDE + size_x else self.halo[x - size_x, tile]


def coarse_kernel(
    flags, received, inverse, vectors, field, velocity, after, corr, rest, even_out, odd_out, even_vel, odd_vel
):
    coarse, _ = gathered(received)
    prolong(solve(coarse, inverse, vectors), vectors, corr)
    subtract_own(field, corr, velocity, rest)
    by_parity(flags[ODD_Y], lambda out, high: write_y_message(out, rest, corr, high), even_out, odd_out)
    write_velocity_x(flags, velocity, even_vel, odd_vel)


def second_coarse_kernel(
    flags, received, second, inverse, vectors, field, image, velocity, corr, rest, middle, alpha, even_out, odd_out
):
    coarse, _ = gathered(received)
    coarse_image, products = gathered(second)
    step = jnp.broadcast_to(products[:, 0:1] / products[:, 1:2], alpha.shape)
    alpha[...] = step
    step = step[0:1, 0:1]
    for x in range(field.shape[0]):
        middle[x] = field[x] - step * image[x]
    prolong(solve(coarse - step * coarse_image, inverse, vectors), vectors, corr)
    subtract_own(middle, corr, velocity, rest)
    by_parity(flags[ODD_Y], lambda out, high: write_y_message(out, rest, corr, high), even_out, odd_out)


def extend_kernel(
    flags, rest, corr, even_in, odd_in, velocity, even_vel, odd_vel, wide, sides, past, even_out, odd_out, corners=True
):
    size_x, size_y, size_z = rest.shape
    rows = size_y + 2 * WIDE
    end = WIDE + size_y

    def place(low, high, high_vel):
        has_low, has_high = flags[LOW_Y] != 0, flags[HIGH_Y] != 0
        for x in range(size_x):
            at, line = size_x + x // WIDE, slice(x % WIDE, x % WIDE + 1)
            past_low = jnp.where(has_low, low[at, line, :], 0.0)
            past_high = jnp.where(has_high, high[at, line, :], 0.0)
            past[0, x : x + 1, :] = past_low
            past[1, x : x + 1, :] = past_high
            wide[x, 0 : WIDE - 1, :] = low[x, 0 : WIDE - 1, :]
            wide[x, WIDE - 1 : WIDE, :] = low[x, WIDE - 1 : WIDE, :] + corr[x, 0:1, :]
            wide[x, WIDE:end, :] = rest[x]
            wide[x, WIDE : WIDE + 1, :] = rest[x, 0:1, :] + (1.0 + velocity[1, x, 0:1, :]) * past_low
            wide[x, end - 1 : end, :] = rest[x, size_y - 1 : size_y, :] + past_high
            weight = 1.0 + high_vel[1, x, 0:1, :]
            wide[x, end : end + 1, :] = high[x, 0:1, :] + weight * corr[x, size_y - 1 : size_y, :]
            wide[x, end + 1 : rows, :] = high[x, 1:WIDE, :]
        last = size_x + size_x // WIDE
        for side, x in enumerate((0, size_x - 1)):
            sides[side, 0:WIDE, :] = low[last + side]
            sides[side, WIDE:end, :] = corr[x]
            sides[side, end:rows, :] = high[last + side]

    @pl.when(flags[ODD_Y] == 0)
    def _():
        place(odd_in, even_in, even_vel)

    @pl.when(flags[ODD_Y] != 0)
    def _():
        place(even_in, odd_in, odd_vel)

    def write(out, high):
        start = size_x - WIDE if high else 0
        for k in range(WIDE):
            out[k] = wide[start + k]
        out[WIDE] = sides[1 if high else 0]

    by_parity(flags[ODD_X], write, even_out, odd_out)
    if not corners:
        return

    def write_corners(low, high):
        def write(out, upper):
            start = size_x - WIDE if upper else 0
            for k in range(WIDE):
                for d in range(3):
                    out[WIDE + 1 + k, 8 * d : 8 * d + WIDE, :] = low[d, start + k]
                    out[WIDE + 1 + k, 8 * d + WIDE : 8 * d + 2 * WIDE, :] = high[d, start + k]

        by_parity(flags[ODD_X], write, even_out, odd_out)

    @pl.when(flags[ODD_Y] == 0)
    def _():
        write_corners(odd_vel, even_vel)

    @pl.when(flags[ODD_Y] != 0)
    def _():
        write_corners(even_vel, odd_vel)


def beside_terms(before, here, after, x, tile, coefs, keep_last):
    inverse, b0, b1, b2 = coefs
    rows = here.shape[0]
    ahead = pltpu.roll(here, rows - 1, 0) + z_after(here, keep_last)
    if after is not None:
        ahead = ahead + after
    total = inverse[x, tile] * ahead + b1[x, tile] * pltpu.roll(here, 1, 0) + b2[x, tile] * z_before(here)
    if before is not None:
        total = total + b0[x, tile] * before
    return total


def chebyshev(planes, tile, inside, source, left, update, coefs, keep_last, wanted):
    sigma = cheb_center / cheb_radius
    rho = 1.0 / sigma
    first, last = planes[0], planes[-1]
    for x in planes:
        update[0, x, tile] = jnp.where(inside, source(x), 0.0)
    estimate = {}
    for sweep in range(1, CHEB):
        rest = CHEB - 1 - sweep
        low, high = max(first, wanted[0] - rest), min(last, wanted[-1] + rest)
        rho_next = 1.0 / (2.0 * sigma - rho)
        for x in range(low, high + 1):
            here = update[sweep - 1, x, tile]
            before = update[sweep - 1, x - 1, tile] if x > first else None
            after = update[sweep - 1, x + 1, tile] if x < last else None
            remainder = (here if sweep == 1 else left[x, tile]) - here
            remainder = remainder + beside_terms(before, here, after, x, tile, coefs, keep_last)
            if rest:
                left[x, tile] = remainder
            value = rho_next * rho * here + (2.0 * rho_next / cheb_radius) * jnp.where(inside, remainder, 0.0)
            if rest:
                update[sweep, x, tile] = value
            else:
                for k in range(CHEB - 1):
                    value = value + update[k, x, tile]
                estimate[x] = value
        rho = rho_next
    return estimate


def smooth(
    flags, wide, sides, past, even_in, odd_in, diagonal, coefs, corr, field_out, image_out, scratch
):
    source, left, update, whole = scratch
    inverse, b0, _, _ = coefs
    size_x, size_y, size_z = corr.shape
    rows = size_y + 2 * WIDE
    span = size_x + 2 * WIDE
    row = lax.broadcasted_iota(jnp.int32, (rows, size_z), 0)
    keep_last = lane_masks((rows, size_z))[1]
    has_low_x, has_high_x = flags[LOW_X] != 0, flags[HIGH_X] != 0
    has_low_y, has_high_y = flags[LOW_Y] != 0, flags[HIGH_Y] != 0
    lowest, highest = slice(0, 8), slice(rows - 8, rows)
    tile_row = lax.broadcasted_iota(jnp.int32, (8, size_z), 0)
    def halo(low, high):
        for k in range(WIDE):
            source[k] = inverse[k] * low[k]
            source[WIDE + size_x + k] = inverse[WIDE + size_x + k] * high[k]
        whole[0] = jnp.where(has_low_x, low[WIDE], 0.0)
        whole[size_x + 1] = jnp.where(has_high_x, high[WIDE], 0.0)

    @pl.when(flags[ODD_X] == 0)
    def _():
        halo(odd_in, even_in)

    @pl.when(flags[ODD_X] != 0)
    def _():
        halo(even_in, odd_in)

    for k in range(size_x):
        source[WIDE + k] = inverse[WIDE + k] * wide[k]

    low_in, high_in = WIDE, WIDE + size_x - 1
    source[low_in - 1] = source[low_in - 1] + inverse[low_in - 1] * sides[0]
    source[low_in] = source[low_in] + b0[low_in] * whole[0]
    source[high_in] = source[high_in] + inverse[high_in] * whole[size_x + 1]
    source[high_in + 1] = source[high_in + 1] + b0[high_in + 1] * sides[1]

    def run(planes, tile, inside, wanted):
        return chebyshev(
            planes,
            tile,
            inside,
            lambda x: source[x, tile],
            left,
            update,
            coefs,
            lane_masks(inside.shape)[1],
            wanted,
        )

    everything = slice(0, rows)
    box_rows = (row >= WIDE - DEPTH) & (row < WIDE + size_y + DEPTH)
    box_planes = range(WIDE - DEPTH, WIDE + size_x + DEPTH)
    own_planes = range(WIDE, WIDE + size_x)
    inner = (row >= WIDE) & (row < WIDE + size_y)

    beside = run(range(0, WIDE + DEPTH), everything, box_rows, (WIDE - 1,))[WIDE - 1]
    whole[0] = jnp.where(has_low_x & inner, whole[0] + beside, 0.0)
    x = WIDE + size_x
    beside = run(range(span - WIDE - DEPTH, span), everything, box_rows, (x,))[x]
    whole[size_x + 1] = jnp.where(has_high_x & inner, whole[size_x + 1] + beside, 0.0)

    own = run(box_planes, everything, box_rows, tuple(own_planes))
    zeros = jnp.zeros((rows - size_y, size_z), F32)
    for k in range(size_x):
        placed = pltpu.roll(jnp.concatenate([corr[k], zeros], axis=0), WIDE, 0)
        whole[k + 1] = jnp.where(inner, placed + own[WIDE + k], 0.0)

    beside = run(box_planes, lowest, tile_row < WIDE + DEPTH, tuple(own_planes))
    for k in range(size_x):
        line = past[0, k : k + 1, :] + beside[WIDE + k]
        here = has_low_y & (tile_row == WIDE - 1)
        whole[k + 1, lowest] = jnp.where(here, line, whole[k + 1, lowest])
    beside = run(box_planes, highest, tile_row >= 8 - WIDE - DEPTH, tuple(own_planes))
    for k in range(size_x):
        line = past[1, k : k + 1, :] + beside[WIDE + k]
        here = has_high_y & (tile_row == 8 - WIDE)
        whole[k + 1, highest] = jnp.where(here, line, whole[k + 1, highest])

    for k in range(size_x):
        x = WIDE + k
        terms = beside_terms(whole[k], whole[k + 1], whole[k + 2], x, everything, coefs, keep_last)
        image = diagonal[k] * (whole[k + 1] - terms)
        image_out[k] = pltpu.roll(image, rows - WIDE, 0)[0:size_y]
        field_out[k] = pltpu.roll(whole[k + 1], rows - WIDE, 0)[0:size_y]


def dot_planes(left, right):
    total = left[0] * right[0]
    for x in range(1, left.shape[0]):
        total = total + left[x] * right[x]
    return total


def search_kernel(
    flags, wide, sides, past, even_in, odd_in, diagonal, own0, own1, own2, own3, corr, even_vel, odd_vel, vectors, right_side,
    search, image, out, halo0, halo1, halo2, halo3, stage, wide_vel, *scratch
):
    halos = (halo0, halo1, halo2, halo3)
    halo_coefficients(flags, even_in, odd_in, even_vel, odd_vel, halos, wide_vel)
    coefs = [Region(*pair) for pair in zip((own0, own1, own2, own3), halos)]
    smooth(flags, wide, sides, past, even_in, odd_in, diagonal, coefs, corr, search, image, scratch)
    products = [dot_planes(right_side, right_side), dot_planes(right_side, image)]
    restrict(vectors, image, products, flags, (out, stage))


def smoothed_kernel(
    flags, wide, sides, past, even_in, odd_in, diagonal, own0, own1, own2, own3, corr, halo0, halo1, halo2, halo3, middle,
    smoothed, turned, out, stage, *scratch
):
    coefs = [Region(*pair) for pair in zip((own0, own1, own2, own3), (halo0, halo1, halo2, halo3))]
    smooth(flags, wide, sides, past, even_in, odd_in, diagonal, coefs, corr, smoothed, turned, scratch)
    stage[...] = jnp.zeros_like(stage)
    for k, total in enumerate((dot_planes(turned, middle), dot_planes(turned, turned))):
        total = jnp.sum(total, axis=0, keepdims=True)
        parts = [total[:, i : i + LANES] for i in range(0, total.shape[1], LANES)]
        stage[LANES + k : LANES + k + 1, :] = functools.reduce(jnp.add, parts)
    write_row(stage, out)


def last_kernel(flags, received, alpha, search, smoothed, middle, turned, solution_field, residual):
    _, sums = gathered(received)
    omega = sums[:, 0:1] / sums[:, 1:2]
    step = alpha[0:1, 0:1]
    for x in range(search.shape[0]):
        solution_field[x] = step * search[x] + omega * smoothed[x]
        residual[x] = middle[x] - omega * turned[x]


def local(right_side, velocity, deflation, inverse_rows):
    size_x, size_y, size_z = right_side.shape
    vectors_count = deflation.shape[0]
    count_x, count_y = lax.axis_size("gx"), lax.axis_size("gy")
    count = count_x * count_y
    at_x, at_y = lax.axis_index("gx"), lax.axis_index("gy")
    flags = place_flags(vectors_count)
    kernel_call = functools.partial(call, vectors_count)
    x_pairs, y_pairs = pair_permutations(count_x, count_y)

    def swap(messages, pairs):
        return [lax.ppermute(message, AXES, pair) for message, pair in zip(messages, pairs)]

    def share(row):
        return lax.all_to_all(row, AXES, 0, 0, tiled=True)

    rows = size_y + 2 * WIDE
    span = size_x + 2 * WIDE
    block = (size_x, size_y, size_z)
    row = (count, 2 * LANES)
    stage = (2 * LANES, LANES)
    y_message = (size_x + size_x // WIDE + 2, WIDE, size_z)
    region = (span, rows, size_z)
    smooth_scratch = [region, region, (CHEB - 1,) + region, (size_x + 2, rows, size_z)]

    rounded = lax.reduce_precision(right_side, 8, 7)
    partial = lax.optimization_barrier(jnp.sum(deflation.astype(F32) * rounded, axis=(1, 2)))
    share_count = LANES // vectors_count
    first_row = jnp.where(jnp.arange(2 * share_count)[:, None] == flags[SLOT], jnp.sum(partial, axis=1)[None, :], 0.0)
    first_row = jnp.broadcast_to(first_row.reshape(1, 2 * LANES), row)

    first = share(first_row)
    faces_y, faces_x = (3, size_x, WIDE, size_z), (3 * WIDE + 2, size_y, size_z)
    velocity_y = kernel_call(velocity_y_kernel, [faces_y] * 2, [], velocity, first_row[0, :8], micros=0.01)
    after = velocity_y[0]
    velocity_y = swap(velocity_y, y_pairs)

    wide_own, wide_halo = (size_x, rows, size_z), (2 * WIDE, rows, size_z)

    def exchange(corr, rest, messages, corners):
        message = (WIDE + 1 + (WIDE if corners else 0), rows, size_z)
        *own, even, odd = kernel_call(
            functools.partial(extend_kernel, corners=corners),
            [wide_own, (2, rows, size_z), (2, size_x, size_z), message, message],
            [],
            rest,
            corr,
            *swap(messages, y_pairs),
            velocity,
            *velocity_y,
            micros=0.01,
        )
        return (*own, *swap((even, odd), x_pairs), *coefs, corr)

    corr, rest, *messages, even_vel, odd_vel = kernel_call(
        coarse_kernel,
        [block, block, y_message, y_message, faces_x, faces_x],
        [],
        first,
        inverse_rows,
        deflation,
        right_side,
        velocity,
        after,
        micros=1.4,
    )
    velocity_x = swap((even_vel, odd_vel), x_pairs)
    coefs = kernel_call(
        coefficients_kernel,
        [wide_own] * 5,
        [(3, size_x, rows, size_z)],
        velocity,
        *velocity_y,
        micros=0.01,
    )
    search, image, second_row, *halo_coefs = kernel_call(
        search_kernel,
        [block, block, row] + [wide_halo] * 4,
        [stage, (3, rows, size_z)] + smooth_scratch,
        *exchange(corr, rest, messages, True),
        *velocity_x,
        deflation,
        right_side,
        micros=3.0,
    )
    second = share(second_row)
    corr, rest, middle, alpha, *messages = kernel_call(
        second_coarse_kernel,
        [block, block, block, (8, LANES), y_message, y_message],
        [],
        first,
        second,
        inverse_rows,
        deflation,
        right_side,
        image,
        velocity,
        micros=1.4,
    )
    smoothed, turned, third_row = kernel_call(
        smoothed_kernel,
        [block, block, row],
        [stage] + smooth_scratch,
        *exchange(corr, rest, messages, False),
        *halo_coefs,
        middle,
        micros=2.5,
    )
    third = share(third_row)
    return tuple(
        kernel_call(last_kernel, [block, block], [], third, alpha, search, smoothed, middle, turned, micros=1.4)
    )


def solution(mesh):
    return jax.shard_map(
        local,
        mesh=mesh,
        in_specs=(
            P("gx", "gy", None),
            P(None, "gx", "gy", None),
            P(None, "gx", "gy", None),
            P(("gx", "gy"), None),
        ),
        out_specs=(P("gx", "gy", None), P("gx", "gy", None)),
        check_vma=False,
    )
```

```python
import functools

import jax
import jax.numpy as jnp
from jax import lax
from jax.experimental import pallas as pl
from jax.experimental.pallas import tpu as pltpu
from jax.sharding import PartitionSpec as P

DEPTH = 2
CHEB = 4
WIDE = 4
EARLY_FIRST = 1
SPARE = 3
LANES = 128
AXES = ("gx", "gy")
F32 = jnp.float32
HIGHEST = lax.Precision.HIGHEST

cheb_center = 1.0
cheb_radius = 0.9

ODD_X, ODD_Y, LOW_X, HIGH_X, LOW_Y, HIGH_Y, SLOT = range(7)

def pair_permutations(count_x, count_y):
    def number(i, j):
        return i * count_y + j

    even_x, odd_x, even_y, odd_y = [], [], [], []
    for i in range(count_x):
        for j in range(count_y):
            here = number(i, j)
            even_x.append((here, number(i ^ 1, j)))
            even_y.append((here, number(i, j ^ 1)))
            other = ((i - 1) ^ 1) + 1
            odd_x.append((here, number(other, j) if 0 <= other < count_x else number(i, j ^ 1)))
            other = ((j - 1) ^ 1) + 1
            odd_y.append((here, number(i, other) if 0 <= other < count_y else number(i ^ 1, j)))
    return (even_x, odd_x), (even_y, odd_y)


def place_flags(vectors_count):
    count_x, count_y = lax.axis_size("gx"), lax.axis_size("gy")
    at_x, at_y = lax.axis_index("gx"), lax.axis_index("gy")
    return (
        lax.rem(at_x, 2),
        lax.rem(at_y, 2),
        (at_x > 0).astype(jnp.int32),
        (at_x < count_x - 1).astype(jnp.int32),
        (at_y > 0).astype(jnp.int32),
        (at_y < count_y - 1).astype(jnp.int32),
        lax.rem(at_x * count_y + at_y, LANES // vectors_count),
    )


def call(vectors, body, outs, scratch, *args, micros):
    def kernel(*refs):
        body(place_flags(vectors), *refs)

    return pl.pallas_call(
        kernel,
        out_shape=[jax.ShapeDtypeStruct(shape, F32) for shape in outs],
        in_specs=[pl.BlockSpec(memory_space=pltpu.VMEM)] * len(args),
        out_specs=[pl.BlockSpec(memory_space=pltpu.VMEM)] * len(outs),
        scratch_shapes=[pltpu.VMEM(shape, F32) for shape in scratch],
        compiler_params=pltpu.CompilerParams(vmem_limit_bytes=24 * 1024 * 1024),
        cost_estimate=pl.CostEstimate(flops=0, bytes_accessed=int(micros * 3.6e6), transcendentals=0),
    )(*args)


def z_before(plane):
    return pltpu.roll(plane, 1, 1)


def z_after(plane, keep_last):
    return jnp.where(keep_last, pltpu.roll(plane, plane.shape[1] - 1, 1), 0.0)


def lane_masks(shape):
    lanes = lax.broadcasted_iota(jnp.int32, shape, 1)
    return lanes > 0, lanes < shape[1] - 1


def restrict(vectors, field, sums, flags, send, copies=()):
    count, size_x, size_y, size_z = vectors.shape
    stage = send[1]
    stage[...] = jnp.zeros_like(stage)

    def lanes_of(total):
        total = jnp.sum(total, axis=0, keepdims=True)
        return functools.reduce(jnp.add, [total[:, k : k + LANES] for k in range(0, size_z, LANES)])

    offset = pl.multiple_of(flags[SLOT] * count, count)
    for j in range(count):
        if copies and j % (count // len(copies)) == 0:
            copies[j // (count // len(copies))].wait()
        total = vectors[j, 0].astype(F32) * field[0]
        for x in range(1, size_x):
            total = total + vectors[j, x].astype(F32) * field[x]
        stage[pl.ds(offset + j, 1), :] = lanes_of(total)
    for k, total in enumerate(sums):
        stage[LANES + k : LANES + k + 1, :] = lanes_of(total)
    write_row(stage, send[0])


def write_row(stage, out):
    row = lax.dot_general(
        jnp.ones((8, LANES), F32), stage[...], (((1,), (1,)), ((), ())), precision=HIGHEST, preferred_element_type=F32
    )
    for k in range(0, out.shape[0], 8):
        out[k : k + 8, :] = row


def gathered(received):
    count = received.shape[0]
    return received[:, :LANES], jnp.sum(received[:, LANES:], axis=0, keepdims=True)


def solve(coarse, inverse, vectors):
    count = coarse.shape[0]
    share = LANES // vectors.shape[0]
    groups = count // share
    pick = (
        lax.broadcasted_iota(jnp.int32, (groups, count), 1) // share
        == lax.broadcasted_iota(jnp.int32, (groups, count), 0)
    ).astype(F32)
    packed = jnp.dot(pick, coarse, precision=HIGHEST, preferred_element_type=F32)
    total = inverse[:, :LANES] * packed[0:1]
    for k in range(1, groups):
        total = total + inverse[:, k * LANES : (k + 1) * LANES] * packed[k : k + 1]
    return jnp.sum(total, axis=1, keepdims=True).astype(jnp.bfloat16).astype(F32)


def prolong(solved, vectors, corr):
    count, size_x, size_y, size_z = vectors.shape
    totals = [jnp.zeros((size_y, size_z), F32) for _ in range(size_x)]
    for j in range(count):
        weight = jnp.broadcast_to(solved[j : j + 1], (size_y, size_z))
        for x in range(size_x):
            totals[x] = totals[x] + vectors[j, x].astype(F32) * weight
    for x in range(size_x):
        corr[x] = totals[x]


def subtract_own(field, corr, velocity, out):
    size_x, size_y, size_z = corr.shape
    keep_first, keep_last = lane_masks((size_y, size_z))
    rows = lax.broadcasted_iota(jnp.int32, (size_y, size_z), 0)
    for x in range(size_x):
        v0, v1, v2 = velocity[0, x], velocity[1, x], velocity[2, x]
        here = corr[x]
        image = (6.0 + v0 + v1 + v2) * here
        if x + 1 < size_x:
            image = image - corr[x + 1]
        if x > 0:
            image = image - (1.0 + v0) * corr[x - 1]
        image = image - jnp.where(rows < size_y - 1, pltpu.roll(here, size_y - 1, 0), 0.0)
        image = image - (1.0 + v1) * jnp.where(rows > 0, pltpu.roll(here, 1, 0), 0.0)
        image = image - z_after(here, keep_last) - (1.0 + v2) * jnp.where(keep_first, z_before(here), 0.0)
        out[x] = field[x] - image


def write_y_message(out, field, corr, high):
    size_x, size_y, _ = corr.shape
    start = size_y - WIDE if high else 0
    edge = size_y - 1 if high else 0
    for x in range(size_x):
        out[x] = field[x, start : start + WIDE, :]
        out[size_x + x // WIDE, x % WIDE : x % WIDE + 1, :] = corr[x, edge : edge + 1, :]
    last = size_x + size_x // WIDE
    out[last] = corr[0, start : start + WIDE, :]
    out[last + 1] = corr[size_x - 1, start : start + WIDE, :]


def by_parity(odd, write, even_out, odd_out):
    @pl.when(odd == 0)
    def _():
        write(even_out, True)
        write(odd_out, False)

    @pl.when(odd != 0)
    def _():
        write(even_out, False)
        write(odd_out, True)


def by_side(odd, use, *pairs):
    evens, odds = [pair[0] for pair in pairs], [pair[1] for pair in pairs]

    @pl.when(odd == 0)
    def _():
        use(odds, evens)

    @pl.when(odd != 0)
    def _():
        use(evens, odds)


def velocity_y_kernel(flags, velocity, after, even_out, odd_out):
    _, size_x, size_y, _ = velocity.shape

    def write_y(out, high):
        start = size_y - WIDE if high else 0
        for d in range(3):
            for x in range(size_x):
                out[d, x] = velocity[d, x, start : start + WIDE, :]

    by_parity(flags[ODD_Y], write_y, even_out, odd_out)


def write_x_early(flags, planes, rest, corr, velocity, even_out, odd_out):
    size_x = rest.shape[0]

    def write(out, high):
        start = size_x - WIDE if high else 0
        out[0] = corr[size_x - 1 if high else 0]
        for k in range(planes):
            out[1 + k] = rest[start + k]
        if velocity is not None:
            for d in range(3):
                for k in range(WIDE):
                    out[1 + planes + d * WIDE + k] = velocity[d, start + k]

    by_parity(flags[ODD_X], write, even_out, odd_out)


def coefficients(x, v0, v1, v2, kept, keep_first, outs):
    inverse, b0, b1, b2 = outs
    total = 6.0 + v0 + v1 + v2
    value = jnp.where(kept, 1.0 / total, 0.0)
    inverse[x] = value
    b0[x] = value * (1.0 + v0)
    b1[x] = value * (1.0 + v1)
    b2[x] = jnp.where(keep_first, value * (1.0 + v2), 0.0)
    return total


def rows_in_grid(flags, shape):
    row = lax.broadcasted_iota(jnp.int32, shape, 0)
    first_row = jnp.where(flags[LOW_Y] != 0, 0, WIDE)
    end_row = jnp.where(flags[HIGH_Y] != 0, shape[0], shape[0] - WIDE)
    return (row >= first_row) & (row < end_row)


def coefficients_kernel(flags, velocity, even_in, odd_in, diagonal, inverse, b0, b1, b2, wide):
    _, size_x, size_y, size_z = velocity.shape
    rows = size_y + 2 * WIDE

    def place(low, high):
        for d in range(3):
            for x in range(size_x):
                wide[d, x, 0:WIDE, :] = low[d, x]
                wide[d, x, WIDE : WIDE + size_y, :] = velocity[d, x]
                wide[d, x, WIDE + size_y : rows, :] = high[d, x]

    @pl.when(flags[ODD_Y] == 0)
    def _():
        place(odd_in, even_in)

    @pl.when(flags[ODD_Y] != 0)
    def _():
        place(even_in, odd_in)

    kept = rows_in_grid(flags, (rows, size_z))
    keep_first, _ = lane_masks((rows, size_z))
    for x in range(size_x):
        diagonal[x] = coefficients(x, wide[0, x], wide[1, x], wide[2, x], kept, keep_first, (inverse, b0, b1, b2))


def halo_coefficients(flags, early, late, outs, wide):
    size_y, size_z = early[0].shape[1:]
    rows = size_y + 2 * WIDE
    kept = rows_in_grid(flags, (rows, size_z))
    keep_first, _ = lane_masks((rows, size_z))

    def side(start, message, corners, present):
        for k in range(WIDE):
            for d in range(3):
                tile = WIDE + 2 + d * WIDE + k
                wide[d, 0:WIDE, :] = corners[tile, 0:WIDE, :]
                wide[d, WIDE : WIDE + size_y, :] = message[1 + EARLY_FIRST + d * WIDE + k]
                wide[d, WIDE + size_y : rows, :] = corners[tile, WIDE : 2 * WIDE, :]
            coefficients(start + k, wide[0], wide[1], wide[2], kept & (flags[present] != 0), keep_first, outs)

    by_side(flags[ODD_X], lambda low, high: (side(0, *low, LOW_X), side(WIDE, *high, HIGH_X)), early, late)


class Region:
    def __init__(self, own, halo):
        self.own, self.halo = own, halo

    def __getitem__(self, index):
        x, tile = index if isinstance(index, tuple) else (index, slice(None))
        size_x = self.own.shape[0]
        if x < WIDE:
            return self.halo[x, tile]
        return self.own[x - WIDE, tile] if x < WIDE + size_x else self.halo[x - size_x, tile]


def coarse_kernel(
    flags, received, inverse, vectors, field, velocity, after, corr, rest, even_out, odd_out, even_x, odd_x
):
    coarse, _ = gathered(received)
    prolong(solve(coarse, inverse, vectors), vectors, corr)
    subtract_own(field, corr, velocity, rest)
    by_parity(flags[ODD_Y], lambda out, high: write_y_message(out, rest, corr, high), even_out, odd_out)
    write_x_early(flags, EARLY_FIRST, rest, corr, velocity, even_x, odd_x)


def second_coarse_kernel(
    flags, received, second, inverse, vectors, field, image, velocity, corr, rest, middle, alpha, even_out, odd_out,
    even_x, odd_x
):
    coarse, _ = gathered(received)
    coarse_image, products = gathered(second)
    step = jnp.broadcast_to(products[:, 0:1] / products[:, 1:2], alpha.shape)
    alpha[...] = step
    step = step[0:1, 0:1]
    for x in range(field.shape[0]):
        middle[x] = field[x] - step * image[x]
    prolong(solve(coarse - step * coarse_image, inverse, vectors), vectors, corr)
    subtract_own(middle, corr, velocity, rest)
    by_parity(flags[ODD_Y], lambda out, high: write_y_message(out, rest, corr, high), even_out, odd_out)
    write_x_early(flags, WIDE, rest, corr, None, even_x, odd_x)


def extend_kernel(
    flags, rest, corr, odd_in, even_in, velocity, even_vel, odd_vel, wide, sides, past, even_out, odd_out, corners, early_planes
):
    size_x, size_y, size_z = rest.shape
    rows = size_y + 2 * WIDE
    end = WIDE + size_y

    def place(low, high, high_vel):
        has_low, has_high = flags[LOW_Y] != 0, flags[HIGH_Y] != 0
        for x in range(size_x):
            at, line = size_x + x // WIDE, slice(x % WIDE, x % WIDE + 1)
            past_low = jnp.where(has_low, low[at, line, :], 0.0)
            past_high = jnp.where(has_high, high[at, line, :], 0.0)
            past[0, x : x + 1, :] = past_low
            past[1, x : x + 1, :] = past_high
            wide[x, 0 : WIDE - 1, :] = low[x, 0 : WIDE - 1, :]
            wide[x, WIDE - 1 : WIDE, :] = low[x, WIDE - 1 : WIDE, :] + corr[x, 0:1, :]
            wide[x, WIDE:end, :] = rest[x]
            wide[x, WIDE : WIDE + 1, :] = rest[x, 0:1, :] + (1.0 + velocity[1, x, 0:1, :]) * past_low
            wide[x, end - 1 : end, :] = rest[x, size_y - 1 : size_y, :] + past_high
            weight = 1.0 + high_vel[1, x, 0:1, :]
            wide[x, end : end + 1, :] = high[x, 0:1, :] + weight * corr[x, size_y - 1 : size_y, :]
            wide[x, end + 1 : rows, :] = high[x, 1:WIDE, :]
        last = size_x + size_x // WIDE
        for side, x in enumerate((0, size_x - 1)):
            sides[side, 0:WIDE, :] = low[last + side]
            sides[side, WIDE:end, :] = corr[x]
            sides[side, end:rows, :] = high[last + side]

    @pl.when(flags[ODD_Y] == 0)
    def _():
        place(odd_in, even_in, even_vel)

    @pl.when(flags[ODD_Y] != 0)
    def _():
        place(even_in, odd_in, odd_vel)

    def write(out, high):
        start = size_x - WIDE if high else 0
        for k in range(WIDE):
            out[k, 0:WIDE, :] = wide[start + k, 0:WIDE, :]
            out[k, WIDE : 2 * WIDE, :] = wide[start + k, end:rows, :]
        side = 1 if high else 0
        out[WIDE, 0:WIDE, :] = sides[side, 0:WIDE, :]
        out[WIDE, WIDE : 2 * WIDE, :] = sides[side, end:rows, :]
        out[WIDE + 1, 0:WIDE, :] = past[0, start : start + WIDE, :]
        out[WIDE + 1, WIDE : 2 * WIDE, :] = past[1, start : start + WIDE, :]

        tile = WIDE + 2 + (3 * WIDE if corners else 0)
        for k in range(early_planes, WIDE):
            for row in range(0, size_y, 8):
                out[tile] = rest[start + k, row : row + 8, :]
                tile += 1

    by_parity(flags[ODD_X], write, even_out, odd_out)
    if not corners:
        return

    def write_corners(low, high):
        def write(out, upper):
            start = size_x - WIDE if upper else 0
            for d in range(3):
                for k in range(WIDE):
                    tile = WIDE + 2 + d * WIDE + k
                    out[tile, 0:WIDE, :] = low[0][d, start + k]
                    out[tile, WIDE : 2 * WIDE, :] = high[0][d, start + k]

        by_parity(flags[ODD_X], write, even_out, odd_out)

    by_side(flags[ODD_Y], write_corners, (even_vel, odd_vel))


def beside_terms(before, here, after, x, tile, coefs, keep_last):
    inverse, b0, b1, b2 = coefs
    rows = here.shape[0]
    ahead = pltpu.roll(here, rows - 1, 0) + z_after(here, keep_last)
    if after is not None:
        ahead = ahead + after
    total = inverse[x, tile] * ahead + b1[x, tile] * pltpu.roll(here, 1, 0) + b2[x, tile] * z_before(here)
    if before is not None:
        total = total + b0[x, tile] * before
    return total


def chebyshev(planes, tile, inside, source, left, update, coefs, keep_last, wanted):
    sigma = cheb_center / cheb_radius
    rho = 1.0 / sigma
    first, last = planes[0], planes[-1]
    for x in planes:
        update[0, x, tile] = jnp.where(inside, source(x), 0.0)
    estimate = {}
    for sweep in range(1, CHEB):
        rest = CHEB - 1 - sweep
        low, high = max(first, wanted[0] - rest), min(last, wanted[-1] + rest)
        rho_next = 1.0 / (2.0 * sigma - rho)
        for x in range(low, high + 1):
            here = update[sweep - 1, x, tile]
            before = update[sweep - 1, x - 1, tile] if x > first else None
            after = update[sweep - 1, x + 1, tile] if x < last else None
            remainder = (here if sweep == 1 else left[x, tile]) - here
            remainder = remainder + beside_terms(before, here, after, x, tile, coefs, keep_last)
            if rest:
                left[x, tile] = remainder
            value = rho_next * rho * here + (2.0 * rho_next / cheb_radius) * jnp.where(inside, remainder, 0.0)
            if rest:
                update[sweep, x, tile] = value
            else:
                for k in range(CHEB - 1):
                    value = value + update[k, x, tile]
                estimate[x] = value
        rho = rho_next
    return estimate


def smooth(
    flags, early_planes, wide, sides, past, early, late, diagonal, coefs, corr, field_out, image_out, scratch
):
    source, left, update, whole = scratch
    inverse, b0, b1, _ = coefs
    size_x, size_y, size_z = corr.shape
    rows = size_y + 2 * WIDE
    span = size_x + 2 * WIDE
    row = lax.broadcasted_iota(jnp.int32, (rows, size_z), 0)
    keep_last = lane_masks((rows, size_z))[1]
    has_low_x, has_high_x = flags[LOW_X] != 0, flags[HIGH_X] != 0
    has_low_y, has_high_y = flags[LOW_Y] != 0, flags[HIGH_Y] != 0
    lowest, highest = slice(0, 8), slice(rows - 8, rows)
    tile_row = lax.broadcasted_iota(jnp.int32, (8, size_z), 0)
    end = WIDE + size_y

    def put(out, x, middle, ends):
        out[x, 0:WIDE, :] = ends[0:WIDE, :]
        for row_ in range(0, size_y, 8):
            out[x, WIDE + row_ : WIDE + row_ + 8, :] = middle(row_)
        out[x, end:rows, :] = ends[WIDE : 2 * WIDE, :]

    def halo(side, first, edge, present):
        message, ends = side
        for k in range(WIDE):
            x = first + k
            if k < early_planes:
                middle = lambda row_: message[1 + k, row_ : row_ + 8, :]
            else:
                tile = ends.shape[0] - SPARE - (WIDE - k) * (size_y // 8)
                middle = lambda row_: ends[tile + row_ // 8]
            put(source, x, middle, ends.at[k])
            source[x] = inverse[x] * source[x]
            for row_, weight, line in ((WIDE, b1, k), (end - 1, inverse, WIDE + k)):
                at = slice(row_, row_ + 1)
                source[x, at] = source[x, at] + weight[x, at] * ends[WIDE + 1, line : line + 1, :]
        put(whole, edge, lambda row_: message[0, row_ : row_ + 8, :], ends.at[WIDE])
        whole[edge] = jnp.where(present, whole[edge], 0.0)

    def halos(low, high):
        halo(low, 0, 0, has_low_x)
        halo(high, WIDE + size_x, size_x + 1, has_high_x)

    by_side(flags[ODD_X], halos, early, late)

    for k in range(size_x):
        source[WIDE + k] = inverse[WIDE + k] * wide[k]

    low_in, high_in = WIDE, WIDE + size_x - 1
    source[low_in - 1] = source[low_in - 1] + inverse[low_in - 1] * sides[0]
    source[low_in] = source[low_in] + b0[low_in] * whole[0]
    source[high_in] = source[high_in] + inverse[high_in] * whole[size_x + 1]
    source[high_in + 1] = source[high_in + 1] + b0[high_in + 1] * sides[1]

    def run(planes, tile, inside, wanted):
        return chebyshev(
            planes,
            tile,
            inside,
            lambda x: source[x, tile],
            left,
            update,
            coefs,
            lane_masks(inside.shape)[1],
            wanted,
        )

    everything = slice(0, rows)
    box_rows = (row >= WIDE - DEPTH) & (row < WIDE + size_y + DEPTH)
    box_planes = range(WIDE - DEPTH, WIDE + size_x + DEPTH)
    own_planes = range(WIDE, WIDE + size_x)
    inner = (row >= WIDE) & (row < WIDE + size_y)

    beside = run(range(0, WIDE + DEPTH), everything, box_rows, (WIDE - 1,))[WIDE - 1]
    whole[0] = jnp.where(has_low_x & inner, whole[0] + beside, 0.0)
    x = WIDE + size_x
    beside = run(range(span - WIDE - DEPTH, span), everything, box_rows, (x,))[x]
    whole[size_x + 1] = jnp.where(has_high_x & inner, whole[size_x + 1] + beside, 0.0)

    own = run(box_planes, everything, box_rows, tuple(own_planes))
    zeros = jnp.zeros((rows - size_y, size_z), F32)
    for k in range(size_x):
        placed = pltpu.roll(jnp.concatenate([corr[k], zeros], axis=0), WIDE, 0)
        whole[k + 1] = jnp.where(inner, placed + own[WIDE + k], 0.0)

    beside = run(box_planes, lowest, tile_row < WIDE + DEPTH, tuple(own_planes))
    for k in range(size_x):
        line = past[0, k : k + 1, :] + beside[WIDE + k]
        here = has_low_y & (tile_row == WIDE - 1)
        whole[k + 1, lowest] = jnp.where(here, line, whole[k + 1, lowest])
    beside = run(box_planes, highest, tile_row >= 8 - WIDE - DEPTH, tuple(own_planes))
    for k in range(size_x):
        line = past[1, k : k + 1, :] + beside[WIDE + k]
        here = has_high_y & (tile_row == 8 - WIDE)
        whole[k + 1, highest] = jnp.where(here, line, whole[k + 1, highest])

    for k in range(size_x):
        x = WIDE + k
        terms = beside_terms(whole[k], whole[k + 1], whole[k + 2], x, everything, coefs, keep_last)
        image = diagonal[k] * (whole[k + 1] - terms)
        image_out[k] = pltpu.roll(image, rows - WIDE, 0)[0:size_y]
        field_out[k] = pltpu.roll(whole[k + 1], rows - WIDE, 0)[0:size_y]


def dot_planes(left, right):
    total = left[0] * right[0]
    for x in range(1, left.shape[0]):
        total = total + left[x] * right[x]
    return total


def search_kernel(
    flags, wide, sides, past, odd_late, even_late, diagonal, own0, own1, own2, own3, corr, odd_early, even_early, vectors,
    right_side, search, image, out, halo0, halo1, halo2, halo3, stage, wide_vel, *scratch
):
    halos = (halo0, halo1, halo2, halo3)
    early, late = (even_early, odd_early), (even_late, odd_late)
    halo_coefficients(flags, early, late, halos, wide_vel)
    coefs = [Region(*pair) for pair in zip((own0, own1, own2, own3), halos)]
    smooth(flags, EARLY_FIRST, wide, sides, past, early, late, diagonal, coefs, corr, search, image, scratch)
    products = [dot_planes(right_side, right_side), dot_planes(right_side, image)]
    restrict(vectors, image, products, flags, (out, stage))


def smoothed_kernel(
    flags, wide, sides, past, odd_late, even_late, diagonal, own0, own1, own2, own3, corr, odd_early, even_early, halo0,
    halo1, halo2, halo3, middle, smoothed, turned, out, stage, *scratch
):
    early, late = (even_early, odd_early), (even_late, odd_late)
    coefs = [Region(*pair) for pair in zip((own0, own1, own2, own3), (halo0, halo1, halo2, halo3))]
    smooth(flags, WIDE, wide, sides, past, early, late, diagonal, coefs, corr, smoothed, turned, scratch)
    stage[...] = jnp.zeros_like(stage)
    for k, total in enumerate((dot_planes(turned, middle), dot_planes(turned, turned))):
        total = jnp.sum(total, axis=0, keepdims=True)
        parts = [total[:, i : i + LANES] for i in range(0, total.shape[1], LANES)]
        stage[LANES + k : LANES + k + 1, :] = functools.reduce(jnp.add, parts)
    write_row(stage, out)


def last_kernel(flags, received, alpha, search, smoothed, middle, turned, solution_field, residual):
    _, sums = gathered(received)
    omega = sums[:, 0:1] / sums[:, 1:2]
    step = alpha[0:1, 0:1]
    for x in range(search.shape[0]):
        solution_field[x] = step * search[x] + omega * smoothed[x]
        residual[x] = middle[x] - omega * turned[x]


def local(right_side, velocity, deflation, inverse_rows):
    size_x, size_y, size_z = right_side.shape
    vectors_count = deflation.shape[0]
    count_x, count_y = lax.axis_size("gx"), lax.axis_size("gy")
    count = count_x * count_y
    at_x, at_y = lax.axis_index("gx"), lax.axis_index("gy")
    flags = place_flags(vectors_count)
    kernel_call = functools.partial(call, vectors_count)
    x_pairs, y_pairs = pair_permutations(count_x, count_y)

    def swap(messages, pairs):
        odd = lax.ppermute(messages[1], AXES, pairs[1])
        return [lax.ppermute(messages[0], AXES, pairs[0]), odd]

    def share(row):
        return lax.all_to_all(row, AXES, 0, 0, tiled=True)

    rows = size_y + 2 * WIDE
    span = size_x + 2 * WIDE
    block = (size_x, size_y, size_z)
    row = (count, 2 * LANES)
    stage = (2 * LANES, LANES)
    y_message = (size_x + size_x // WIDE + 2, WIDE, size_z)
    region = (span, rows, size_z)
    smooth_scratch = [region, region, (CHEB - 1,) + region, (size_x + 2, rows, size_z)]

    rounded = lax.reduce_precision(right_side, 8, 7)
    partial = lax.optimization_barrier(jnp.sum(deflation.astype(F32) * rounded, axis=(1, 2)))
    share_count = LANES // vectors_count
    first_row = jnp.where(jnp.arange(2 * share_count)[:, None] == flags[SLOT], jnp.sum(partial, axis=1)[None, :], 0.0)
    first_row = jnp.broadcast_to(first_row.reshape(1, 2 * LANES), row)

    first = share(first_row)
    faces_y = (3, size_x, WIDE, size_z)
    x_early = (WIDE + 1, size_y, size_z)
    x_early_first = (1 + EARLY_FIRST + 3 * WIDE, size_y, size_z)
    velocity_y = kernel_call(velocity_y_kernel, [faces_y] * 2, [], velocity, first_row[0, :8], micros=0.01)
    after = velocity_y[0]
    velocity_y = swap(velocity_y, y_pairs)

    wide_own, wide_halo = (size_x, rows, size_z), (2 * WIDE, rows, size_z)

    def exchange(corr, rest, messages, corners, early_planes):
        tiles = WIDE + 2 + (3 * WIDE if corners else 0) + (WIDE - early_planes) * (size_y // 8)
        message = (tiles + (SPARE if corners else 0), 2 * WIDE, size_z)
        y_messages, early = swap(messages[:2], y_pairs), swap(messages[2:], x_pairs)
        *own, even, odd = kernel_call(
            functools.partial(extend_kernel, corners=corners, early_planes=early_planes),
            [wide_own, (2, rows, size_z), (2, size_x, size_z), message, message],
            [],
            rest,
            corr,
            *y_messages[::-1],
            velocity,
            *velocity_y,
            micros=0.01,
        )
        return (*own, *swap((even, odd), x_pairs)[::-1], *coefs, corr, *early[::-1])

    corr, rest, *messages = kernel_call(
        coarse_kernel,
        [block, block, y_message, y_message, x_early_first, x_early_first],
        [],
        first,
        inverse_rows,
        deflation,
        right_side,
        velocity,
        after,
        micros=1.4,
    )
    coefs = kernel_call(
        coefficients_kernel,
        [wide_own] * 5,
        [(3, size_x, rows, size_z)],
        velocity,
        *velocity_y,
        micros=0.01,
    )
    search, image, second_row, *halo_coefs = kernel_call(
        search_kernel,
        [block, block, row] + [wide_halo] * 4,
        [stage, (3, rows, size_z)] + smooth_scratch,
        *exchange(corr, rest, messages, True, EARLY_FIRST),
        deflation,
        right_side,
        micros=3.0,
    )
    second = share(second_row)
    corr, rest, middle, alpha, *messages = kernel_call(
        second_coarse_kernel,
        [block, block, block, (8, LANES), y_message, y_message, x_early, x_early],
        [],
        first,
        second,
        inverse_rows,
        deflation,
        right_side,
        image,
        velocity,
        micros=1.4,
    )
    smoothed, turned, third_row = kernel_call(
        smoothed_kernel,
        [block, block, row],
        [stage] + smooth_scratch,
        *exchange(corr, rest, messages, False, WIDE),
        *halo_coefs,
        middle,
        micros=2.5,
    )
    third = share(third_row)
    return tuple(
        kernel_call(last_kernel, [block, block], [], third, alpha, search, smoothed, middle, turned, micros=1.4)
    )


def solution(mesh):
    return jax.shard_map(
        local,
        mesh=mesh,
        in_specs=(
            P("gx", "gy", None),
            P(None, "gx", "gy", None),
            P(None, "gx", "gy", None),
            P(("gx", "gy"), None),
        ),
        out_specs=(P("gx", "gy", None), P("gx", "gy", None)),
        check_vma=False,
    )
```

```python
import functools

import jax
import jax.numpy as jnp
from jax import lax
from jax.experimental import pallas as pl
from jax.experimental.pallas import tpu as pltpu
from jax.sharding import PartitionSpec as P

DEPTH = 2
CHEB = 4
WIDE = 4
EARLY_FIRST = 1
SPARE = 3
LANES = 128
AXES = ("gx", "gy")
F32 = jnp.float32
HIGHEST = lax.Precision.HIGHEST

cheb_center = 1.0
cheb_radius = 0.9

ODD_X, ODD_Y, LOW_X, HIGH_X, LOW_Y, HIGH_Y, SLOT = range(7)

def pair_permutations(count_x, count_y):
    def number(i, j):
        return i * count_y + j

    even_x, odd_x, even_y, odd_y = [], [], [], []
    for i in range(count_x):
        for j in range(count_y):
            here = number(i, j)
            even_x.append((here, number(i ^ 1, j)))
            even_y.append((here, number(i, j ^ 1)))
            other = ((i - 1) ^ 1) + 1
            odd_x.append((here, number(other, j) if 0 <= other < count_x else number(i, j ^ 1)))
            other = ((j - 1) ^ 1) + 1
            odd_y.append((here, number(i, other) if 0 <= other < count_y else number(i ^ 1, j)))
    return (even_x, odd_x), (even_y, odd_y)


def place_flags(vectors_count):
    count_x, count_y = lax.axis_size("gx"), lax.axis_size("gy")
    at_x, at_y = lax.axis_index("gx"), lax.axis_index("gy")
    return (
        lax.rem(at_x, 2),
        lax.rem(at_y, 2),
        (at_x > 0).astype(jnp.int32),
        (at_x < count_x - 1).astype(jnp.int32),
        (at_y > 0).astype(jnp.int32),
        (at_y < count_y - 1).astype(jnp.int32),
        lax.rem(at_x * count_y + at_y, LANES // vectors_count),
    )


def call(vectors, body, outs, scratch, *args, micros, streamed=False):
    def kernel(*refs):
        body(place_flags(vectors), *refs)

    return pl.pallas_call(
        kernel,
        out_shape=[jax.ShapeDtypeStruct(kind, F32) if isinstance(kind, tuple) else kind for kind in outs],
        in_specs=[pl.BlockSpec(memory_space=pltpu.HBM if streamed else pltpu.VMEM)] * len(args),
        out_specs=[pl.BlockSpec(memory_space=pltpu.VMEM)] * len(outs),
        scratch_shapes=[pltpu.VMEM(kind, F32) if isinstance(kind, tuple) else kind for kind in scratch],
        compiler_params=pltpu.CompilerParams(vmem_limit_bytes=24 * 1024 * 1024),
        cost_estimate=pl.CostEstimate(flops=0, bytes_accessed=int(micros * 3.6e6), transcendentals=0),
    )(*args)


def shift_z(plane, ahead):
    width = plane.shape[1]
    lane = lax.broadcasted_iota(jnp.int32, (plane.shape[0], LANES), 1)
    edge = LANES - 1 if ahead else 0
    turned = [pltpu.roll(plane[:, i : i + LANES], LANES - 1 if ahead else 1, 1) for i in range(0, width, LANES)]
    beside = turned[1:] + [0.0] if ahead else [0.0] + turned[:-1]
    return jnp.concatenate([jnp.where(lane == edge, far, near) for near, far in zip(turned, beside)], axis=1)


def restrict(vectors, field, sums, flags, send, copies=()):
    count, size_x, size_y, size_z = vectors.shape
    stage = send[1]
    stage[...] = jnp.zeros_like(stage)

    def lanes_of(total):
        total = jnp.sum(total, axis=0, keepdims=True)
        return functools.reduce(jnp.add, [total[:, k : k + LANES] for k in range(0, size_z, LANES)])

    offset = pl.multiple_of(flags[SLOT] * count, count)
    for j in range(count):
        if copies and j % (count // len(copies)) == 0:
            copies[j // (count // len(copies))].wait()
        total = vectors[j, 0].astype(F32) * field[0]
        for x in range(1, size_x):
            total = total + vectors[j, x].astype(F32) * field[x]
        stage[pl.ds(offset + j, 1), :] = lanes_of(total)
    for k, total in enumerate(sums):
        stage[LANES + k : LANES + k + 1, :] = lanes_of(total)
    write_row(stage, send[0])


def write_row(stage, out):
    row = lax.dot_general(
        jnp.ones((8, LANES), F32), stage[...], (((1,), (1,)), ((), ())), precision=HIGHEST, preferred_element_type=F32
    )
    for k in range(out.shape[0]):
        out[k] = row[0:1]


def gathered(received, vectors):
    share = LANES // vectors.shape[0]
    return [
        functools.reduce(jnp.add, [received[k + i, :, :LANES] for i in range(share)])
        for k in range(0, received.shape[0], share)
    ]


def summed(received):
    return functools.reduce(jnp.add, [received[k, :, LANES:] for k in range(received.shape[0])])


def solve(coarse, inverse):
    total = inverse[:, :LANES] * coarse[0]
    for k in range(1, len(coarse)):
        total = total + inverse[:, k * LANES : (k + 1) * LANES] * coarse[k]
    return jnp.sum(total, axis=1, keepdims=True).astype(jnp.bfloat16).astype(F32)


def prolong(solved, vectors, corr):
    count, size_x, size_y, size_z = vectors.shape
    totals = [jnp.zeros((size_y, size_z), F32) for _ in range(size_x)]
    for j in range(count):
        weight = jnp.broadcast_to(solved[j : j + 1], (size_y, size_z))
        for x in range(size_x):
            totals[x] = totals[x] + vectors[j, x].astype(F32) * weight
    for x in range(size_x):
        corr[x] = totals[x]


def subtract_own(field, corr, velocity, out):
    size_x, size_y, size_z = corr.shape
    rows = lax.broadcasted_iota(jnp.int32, (size_y, size_z), 0)
    for x in range(size_x):
        v0, v1, v2 = velocity[0, x], velocity[1, x], velocity[2, x]
        here = corr[x]
        image = (6.0 + v0 + v1 + v2) * here
        if x + 1 < size_x:
            image = image - corr[x + 1]
        if x > 0:
            image = image - (1.0 + v0) * corr[x - 1]
        image = image - jnp.where(rows < size_y - 1, pltpu.roll(here, size_y - 1, 0), 0.0)
        image = image - (1.0 + v1) * jnp.where(rows > 0, pltpu.roll(here, 1, 0), 0.0)
        image = image - shift_z(here, True) - (1.0 + v2) * shift_z(here, False)
        out[x] = field[x] - image


def write_y_message(out, field, corr, high):
    size_x, size_y, _ = corr.shape
    start = size_y - WIDE if high else 0
    edge = size_y - 1 if high else 0
    for x in range(size_x):
        out[x] = field[x, start : start + WIDE, :]
        out[size_x + x // WIDE, x % WIDE : x % WIDE + 1, :] = corr[x, edge : edge + 1, :]
    last = size_x + size_x // WIDE
    out[last] = corr[0, start : start + WIDE, :]
    out[last + 1] = corr[size_x - 1, start : start + WIDE, :]


def by_parity(odd, write, even_out, odd_out):
    @pl.when(odd == 0)
    def _():
        write(even_out, True)
        write(odd_out, False)

    @pl.when(odd != 0)
    def _():
        write(even_out, False)
        write(odd_out, True)


def first_kernel(
    flags, field, vectors, velocity, inverse, out, held_field, held_vectors, held_velocity, held_inverse, stage, sems
):
    parts = sems.shape[0] - 3
    step = vectors.shape[0] // parts
    chunks = [pl.ds(part * step, step) for part in range(parts)]
    pairs = [(field, held_field)] + [(vectors.at[chunk], held_vectors.at[chunk]) for chunk in chunks]
    pairs += [(velocity, held_velocity), (inverse, held_inverse)]
    copies = [pltpu.make_async_copy(here, there, sems.at[k]) for k, (here, there) in enumerate(pairs)]
    for copy in copies:
        copy.start()
    copies[0].wait()
    rounded = [held_field[x].astype(jnp.bfloat16).astype(F32) for x in range(field.shape[0])]
    restrict(held_vectors, rounded, [], flags, (out, stage), copies[1 : 1 + parts])
    for copy in copies[1 + parts :]:
        copy.wait()


def by_side(odd, use, *pairs):
    evens, odds = [pair[0] for pair in pairs], [pair[1] for pair in pairs]

    @pl.when(odd == 0)
    def _():
        use(odds, evens)

    @pl.when(odd != 0)
    def _():
        use(evens, odds)


def velocity_y_kernel(flags, velocity, even_out, odd_out):
    _, size_x, size_y, _ = velocity.shape

    def write_y(out, high):
        start = size_y - WIDE if high else 0
        for d in range(3):
            for x in range(size_x):
                out[d, x] = velocity[d, x, start : start + WIDE, :]

    by_parity(flags[ODD_Y], write_y, even_out, odd_out)


def write_x_early(flags, planes, rest, corr, velocity, even_out, odd_out):
    size_x = rest.shape[0]

    def write(out, high):
        start = size_x - WIDE if high else 0
        out[0] = corr[size_x - 1 if high else 0]
        for k in range(planes):
            out[1 + k] = rest[start + k]
        if velocity is not None:
            for d in range(3):
                for k in range(WIDE):
                    out[1 + planes + d * WIDE + k] = velocity[d, start + k]

    by_parity(flags[ODD_X], write, even_out, odd_out)


def coefficients(x, v0, v1, v2, kept, outs):
    inverse, b0, b1, b2 = outs
    total = 6.0 + v0 + v1 + v2
    value = jnp.where(kept, 1.0 / total, 0.0)
    inverse[x] = value
    b0[x] = value * (1.0 + v0)
    b1[x] = value * (1.0 + v1)
    b2[x] = value * (1.0 + v2)
    return total


def rows_in_grid(flags, shape):
    row = lax.broadcasted_iota(jnp.int32, shape, 0)
    first_row = jnp.where(flags[LOW_Y] != 0, 0, WIDE)
    end_row = jnp.where(flags[HIGH_Y] != 0, shape[0], shape[0] - WIDE)
    return (row >= first_row) & (row < end_row)


def coefficients_kernel(flags, velocity, even_in, odd_in, diagonal, inverse, b0, b1, b2, wide):
    _, size_x, size_y, size_z = velocity.shape
    rows = size_y + 2 * WIDE

    def place(low, high):
        for d in range(3):
            for x in range(size_x):
                wide[d, x, 0:WIDE, :] = low[d, x]
                wide[d, x, WIDE : WIDE + size_y, :] = velocity[d, x]
                wide[d, x, WIDE + size_y : rows, :] = high[d, x]

    @pl.when(flags[ODD_Y] == 0)
    def _():
        place(odd_in, even_in)

    @pl.when(flags[ODD_Y] != 0)
    def _():
        place(even_in, odd_in)

    kept = rows_in_grid(flags, (rows, size_z))
    for x in range(size_x):
        diagonal[x] = coefficients(x, wide[0, x], wide[1, x], wide[2, x], kept, (inverse, b0, b1, b2))


def halo_coefficients(flags, early, late, outs, wide):
    size_y, size_z = early[0].shape[1:]
    rows = size_y + 2 * WIDE
    kept = rows_in_grid(flags, (rows, size_z))

    def side(start, message, corners, present):
        for k in range(WIDE):
            for d in range(3):
                tile = WIDE + 2 + d * WIDE + k
                wide[d, 0:WIDE, :] = corners[tile, 0:WIDE, :]
                wide[d, WIDE : WIDE + size_y, :] = message[1 + EARLY_FIRST + d * WIDE + k]
                wide[d, WIDE + size_y : rows, :] = corners[tile, WIDE : 2 * WIDE, :]
            coefficients(start + k, wide[0], wide[1], wide[2], kept & (flags[present] != 0), outs)

    by_side(flags[ODD_X], lambda low, high: (side(0, *low, LOW_X), side(WIDE, *high, HIGH_X)), early, late)


class Region:
    def __init__(self, own, halo):
        self.own, self.halo = own, halo

    def __getitem__(self, index):
        x, tile = index if isinstance(index, tuple) else (index, slice(None))
        size_x = self.own.shape[0]
        if x < WIDE:
            return self.halo[x, tile]
        return self.own[x - WIDE, tile] if x < WIDE + size_x else self.halo[x - size_x, tile]


def coarse_kernel(
    flags, received, inverse, vectors, field, velocity, after, corr, rest, even_out, odd_out, even_x, odd_x
):
    prolong(solve(gathered(received, vectors), inverse), vectors, corr)
    subtract_own(field, corr, velocity, rest)
    by_parity(flags[ODD_Y], lambda out, high: write_y_message(out, rest, corr, high), even_out, odd_out)
    write_x_early(flags, EARLY_FIRST, rest, corr, velocity, even_x, odd_x)


def second_coarse_kernel(
    flags, received, second, inverse, vectors, field, image, velocity, corr, rest, middle, alpha, even_out, odd_out,
    even_x, odd_x
):
    products = summed(second)
    step = jnp.broadcast_to(products[:, 0:1] / products[:, 1:2], alpha.shape)
    alpha[...] = step
    step = step[0:1, 0:1]
    for x in range(field.shape[0]):
        middle[x] = field[x] - step * image[x]
    pairs = zip(gathered(received, vectors), gathered(second, vectors))
    prolong(solve([coarse - step * of_image for coarse, of_image in pairs], inverse), vectors, corr)
    subtract_own(middle, corr, velocity, rest)
    by_parity(flags[ODD_Y], lambda out, high: write_y_message(out, rest, corr, high), even_out, odd_out)
    write_x_early(flags, WIDE, rest, corr, None, even_x, odd_x)


def extend_kernel(
    flags, rest, corr, odd_in, even_in, velocity, even_vel, odd_vel, wide, sides, past, even_out, odd_out, corners, early_planes
):
    size_x, size_y, size_z = rest.shape
    rows = size_y + 2 * WIDE
    end = WIDE + size_y

    def place(low, high, high_vel):
        has_low, has_high = flags[LOW_Y] != 0, flags[HIGH_Y] != 0
        for x in range(size_x):
            at, line = size_x + x // WIDE, slice(x % WIDE, x % WIDE + 1)
            past_low = jnp.where(has_low, low[at, line, :], 0.0)
            past_high = jnp.where(has_high, high[at, line, :], 0.0)
            past[0, x : x + 1, :] = past_low
            past[1, x : x + 1, :] = past_high
            wide[x, 0 : WIDE - 1, :] = low[x, 0 : WIDE - 1, :]
            wide[x, WIDE - 1 : WIDE, :] = low[x, WIDE - 1 : WIDE, :] + corr[x, 0:1, :]
            wide[x, WIDE:end, :] = rest[x]
            wide[x, WIDE : WIDE + 1, :] = rest[x, 0:1, :] + (1.0 + velocity[1, x, 0:1, :]) * past_low
            wide[x, end - 1 : end, :] = rest[x, size_y - 1 : size_y, :] + past_high
            weight = 1.0 + high_vel[1, x, 0:1, :]
            wide[x, end : end + 1, :] = high[x, 0:1, :] + weight * corr[x, size_y - 1 : size_y, :]
            wide[x, end + 1 : rows, :] = high[x, 1:WIDE, :]
        last = size_x + size_x // WIDE
        for side, x in enumerate((0, size_x - 1)):
            sides[side, 0:WIDE, :] = low[last + side]
            sides[side, WIDE:end, :] = corr[x]
            sides[side, end:rows, :] = high[last + side]

    @pl.when(flags[ODD_Y] == 0)
    def _():
        place(odd_in, even_in, even_vel)

    @pl.when(flags[ODD_Y] != 0)
    def _():
        place(even_in, odd_in, odd_vel)

    def write(out, high):
        start = size_x - WIDE if high else 0
        for k in range(WIDE):
            out[k, 0:WIDE, :] = wide[start + k, 0:WIDE, :]
            out[k, WIDE : 2 * WIDE, :] = wide[start + k, end:rows, :]
        side = 1 if high else 0
        out[WIDE, 0:WIDE, :] = sides[side, 0:WIDE, :]
        out[WIDE, WIDE : 2 * WIDE, :] = sides[side, end:rows, :]
        out[WIDE + 1, 0:WIDE, :] = past[0, start : start + WIDE, :]
        out[WIDE + 1, WIDE : 2 * WIDE, :] = past[1, start : start + WIDE, :]

        tile = WIDE + 2 + (3 * WIDE if corners else 0)
        for k in range(early_planes, WIDE):
            for row in range(0, size_y, 8):
                out[tile] = rest[start + k, row : row + 8, :]
                tile += 1

    by_parity(flags[ODD_X], write, even_out, odd_out)
    if not corners:
        return

    def write_corners(low, high):
        def write(out, upper):
            start = size_x - WIDE if upper else 0
            for d in range(3):
                for k in range(WIDE):
                    tile = WIDE + 2 + d * WIDE + k
                    out[tile, 0:WIDE, :] = low[0][d, start + k]
                    out[tile, WIDE : 2 * WIDE, :] = high[0][d, start + k]

        by_parity(flags[ODD_X], write, even_out, odd_out)

    by_side(flags[ODD_Y], write_corners, (even_vel, odd_vel))


def beside_terms(before, here, after, x, tile, coefs):
    inverse, b0, b1, b2 = coefs
    rows = here.shape[0]
    ahead = pltpu.roll(here, rows - 1, 0) + shift_z(here, True)
    if after is not None:
        ahead = ahead + after
    total = inverse[x, tile] * ahead + b1[x, tile] * pltpu.roll(here, 1, 0) + b2[x, tile] * shift_z(here, False)
    if before is not None:
        total = total + b0[x, tile] * before
    return total


def chebyshev(planes, tile, inside, source, left, update, coefs, wanted):
    sigma = cheb_center / cheb_radius
    rho = 1.0 / sigma
    first, last = planes[0], planes[-1]
    for x in planes:
        update[0, x, tile] = jnp.where(inside, source(x), 0.0)
    estimate = {}
    for sweep in range(1, CHEB):
        rest = CHEB - 1 - sweep
        low, high = max(first, wanted[0] - rest), min(last, wanted[-1] + rest)
        rho_next = 1.0 / (2.0 * sigma - rho)
        for x in range(low, high + 1):
            here = update[sweep - 1, x, tile]
            before = update[sweep - 1, x - 1, tile] if x > first else None
            after = update[sweep - 1, x + 1, tile] if x < last else None
            remainder = beside_terms(before, here, after, x, tile, coefs)
            if sweep > 1:
                remainder = remainder + (left[x, tile] - here)
            if rest:
                left[x, tile] = remainder
            value = rho_next * rho * here + (2.0 * rho_next / cheb_radius) * jnp.where(inside, remainder, 0.0)
            if rest:
                update[sweep, x, tile] = value
            else:
                for k in range(CHEB - 1):
                    value = value + update[k, x, tile]
                estimate[x] = value
        rho = rho_next
    return estimate


def smooth(
    flags, early_planes, wide, sides, past, early, late, diagonal, coefs, corr, field_out, image_out, scratch
):
    source, left, update, whole = scratch
    inverse, b0, b1, _ = coefs
    size_x, size_y, size_z = corr.shape
    rows = size_y + 2 * WIDE
    span = size_x + 2 * WIDE
    row = lax.broadcasted_iota(jnp.int32, (rows, size_z), 0)
    has_low_x, has_high_x = flags[LOW_X] != 0, flags[HIGH_X] != 0
    has_low_y, has_high_y = flags[LOW_Y] != 0, flags[HIGH_Y] != 0
    lowest, highest = slice(0, 8), slice(rows - 8, rows)
    tile_row = lax.broadcasted_iota(jnp.int32, (8, size_z), 0)
    end = WIDE + size_y

    def put(out, x, middle, ends):
        out[x, 0:WIDE, :] = ends[0:WIDE, :]
        for row_ in range(0, size_y, 8):
            out[x, WIDE + row_ : WIDE + row_ + 8, :] = middle(row_)
        out[x, end:rows, :] = ends[WIDE : 2 * WIDE, :]

    def halo(side, first, edge, present):
        message, ends = side
        for k in range(WIDE):
            x = first + k
            if k < early_planes:
                middle = lambda row_: message[1 + k, row_ : row_ + 8, :]
            else:
                tile = ends.shape[0] - SPARE - (WIDE - k) * (size_y // 8)
                middle = lambda row_: ends[tile + row_ // 8]
            put(source, x, middle, ends.at[k])
            source[x] = inverse[x] * source[x]
            for row_, weight, line in ((WIDE, b1, k), (end - 1, inverse, WIDE + k)):
                at = slice(row_, row_ + 1)
                source[x, at] = source[x, at] + weight[x, at] * ends[WIDE + 1, line : line + 1, :]
        put(whole, edge, lambda row_: message[0, row_ : row_ + 8, :], ends.at[WIDE])
        whole[edge] = jnp.where(present, whole[edge], 0.0)

    def halos(low, high):
        halo(low, 0, 0, has_low_x)
        halo(high, WIDE + size_x, size_x + 1, has_high_x)

    by_side(flags[ODD_X], halos, early, late)

    for k in range(size_x):
        source[WIDE + k] = inverse[WIDE + k] * wide[k]

    low_in, high_in = WIDE, WIDE + size_x - 1
    source[low_in - 1] = source[low_in - 1] + inverse[low_in - 1] * sides[0]
    source[low_in] = source[low_in] + b0[low_in] * whole[0]
    source[high_in] = source[high_in] + inverse[high_in] * whole[size_x + 1]
    source[high_in + 1] = source[high_in + 1] + b0[high_in + 1] * sides[1]

    def run(planes, tile, inside, wanted):
        return chebyshev(
            planes,
            tile,
            inside,
            lambda x: source[x, tile],
            left,
            update,
            coefs,
            wanted,
        )

    everything = slice(0, rows)
    box_rows = (row >= WIDE - DEPTH) & (row < WIDE + size_y + DEPTH)
    box_planes = range(WIDE - DEPTH, WIDE + size_x + DEPTH)
    own_planes = range(WIDE, WIDE + size_x)
    inner = (row >= WIDE) & (row < WIDE + size_y)

    beside = run(range(0, WIDE + DEPTH), everything, box_rows, (WIDE - 1,))[WIDE - 1]
    whole[0] = jnp.where(has_low_x & inner, whole[0] + beside, 0.0)
    x = WIDE + size_x
    beside = run(range(span - WIDE - DEPTH, span), everything, box_rows, (x,))[x]
    whole[size_x + 1] = jnp.where(has_high_x & inner, whole[size_x + 1] + beside, 0.0)

    own = run(box_planes, everything, box_rows, tuple(own_planes))
    zeros = jnp.zeros((rows - size_y, size_z), F32)
    for k in range(size_x):
        placed = pltpu.roll(jnp.concatenate([corr[k], zeros], axis=0), WIDE, 0)
        whole[k + 1] = jnp.where(inner, placed + own[WIDE + k], 0.0)

    beside = run(box_planes, lowest, tile_row < WIDE + DEPTH, tuple(own_planes))
    for k in range(size_x):
        line = past[0, k : k + 1, :] + beside[WIDE + k]
        here = has_low_y & (tile_row == WIDE - 1)
        whole[k + 1, lowest] = jnp.where(here, line, whole[k + 1, lowest])
    beside = run(box_planes, highest, tile_row >= 8 - WIDE - DEPTH, tuple(own_planes))
    for k in range(size_x):
        line = past[1, k : k + 1, :] + beside[WIDE + k]
        here = has_high_y & (tile_row == 8 - WIDE)
        whole[k + 1, highest] = jnp.where(here, line, whole[k + 1, highest])

    for k in range(size_x):
        x = WIDE + k
        terms = beside_terms(whole[k], whole[k + 1], whole[k + 2], x, everything, coefs)
        image = diagonal[k] * (whole[k + 1] - terms)
        image_out[k] = pltpu.roll(image, rows - WIDE, 0)[0:size_y]
        field_out[k] = pltpu.roll(whole[k + 1], rows - WIDE, 0)[0:size_y]


def dot_planes(left, right):
    total = left[0] * right[0]
    for x in range(1, left.shape[0]):
        total = total + left[x] * right[x]
    return total


def search_kernel(
    flags, wide, sides, past, odd_late, even_late, diagonal, own0, own1, own2, own3, corr, odd_early, even_early, vectors,
    right_side, search, image, out, halo0, halo1, halo2, halo3, stage, wide_vel, *scratch
):
    halos = (halo0, halo1, halo2, halo3)
    early, late = (even_early, odd_early), (even_late, odd_late)
    halo_coefficients(flags, early, late, halos, wide_vel)
    coefs = [Region(*pair) for pair in zip((own0, own1, own2, own3), halos)]
    smooth(flags, EARLY_FIRST, wide, sides, past, early, late, diagonal, coefs, corr, search, image, scratch)
    products = [dot_planes(right_side, right_side), dot_planes(right_side, image)]
    restrict(vectors, image, products, flags, (out, stage))


def smoothed_kernel(
    flags, wide, sides, past, odd_late, even_late, diagonal, own0, own1, own2, own3, corr, odd_early, even_early, halo0,
    halo1, halo2, halo3, middle, smoothed, turned, out, stage, *scratch
):
    early, late = (even_early, odd_early), (even_late, odd_late)
    coefs = [Region(*pair) for pair in zip((own0, own1, own2, own3), (halo0, halo1, halo2, halo3))]
    smooth(flags, WIDE, wide, sides, past, early, late, diagonal, coefs, corr, smoothed, turned, scratch)
    stage[...] = jnp.zeros_like(stage)
    for k, total in enumerate((dot_planes(turned, middle), dot_planes(turned, turned))):
        total = jnp.sum(total, axis=0, keepdims=True)
        parts = [total[:, i : i + LANES] for i in range(0, total.shape[1], LANES)]
        stage[LANES + k : LANES + k + 1, :] = functools.reduce(jnp.add, parts)
    write_row(stage, out)


def last_kernel(flags, received, alpha, search, smoothed, middle, turned, solution_field, residual):
    sums = summed(received)
    omega = sums[:, 0:1] / sums[:, 1:2]
    step = alpha[0:1, 0:1]
    for x in range(search.shape[0]):
        solution_field[x] = step * search[x] + omega * smoothed[x]
        residual[x] = middle[x] - omega * turned[x]


def local(right_side, velocity, deflation, inverse_rows):
    size_x, size_y, size_z = right_side.shape
    vectors_count = deflation.shape[0]
    count_x, count_y = lax.axis_size("gx"), lax.axis_size("gy")
    count = count_x * count_y
    at_x, at_y = lax.axis_index("gx"), lax.axis_index("gy")
    kernel_call = functools.partial(call, vectors_count)
    x_pairs, y_pairs = pair_permutations(count_x, count_y)

    def swap(messages, pairs):
        odd = lax.ppermute(messages[1], AXES, pairs[1])
        return [lax.ppermute(messages[0], AXES, pairs[0]), odd]

    def share(row):
        return lax.all_to_all(row, AXES, 0, 0)

    rows = size_y + 2 * WIDE
    span = size_x + 2 * WIDE
    block = (size_x, size_y, size_z)
    row = pltpu.VMEM((count, 1, 2 * LANES), F32)
    stage = (2 * LANES, LANES)
    y_message = (size_x + size_x // WIDE + 2, WIDE, size_z)
    region = (span, rows, size_z)
    smooth_scratch = [region, region, (CHEB - 1,) + region, (size_x + 2, rows, size_z)]

    chunks = 4
    arguments = (right_side, deflation, velocity, inverse_rows)
    first_row, right_side, deflation, velocity, inverse_rows = kernel_call(
        first_kernel,
        [row] + [pltpu.VMEM(argument.shape, argument.dtype) for argument in arguments],
        [stage, pltpu.SemaphoreType.DMA((chunks + 3,))],
        *[pltpu.with_memory_space_constraint(argument, pltpu.HBM) for argument in arguments],
        micros=2.0,
        streamed=True,
    )
    first = share(first_row)
    faces_y = (3, size_x, WIDE, size_z)
    x_early = (WIDE + 1, size_y, size_z)
    x_early_first = (1 + EARLY_FIRST + 3 * WIDE, size_y, size_z)
    velocity_y = kernel_call(velocity_y_kernel, [faces_y] * 2, [], velocity, micros=0.01)
    after = velocity_y[0]
    velocity_y = swap(velocity_y, y_pairs)

    wide_own, wide_halo = (size_x, rows, size_z), (2 * WIDE, rows, size_z)

    def exchange(corr, rest, messages, corners, early_planes):
        tiles = WIDE + 2 + (3 * WIDE if corners else 0) + (WIDE - early_planes) * (size_y // 8)
        message = (tiles + (SPARE if corners else 0), 2 * WIDE, size_z)
        y_messages, early = swap(messages[:2], y_pairs), swap(messages[2:], x_pairs)
        *own, even, odd = kernel_call(
            functools.partial(extend_kernel, corners=corners, early_planes=early_planes),
            [wide_own, (2, rows, size_z), (2, size_x, size_z), message, message],
            [],
            rest,
            corr,
            *y_messages[::-1],
            velocity,
            *velocity_y,
            micros=0.01,
        )
        return (*own, *swap((even, odd), x_pairs)[::-1], *coefs, corr, *early[::-1])

    corr, rest, *messages = kernel_call(
        coarse_kernel,
        [block, block, y_message, y_message, x_early_first, x_early_first],
        [],
        first,
        inverse_rows,
        deflation,
        right_side,
        velocity,
        after,
        micros=1.4,
    )
    coefs = kernel_call(
        coefficients_kernel,
        [wide_own] * 5,
        [(3, size_x, rows, size_z)],
        velocity,
        *velocity_y,
        micros=0.01,
    )
    search, image, second_row, *halo_coefs = kernel_call(
        search_kernel,
        [block, block, row] + [wide_halo] * 4,
        [stage, (3, rows, size_z)] + smooth_scratch,
        *exchange(corr, rest, messages, True, EARLY_FIRST),
        deflation,
        right_side,
        micros=3.0,
    )
    second = share(second_row)
    corr, rest, middle, alpha, *messages = kernel_call(
        second_coarse_kernel,
        [block, block, block, (8, LANES), y_message, y_message, x_early, x_early],
        [],
        first,
        second,
        inverse_rows,
        deflation,
        right_side,
        image,
        velocity,
        micros=1.4,
    )
    smoothed, turned, third_row = kernel_call(
        smoothed_kernel,
        [block, block, row],
        [stage] + smooth_scratch,
        *exchange(corr, rest, messages, False, WIDE),
        *halo_coefs,
        middle,
        micros=2.5,
    )
    third = share(third_row)
    return tuple(
        kernel_call(last_kernel, [block, block], [], third, alpha, search, smoothed, middle, turned, micros=1.4)
    )


def solution(mesh):
    return jax.shard_map(
        local,
        mesh=mesh,
        in_specs=(
            P("gx", "gy", None),
            P(None, "gx", "gy", None),
            P(None, "gx", "gy", None),
            P(("gx", "gy"), None),
        ),
        out_specs=(P("gx", "gy", None), P("gx", "gy", None)),
        check_vma=False,
    )
```

```python
import functools

import jax
import jax.numpy as jnp
from jax import lax
from jax.experimental import pallas as pl
from jax.experimental.pallas import tpu as pltpu
from jax.sharding import PartitionSpec as P

DEPTH = 2
CHEB = 4
WIDE = 4
EARLY_FIRST = 0
LANES = 128
AXES = ("gx", "gy")
F32 = jnp.float32
HIGHEST = lax.Precision.HIGHEST

cheb_center = 1.0
cheb_radius = 0.9

ODD_X, ODD_Y, LOW_X, HIGH_X, LOW_Y, HIGH_Y, SLOT = range(7)

def pair_permutations(count_x, count_y):
    def number(i, j):
        return i * count_y + j

    even_x, odd_x, even_y, odd_y = [], [], [], []
    for i in range(count_x):
        for j in range(count_y):
            here = number(i, j)
            even_x.append((here, number(i ^ 1, j)))
            even_y.append((here, number(i, j ^ 1)))
            other = ((i - 1) ^ 1) + 1
            odd_x.append((here, number(other, j) if 0 <= other < count_x else number(i, j ^ 1)))
            other = ((j - 1) ^ 1) + 1
            odd_y.append((here, number(i, other) if 0 <= other < count_y else number(i ^ 1, j)))
    return (even_x, odd_x), (even_y, odd_y)


def place_flags(vectors_count):
    count_x, count_y = lax.axis_size("gx"), lax.axis_size("gy")
    at_x, at_y = lax.axis_index("gx"), lax.axis_index("gy")
    return (
        lax.rem(at_x, 2),
        lax.rem(at_y, 2),
        (at_x > 0).astype(jnp.int32),
        (at_x < count_x - 1).astype(jnp.int32),
        (at_y > 0).astype(jnp.int32),
        (at_y < count_y - 1).astype(jnp.int32),
        lax.rem(at_x * count_y + at_y, LANES // vectors_count),
    )


def call(vectors, body, outs, scratch, *args, micros, streamed=False):
    def kernel(*refs):
        body(place_flags(vectors), *refs)

    return pl.pallas_call(
        kernel,
        out_shape=[jax.ShapeDtypeStruct(kind, F32) if isinstance(kind, tuple) else kind for kind in outs],
        in_specs=[pl.BlockSpec(memory_space=pltpu.HBM if streamed else pltpu.VMEM)] * len(args),
        out_specs=[pl.BlockSpec(memory_space=pltpu.VMEM)] * len(outs),
        scratch_shapes=[pltpu.VMEM(kind, F32) if isinstance(kind, tuple) else kind for kind in scratch],
        compiler_params=pltpu.CompilerParams(vmem_limit_bytes=24 * 1024 * 1024),
        cost_estimate=pl.CostEstimate(flops=0, bytes_accessed=int(micros * 3.6e6), transcendentals=0),
    )(*args)


def shift_z(plane, ahead):
    width = plane.shape[1]
    lane = lax.broadcasted_iota(jnp.int32, (plane.shape[0], LANES), 1)
    edge = LANES - 1 if ahead else 0
    turned = [pltpu.roll(plane[:, i : i + LANES], LANES - 1 if ahead else 1, 1) for i in range(0, width, LANES)]
    beside = turned[1:] + [0.0] if ahead else [0.0] + turned[:-1]
    return jnp.concatenate([jnp.where(lane == edge, far, near) for near, far in zip(turned, beside)], axis=1)


def restrict(vectors, field, sums, flags, send, copies=()):
    count, size_x, size_y, size_z = vectors.shape
    stage = send[1]
    stage[...] = jnp.zeros_like(stage)

    def lanes_of(total):
        total = jnp.sum(total, axis=0, keepdims=True)
        return functools.reduce(jnp.add, [total[:, k : k + LANES] for k in range(0, size_z, LANES)])

    offset = pl.multiple_of(flags[SLOT] * count, count)
    for j in range(count):
        if copies and j % (count // len(copies)) == 0:
            copies[j // (count // len(copies))].wait()
        total = vectors[j, 0].astype(F32) * field[0]
        for x in range(1, size_x):
            total = total + vectors[j, x].astype(F32) * field[x]
        stage[pl.ds(offset + j, 1), :] = lanes_of(total)
    for k, total in enumerate(sums):
        stage[LANES + k : LANES + k + 1, :] = lanes_of(total)
    write_row(stage, send[0])


def write_row(stage, out):
    row = lax.dot_general(
        jnp.ones((8, LANES), F32), stage[...], (((1,), (1,)), ((), ())), precision=HIGHEST, preferred_element_type=F32
    )
    for k in range(out.shape[0]):
        out[k] = row[0:1]


def gathered(received, vectors):
    share = LANES // vectors.shape[0]
    return [
        functools.reduce(jnp.add, [received[k + i, :, :LANES] for i in range(share)])
        for k in range(0, received.shape[0], share)
    ]


def summed(received):
    return functools.reduce(jnp.add, [received[k, :, LANES:] for k in range(received.shape[0])])


def solve(coarse, inverse):
    total = inverse[:, :LANES] * coarse[0]
    for k in range(1, len(coarse)):
        total = total + inverse[:, k * LANES : (k + 1) * LANES] * coarse[k]
    return jnp.sum(total, axis=1, keepdims=True).astype(jnp.bfloat16).astype(F32)


def prolong(solved, vectors, corr):
    count, size_x, size_y, size_z = vectors.shape
    totals = [jnp.zeros((size_y, size_z), F32) for _ in range(size_x)]
    for j in range(count):
        weight = jnp.broadcast_to(solved[j : j + 1], (size_y, size_z))
        for x in range(size_x):
            totals[x] = totals[x] + vectors[j, x].astype(F32) * weight
    for x in range(size_x):
        corr[x] = totals[x]


def subtract_own(field, corr, velocity, out):
    size_x, size_y, size_z = corr.shape
    rows = lax.broadcasted_iota(jnp.int32, (size_y, size_z), 0)
    for x in range(size_x):
        v0, v1, v2 = velocity[0, x], velocity[1, x], velocity[2, x]
        here = corr[x]
        image = (6.0 + v0 + v1 + v2) * here
        if x + 1 < size_x:
            image = image - corr[x + 1]
        if x > 0:
            image = image - (1.0 + v0) * corr[x - 1]
        image = image - jnp.where(rows < size_y - 1, pltpu.roll(here, size_y - 1, 0), 0.0)
        image = image - (1.0 + v1) * jnp.where(rows > 0, pltpu.roll(here, 1, 0), 0.0)
        image = image - shift_z(here, True) - (1.0 + v2) * shift_z(here, False)
        out[x] = field[x] - image


def write_y_message(out, field, corr, high):
    size_x, size_y, _ = corr.shape
    start = size_y - WIDE if high else 0
    edge = size_y - 1 if high else 0
    for x in range(size_x):
        out[x] = field[x, start : start + WIDE, :]
        out[size_x + x // WIDE, x % WIDE : x % WIDE + 1, :] = corr[x, edge : edge + 1, :]
    last = size_x + size_x // WIDE
    out[last] = corr[0, start : start + WIDE, :]
    out[last + 1] = corr[size_x - 1, start : start + WIDE, :]


def by_parity(odd, write, even_out, odd_out):
    @pl.when(odd == 0)
    def _():
        write(even_out, True)
        write(odd_out, False)

    @pl.when(odd != 0)
    def _():
        write(even_out, False)
        write(odd_out, True)


def first_kernel(
    flags, field, vectors, velocity, inverse, out, held_field, held_vectors, held_velocity, held_inverse, stage, sems
):
    parts = sems.shape[0] - 3
    step = vectors.shape[0] // parts
    chunks = [pl.ds(part * step, step) for part in range(parts)]
    pairs = [(field, held_field)] + [(vectors.at[chunk], held_vectors.at[chunk]) for chunk in chunks]
    pairs += [(velocity, held_velocity), (inverse, held_inverse)]
    copies = [pltpu.make_async_copy(here, there, sems.at[k]) for k, (here, there) in enumerate(pairs)]
    for copy in copies:
        copy.start()
    copies[0].wait()
    rounded = [held_field[x].astype(jnp.bfloat16).astype(F32) for x in range(field.shape[0])]
    restrict(held_vectors, rounded, [], flags, (out, stage), copies[1 : 1 + parts])
    for copy in copies[1 + parts :]:
        copy.wait()


def by_side(odd, use, *pairs):
    evens, odds = [pair[0] for pair in pairs], [pair[1] for pair in pairs]

    @pl.when(odd == 0)
    def _():
        use(odds, evens)

    @pl.when(odd != 0)
    def _():
        use(evens, odds)


def velocity_y_kernel(flags, velocity, even_out, odd_out):
    _, size_x, size_y, _ = velocity.shape

    def write_y(out, high):
        start = size_y - WIDE if high else 0
        for d in range(3):
            for x in range(size_x):
                out[d, x] = velocity[d, x, start : start + WIDE, :]

    by_parity(flags[ODD_Y], write_y, even_out, odd_out)


def write_x_early(flags, planes, rest, corr, velocity, even_out, odd_out):
    size_x = rest.shape[0]

    def write(out, high):
        start = size_x - WIDE if high else 0
        out[0] = corr[size_x - 1 if high else 0]
        for k in range(planes):
            out[1 + k] = rest[start + k]
        if velocity is not None:
            for d in range(3):
                for k in range(WIDE):
                    out[1 + planes + d * WIDE + k] = velocity[d, start + k]

    by_parity(flags[ODD_X], write, even_out, odd_out)


def coefficients(x, v0, v1, v2, kept, outs):
    inverse, b0, b1, b2 = outs
    total = 6.0 + v0 + v1 + v2
    value = jnp.where(kept, 1.0 / total, 0.0)
    inverse[x] = value
    b0[x] = value * (1.0 + v0)
    b1[x] = value * (1.0 + v1)
    b2[x] = value * (1.0 + v2)
    return total


def rows_in_grid(flags, shape):
    row = lax.broadcasted_iota(jnp.int32, shape, 0)
    first_row = jnp.where(flags[LOW_Y] != 0, 0, WIDE)
    end_row = jnp.where(flags[HIGH_Y] != 0, shape[0], shape[0] - WIDE)
    return (row >= first_row) & (row < end_row)


def coefficients_kernel(flags, velocity, even_in, odd_in, diagonal, inverse, b0, b1, b2, wide):
    _, size_x, size_y, size_z = velocity.shape
    rows = size_y + 2 * WIDE

    def place(low, high):
        for d in range(3):
            for x in range(size_x):
                wide[d, x, 0:WIDE, :] = low[d, x]
                wide[d, x, WIDE : WIDE + size_y, :] = velocity[d, x]
                wide[d, x, WIDE + size_y : rows, :] = high[d, x]

    @pl.when(flags[ODD_Y] == 0)
    def _():
        place(odd_in, even_in)

    @pl.when(flags[ODD_Y] != 0)
    def _():
        place(even_in, odd_in)

    kept = rows_in_grid(flags, (rows, size_z))
    for x in range(size_x):
        diagonal[x] = coefficients(x, wide[0, x], wide[1, x], wide[2, x], kept, (inverse, b0, b1, b2))


def halo_coefficients(flags, early, late, outs, wide):
    size_y, size_z = early[0].shape[1:]
    rows = size_y + 2 * WIDE
    kept = rows_in_grid(flags, (rows, size_z))

    def side(start, message, corners, present):
        for k in range(WIDE):
            for d in range(3):
                tile = WIDE + 2 + d * WIDE + k
                wide[d, 0:WIDE, :] = corners[tile, 0:WIDE, :]
                wide[d, WIDE : WIDE + size_y, :] = message[1 + EARLY_FIRST + d * WIDE + k]
                wide[d, WIDE + size_y : rows, :] = corners[tile, WIDE : 2 * WIDE, :]
            coefficients(start + k, wide[0], wide[1], wide[2], kept & (flags[present] != 0), outs)

    by_side(flags[ODD_X], lambda low, high: (side(0, *low, LOW_X), side(WIDE, *high, HIGH_X)), early, late)


class Region:
    def __init__(self, own, halo):
        self.own, self.halo = own, halo

    def __getitem__(self, index):
        x, tile = index if isinstance(index, tuple) else (index, slice(None))
        size_x = self.own.shape[0]
        if x < WIDE:
            return self.halo[x, tile]
        return self.own[x - WIDE, tile] if x < WIDE + size_x else self.halo[x - size_x, tile]


def coarse_kernel(
    flags, received, inverse, vectors, field, velocity, after, corr, rest, even_out, odd_out, even_x, odd_x
):
    prolong(solve(gathered(received, vectors), inverse), vectors, corr)
    subtract_own(field, corr, velocity, rest)
    by_parity(flags[ODD_Y], lambda out, high: write_y_message(out, rest, corr, high), even_out, odd_out)
    write_x_early(flags, EARLY_FIRST, rest, corr, velocity, even_x, odd_x)


def second_coarse_kernel(
    flags, received, second, inverse, vectors, field, image, velocity, corr, rest, middle, alpha, even_out, odd_out,
    even_x, odd_x
):
    products = summed(second)
    step = jnp.broadcast_to(products[:, 0:1] / products[:, 1:2], alpha.shape)
    alpha[...] = step
    step = step[0:1, 0:1]
    for x in range(field.shape[0]):
        middle[x] = field[x] - step * image[x]
    pairs = zip(gathered(received, vectors), gathered(second, vectors))
    prolong(solve([coarse - step * of_image for coarse, of_image in pairs], inverse), vectors, corr)
    subtract_own(middle, corr, velocity, rest)
    by_parity(flags[ODD_Y], lambda out, high: write_y_message(out, rest, corr, high), even_out, odd_out)
    write_x_early(flags, WIDE, rest, corr, None, even_x, odd_x)


def extend_kernel(
    flags, rest, corr, odd_in, even_in, velocity, even_vel, odd_vel, wide, sides, past, even_out, odd_out, corners, early_planes
):
    size_x, size_y, size_z = rest.shape
    rows = size_y + 2 * WIDE
    end = WIDE + size_y

    def place(low, high, high_vel):
        has_low, has_high = flags[LOW_Y] != 0, flags[HIGH_Y] != 0
        for x in range(size_x):
            at, line = size_x + x // WIDE, slice(x % WIDE, x % WIDE + 1)
            past_low = jnp.where(has_low, low[at, line, :], 0.0)
            past_high = jnp.where(has_high, high[at, line, :], 0.0)
            past[0, x : x + 1, :] = past_low
            past[1, x : x + 1, :] = past_high
            wide[x, 0 : WIDE - 1, :] = low[x, 0 : WIDE - 1, :]
            wide[x, WIDE - 1 : WIDE, :] = low[x, WIDE - 1 : WIDE, :] + corr[x, 0:1, :]
            wide[x, WIDE:end, :] = rest[x]
            wide[x, WIDE : WIDE + 1, :] = rest[x, 0:1, :] + (1.0 + velocity[1, x, 0:1, :]) * past_low
            wide[x, end - 1 : end, :] = rest[x, size_y - 1 : size_y, :] + past_high
            weight = 1.0 + high_vel[1, x, 0:1, :]
            wide[x, end : end + 1, :] = high[x, 0:1, :] + weight * corr[x, size_y - 1 : size_y, :]
            wide[x, end + 1 : rows, :] = high[x, 1:WIDE, :]
        last = size_x + size_x // WIDE
        for side, x in enumerate((0, size_x - 1)):
            sides[side, 0:WIDE, :] = low[last + side]
            sides[side, WIDE:end, :] = corr[x]
            sides[side, end:rows, :] = high[last + side]

    @pl.when(flags[ODD_Y] == 0)
    def _():
        place(odd_in, even_in, even_vel)

    @pl.when(flags[ODD_Y] != 0)
    def _():
        place(even_in, odd_in, odd_vel)

    def write(out, high):
        start = size_x - WIDE if high else 0
        for k in range(WIDE):
            out[k, 0:WIDE, :] = wide[start + k, 0:WIDE, :]
            out[k, WIDE : 2 * WIDE, :] = wide[start + k, end:rows, :]
        side = 1 if high else 0
        out[WIDE, 0:WIDE, :] = sides[side, 0:WIDE, :]
        out[WIDE, WIDE : 2 * WIDE, :] = sides[side, end:rows, :]
        out[WIDE + 1, 0:WIDE, :] = past[0, start : start + WIDE, :]
        out[WIDE + 1, WIDE : 2 * WIDE, :] = past[1, start : start + WIDE, :]

        tile = WIDE + 2 + (3 * WIDE if corners else 0)
        for k in range(early_planes, WIDE):
            for row in range(0, size_y, 8):
                out[tile] = rest[start + k, row : row + 8, :]
                tile += 1

    by_parity(flags[ODD_X], write, even_out, odd_out)
    if not corners:
        return

    def write_corners(low, high):
        def write(out, upper):
            start = size_x - WIDE if upper else 0
            for d in range(3):
                for k in range(WIDE):
                    tile = WIDE + 2 + d * WIDE + k
                    out[tile, 0:WIDE, :] = low[0][d, start + k]
                    out[tile, WIDE : 2 * WIDE, :] = high[0][d, start + k]

        by_parity(flags[ODD_X], write, even_out, odd_out)

    by_side(flags[ODD_Y], write_corners, (even_vel, odd_vel))


def beside_terms(before, here, after, x, tile, coefs):
    inverse, b0, b1, b2 = coefs
    rows = here.shape[0]
    ahead = pltpu.roll(here, rows - 1, 0) + shift_z(here, True)
    if after is not None:
        ahead = ahead + after
    total = inverse[x, tile] * ahead + b1[x, tile] * pltpu.roll(here, 1, 0) + b2[x, tile] * shift_z(here, False)
    if before is not None:
        total = total + b0[x, tile] * before
    return total


def chebyshev(planes, tile, inside, source, left, update, coefs, wanted):
    sigma = cheb_center / cheb_radius
    rho = 1.0 / sigma
    first, last = planes[0], planes[-1]
    for x in planes:
        update[0, x, tile] = jnp.where(inside, source(x), 0.0)
    estimate = {}
    for sweep in range(1, CHEB):
        rest = CHEB - 1 - sweep
        low, high = max(first, wanted[0] - rest), min(last, wanted[-1] + rest)
        rho_next = 1.0 / (2.0 * sigma - rho)
        for x in range(low, high + 1):
            here = update[sweep - 1, x, tile]
            before = update[sweep - 1, x - 1, tile] if x > first else None
            after = update[sweep - 1, x + 1, tile] if x < last else None
            remainder = beside_terms(before, here, after, x, tile, coefs)
            if sweep > 1:
                remainder = remainder + (left[x, tile] - here)
            if rest:
                left[x, tile] = remainder
            value = rho_next * rho * here + (2.0 * rho_next / cheb_radius) * jnp.where(inside, remainder, 0.0)
            if rest:
                update[sweep, x, tile] = value
            else:
                for k in range(CHEB - 1):
                    value = value + update[k, x, tile]
                estimate[x] = value
        rho = rho_next
    return estimate


def smooth(
    flags, early_planes, wide, sides, past, early, late, diagonal, coefs, corr, field_out, image_out, scratch
):
    source, left, update, whole = scratch
    inverse, b0, b1, _ = coefs
    size_x, size_y, size_z = corr.shape
    rows = size_y + 2 * WIDE
    span = size_x + 2 * WIDE
    row = lax.broadcasted_iota(jnp.int32, (rows, size_z), 0)
    has_low_x, has_high_x = flags[LOW_X] != 0, flags[HIGH_X] != 0
    has_low_y, has_high_y = flags[LOW_Y] != 0, flags[HIGH_Y] != 0
    lowest, highest = slice(0, 8), slice(rows - 8, rows)
    tile_row = lax.broadcasted_iota(jnp.int32, (8, size_z), 0)
    end = WIDE + size_y

    def put(out, x, middle, ends):
        out[x, 0:WIDE, :] = ends[0:WIDE, :]
        for row_ in range(0, size_y, 8):
            out[x, WIDE + row_ : WIDE + row_ + 8, :] = middle(row_)
        out[x, end:rows, :] = ends[WIDE : 2 * WIDE, :]

    def halo(side, first, edge, present):
        message, ends = side
        for k in range(WIDE):
            x = first + k
            if k < early_planes:
                middle = lambda row_: message[1 + k, row_ : row_ + 8, :]
            else:
                tile = ends.shape[0] - (WIDE - k) * (size_y // 8)
                middle = lambda row_: ends[tile + row_ // 8]
            put(source, x, middle, ends.at[k])
            source[x] = inverse[x] * source[x]
            for row_, weight, line in ((WIDE, b1, k), (end - 1, inverse, WIDE + k)):
                at = slice(row_, row_ + 1)
                source[x, at] = source[x, at] + weight[x, at] * ends[WIDE + 1, line : line + 1, :]
        put(whole, edge, lambda row_: message[0, row_ : row_ + 8, :], ends.at[WIDE])
        whole[edge] = jnp.where(present, whole[edge], 0.0)

    def halos(low, high):
        halo(low, 0, 0, has_low_x)
        halo(high, WIDE + size_x, size_x + 1, has_high_x)

    by_side(flags[ODD_X], halos, early, late)

    for k in range(size_x):
        source[WIDE + k] = inverse[WIDE + k] * wide[k]

    low_in, high_in = WIDE, WIDE + size_x - 1
    source[low_in - 1] = source[low_in - 1] + inverse[low_in - 1] * sides[0]
    source[low_in] = source[low_in] + b0[low_in] * whole[0]
    source[high_in] = source[high_in] + inverse[high_in] * whole[size_x + 1]
    source[high_in + 1] = source[high_in + 1] + b0[high_in + 1] * sides[1]

    def run(planes, tile, inside, wanted):
        return chebyshev(
            planes,
            tile,
            inside,
            lambda x: source[x, tile],
            left,
            update,
            coefs,
            wanted,
        )

    everything = slice(0, rows)
    box_rows = (row >= WIDE - DEPTH) & (row < WIDE + size_y + DEPTH)
    box_planes = range(WIDE - DEPTH, WIDE + size_x + DEPTH)
    own_planes = range(WIDE, WIDE + size_x)
    inner = (row >= WIDE) & (row < WIDE + size_y)

    beside = run(range(0, WIDE + DEPTH), everything, box_rows, (WIDE - 1,))[WIDE - 1]
    whole[0] = jnp.where(has_low_x & inner, whole[0] + beside, 0.0)
    x = WIDE + size_x
    beside = run(range(span - WIDE - DEPTH, span), everything, box_rows, (x,))[x]
    whole[size_x + 1] = jnp.where(has_high_x & inner, whole[size_x + 1] + beside, 0.0)

    own = run(box_planes, everything, box_rows, tuple(own_planes))
    zeros = jnp.zeros((rows - size_y, size_z), F32)
    for k in range(size_x):
        placed = pltpu.roll(jnp.concatenate([corr[k], zeros], axis=0), WIDE, 0)
        whole[k + 1] = jnp.where(inner, placed + own[WIDE + k], 0.0)

    beside = run(box_planes, lowest, tile_row < WIDE + DEPTH, tuple(own_planes))
    for k in range(size_x):
        line = past[0, k : k + 1, :] + beside[WIDE + k]
        here = has_low_y & (tile_row == WIDE - 1)
        whole[k + 1, lowest] = jnp.where(here, line, whole[k + 1, lowest])
    beside = run(box_planes, highest, tile_row >= 8 - WIDE - DEPTH, tuple(own_planes))
    for k in range(size_x):
        line = past[1, k : k + 1, :] + beside[WIDE + k]
        here = has_high_y & (tile_row == 8 - WIDE)
        whole[k + 1, highest] = jnp.where(here, line, whole[k + 1, highest])

    for k in range(size_x):
        x = WIDE + k
        terms = beside_terms(whole[k], whole[k + 1], whole[k + 2], x, everything, coefs)
        image = diagonal[k] * (whole[k + 1] - terms)
        image_out[k] = pltpu.roll(image, rows - WIDE, 0)[0:size_y]
        field_out[k] = pltpu.roll(whole[k + 1], rows - WIDE, 0)[0:size_y]


def dot_planes(left, right):
    total = left[0] * right[0]
    for x in range(1, left.shape[0]):
        total = total + left[x] * right[x]
    return total


def search_kernel(
    flags, wide, sides, past, odd_late, even_late, diagonal, own0, own1, own2, own3, corr, odd_early, even_early, vectors,
    right_side, search, image, out, halo0, halo1, halo2, halo3, stage, wide_vel, *scratch
):
    halos = (halo0, halo1, halo2, halo3)
    early, late = (even_early, odd_early), (even_late, odd_late)
    halo_coefficients(flags, early, late, halos, wide_vel)
    coefs = [Region(*pair) for pair in zip((own0, own1, own2, own3), halos)]
    smooth(flags, EARLY_FIRST, wide, sides, past, early, late, diagonal, coefs, corr, search, image, scratch)
    products = [dot_planes(right_side, right_side), dot_planes(right_side, image)]
    restrict(vectors, image, products, flags, (out, stage))


def smoothed_kernel(
    flags, wide, sides, past, odd_late, even_late, diagonal, own0, own1, own2, own3, corr, odd_early, even_early, halo0,
    halo1, halo2, halo3, middle, smoothed, turned, out, *scratch
):
    early, late = (even_early, odd_early), (even_late, odd_late)
    coefs = [Region(*pair) for pair in zip((own0, own1, own2, own3), (halo0, halo1, halo2, halo3))]
    smooth(flags, WIDE, wide, sides, past, early, late, diagonal, coefs, corr, smoothed, turned, scratch)
    lane = lax.broadcasted_iota(jnp.int32, (1, LANES), 1)
    sums = jnp.zeros((1, LANES), F32)
    for k, total in enumerate((dot_planes(turned, middle), dot_planes(turned, turned))):
        total = jnp.sum(jnp.sum(total, axis=0, keepdims=True), axis=1, keepdims=True)
        sums = jnp.where(lane == k, total, sums)
    row = jnp.concatenate([jnp.zeros((1, LANES), F32), sums], axis=1)
    for k in range(out.shape[0]):
        out[k] = row


def last_kernel(flags, received, alpha, search, smoothed, middle, turned, solution_field, residual):
    sums = summed(received)
    omega = sums[:, 0:1] / sums[:, 1:2]
    step = alpha[0:1, 0:1]
    for x in range(search.shape[0]):
        solution_field[x] = step * search[x] + omega * smoothed[x]
        residual[x] = middle[x] - omega * turned[x]


def local(right_side, velocity, deflation, inverse_rows):
    size_x, size_y, size_z = right_side.shape
    vectors_count = deflation.shape[0]
    count_x, count_y = lax.axis_size("gx"), lax.axis_size("gy")
    count = count_x * count_y
    at_x, at_y = lax.axis_index("gx"), lax.axis_index("gy")
    kernel_call = functools.partial(call, vectors_count)
    x_pairs, y_pairs = pair_permutations(count_x, count_y)

    def swap(messages, pairs):
        odd = lax.ppermute(messages[1], AXES, pairs[1])
        return [lax.ppermute(messages[0], AXES, pairs[0]), odd]

    def share(row):
        return lax.all_to_all(row, AXES, 0, 0)

    rows = size_y + 2 * WIDE
    span = size_x + 2 * WIDE
    block = (size_x, size_y, size_z)
    row = pltpu.VMEM((count, 1, 2 * LANES), F32)
    stage = (2 * LANES, LANES)
    y_message = (size_x + size_x // WIDE + 2, WIDE, size_z)
    region = (span, rows, size_z)
    smooth_scratch = [region, region, (CHEB - 1,) + region, (size_x + 2, rows, size_z)]

    chunks = 8
    arguments = (right_side, deflation, velocity, inverse_rows)
    first_row, right_side, deflation, velocity, inverse_rows = kernel_call(
        first_kernel,
        [row] + [pltpu.VMEM(argument.shape, argument.dtype) for argument in arguments],
        [stage, pltpu.SemaphoreType.DMA((chunks + 3,))],
        *[pltpu.with_memory_space_constraint(argument, pltpu.HBM) for argument in arguments],
        micros=2.0,
        streamed=True,
    )
    first = share(first_row)
    faces_y = (3, size_x, WIDE, size_z)
    x_early = (WIDE + 1, size_y, size_z)
    x_early_first = (1 + EARLY_FIRST + 3 * WIDE, size_y, size_z)
    velocity_y = kernel_call(velocity_y_kernel, [faces_y] * 2, [], velocity, micros=0.01)
    after = velocity_y[0]
    velocity_y = swap(velocity_y, y_pairs)

    wide_own, wide_halo = (size_x, rows, size_z), (2 * WIDE, rows, size_z)

    def exchange(corr, rest, messages, corners, early_planes):
        tiles = WIDE + 2 + (3 * WIDE if corners else 0) + (WIDE - early_planes) * (size_y // 8)
        message = (tiles, 2 * WIDE, size_z)
        y_messages, early = swap(messages[:2], y_pairs), swap(messages[2:], x_pairs)
        *own, even, odd = kernel_call(
            functools.partial(extend_kernel, corners=corners, early_planes=early_planes),
            [wide_own, (2, rows, size_z), (2, size_x, size_z), message, message],
            [],
            rest,
            corr,
            *y_messages[::-1],
            velocity,
            *velocity_y,
            micros=0.01,
        )
        return (*own, *swap((even, odd), x_pairs)[::-1], *coefs, corr, *early[::-1])

    corr, rest, *messages = kernel_call(
        coarse_kernel,
        [block, block, y_message, y_message, x_early_first, x_early_first],
        [],
        first,
        inverse_rows,
        deflation,
        right_side,
        velocity,
        after,
        micros=1.4,
    )
    coefs = kernel_call(
        coefficients_kernel,
        [wide_own] * 5,
        [(3, size_x, rows, size_z)],
        velocity,
        *velocity_y,
        micros=0.01,
    )
    search, image, second_row, *halo_coefs = kernel_call(
        search_kernel,
        [block, block, row] + [wide_halo] * 4,
        [stage, (3, rows, size_z)] + smooth_scratch,
        *exchange(corr, rest, messages, True, EARLY_FIRST),
        deflation,
        right_side,
        micros=3.0,
    )
    second = share(second_row)
    corr, rest, middle, alpha, *messages = kernel_call(
        second_coarse_kernel,
        [block, block, block, (8, LANES), y_message, y_message, x_early, x_early],
        [],
        first,
        second,
        inverse_rows,
        deflation,
        right_side,
        image,
        velocity,
        micros=1.4,
    )
    smoothed, turned, third_row = kernel_call(
        smoothed_kernel,
        [block, block, row],
        smooth_scratch,
        *exchange(corr, rest, messages, False, WIDE),
        *halo_coefs,
        middle,
        micros=2.5,
    )
    third = share(third_row)
    return tuple(
        kernel_call(last_kernel, [block, block], [], third, alpha, search, smoothed, middle, turned, micros=1.4)
    )


def solution(mesh):
    return jax.shard_map(
        local,
        mesh=mesh,
        in_specs=(
            P("gx", "gy", None),
            P(None, "gx", "gy", None),
            P(None, "gx", "gy", None),
            P(("gx", "gy"), None),
        ),
        out_specs=(P("gx", "gy", None), P("gx", "gy", None)),
        check_vma=False,
    )
```

```python
import functools

import jax
import jax.numpy as jnp
from jax import lax
from jax.experimental import pallas as pl
from jax.experimental.pallas import tpu as pltpu
from jax.sharding import PartitionSpec as P

DEPTH = 2
CHEB = 4
WIDE = 4
EARLY_FIRST = 0
LANES = 128
AXES = ("gx", "gy")
F32 = jnp.float32
HIGHEST = lax.Precision.HIGHEST

cheb_center = 1.0
cheb_radius = 0.9

ODD_X, ODD_Y, LOW_X, HIGH_X, LOW_Y, HIGH_Y, SLOT = range(7)

def pair_permutations(count_x, count_y):
    def number(i, j):
        return i * count_y + j

    even_x, odd_x, even_y, odd_y = [], [], [], []
    for i in range(count_x):
        for j in range(count_y):
            here = number(i, j)
            even_x.append((here, number(i ^ 1, j)))
            even_y.append((here, number(i, j ^ 1)))
            other = ((i - 1) ^ 1) + 1
            odd_x.append((here, number(other, j) if 0 <= other < count_x else number(i, j ^ 1)))
            other = ((j - 1) ^ 1) + 1
            odd_y.append((here, number(i, other) if 0 <= other < count_y else number(i ^ 1, j)))
    return (even_x, odd_x), (even_y, odd_y)


def place_flags(vectors_count):
    count_x, count_y = lax.axis_size("gx"), lax.axis_size("gy")
    at_x, at_y = lax.axis_index("gx"), lax.axis_index("gy")
    return (
        lax.rem(at_x, 2),
        lax.rem(at_y, 2),
        (at_x > 0).astype(jnp.int32),
        (at_x < count_x - 1).astype(jnp.int32),
        (at_y > 0).astype(jnp.int32),
        (at_y < count_y - 1).astype(jnp.int32),
        lax.rem(at_x * count_y + at_y, LANES // vectors_count),
    )


def call(vectors, body, outs, scratch, *args, micros, streamed=False):
    def kernel(*refs):
        body(place_flags(vectors), *refs)

    return pl.pallas_call(
        kernel,
        out_shape=[jax.ShapeDtypeStruct(kind, F32) if isinstance(kind, tuple) else kind for kind in outs],
        in_specs=[pl.BlockSpec(memory_space=pltpu.HBM if streamed else pltpu.VMEM)] * len(args),
        out_specs=[pl.BlockSpec(memory_space=pltpu.VMEM)] * len(outs),
        scratch_shapes=[pltpu.VMEM(kind, F32) if isinstance(kind, tuple) else kind for kind in scratch],
        compiler_params=pltpu.CompilerParams(vmem_limit_bytes=24 * 1024 * 1024),
        cost_estimate=pl.CostEstimate(flops=0, bytes_accessed=int(micros * 3.6e6), transcendentals=0),
    )(*args)


def shift_z(plane, ahead):
    width = plane.shape[1]
    lane = lax.broadcasted_iota(jnp.int32, (plane.shape[0], LANES), 1)
    edge = LANES - 1 if ahead else 0
    turned = [pltpu.roll(plane[:, i : i + LANES], LANES - 1 if ahead else 1, 1) for i in range(0, width, LANES)]
    beside = turned[1:] + [0.0] if ahead else [0.0] + turned[:-1]
    return jnp.concatenate([jnp.where(lane == edge, far, near) for near, far in zip(turned, beside)], axis=1)


def restrict(vectors, fields, sums, flags, send, copies=()):
    count, size_x, size_y, size_z = vectors.shape
    out, stage = send
    stage[...] = jnp.zeros_like(stage)

    def lanes_of(total):
        total = jnp.sum(total, axis=0, keepdims=True)
        return functools.reduce(jnp.add, [total[:, k : k + LANES] for k in range(0, size_z, LANES)])

    offset = pl.multiple_of(flags[SLOT] * count, count)
    for j in range(count):
        if copies and j % (count // len(copies)) == 0:
            copies[j // (count // len(copies))].wait()
        totals = [0.0] * len(fields)
        for x in range(size_x):
            plane = vectors[j, x].astype(F32)
            totals = [total + plane * field[x] for total, field in zip(totals, fields)]
        for k, total in enumerate(totals):
            stage[pl.ds(k * LANES + offset + j, 1), :] = lanes_of(total)
    for k, total in enumerate(sums):
        stage[LANES + k : LANES + k + 1, :] = lanes_of(total)
    write_row(stage, out)


def write_row(stage, out):
    row = lax.dot_general(
        jnp.ones((8, LANES), F32), stage[...], (((1,), (1,)), ((), ())), precision=HIGHEST, preferred_element_type=F32
    )
    for k in range(out.shape[0]):
        out[k] = row[0:1]


def gathered(received, vectors, part=0):
    share = LANES // vectors.shape[0]
    return [
        functools.reduce(jnp.add, [received[k + i, :, part * LANES : (part + 1) * LANES] for i in range(share)])
        for k in range(0, received.shape[0], share)
    ]


def summed(received):
    return functools.reduce(jnp.add, [received[k, :, LANES:] for k in range(received.shape[0])])


def solve(coarse, inverse):
    total = inverse[:, :LANES] * coarse[0]
    for k in range(1, len(coarse)):
        total = total + inverse[:, k * LANES : (k + 1) * LANES] * coarse[k]
    return jnp.sum(total, axis=1, keepdims=True).astype(jnp.bfloat16).astype(F32)


def prolong(solved, vectors, corr):
    count, size_x, size_y, size_z = vectors.shape
    totals = [jnp.zeros((size_y, size_z), F32) for _ in range(size_x)]
    for j in range(count):
        weight = jnp.broadcast_to(solved[j : j + 1], (size_y, size_z))
        for x in range(size_x):
            totals[x] = totals[x] + vectors[j, x].astype(F32) * weight
    for x in range(size_x):
        corr[x] = totals[x]


def subtract_own(field, corr, velocity, out):
    size_x, size_y, size_z = corr.shape
    rows = lax.broadcasted_iota(jnp.int32, (size_y, size_z), 0)
    for x in range(size_x):
        v0, v1, v2 = velocity[0, x], velocity[1, x], velocity[2, x]
        here = corr[x]
        image = (6.0 + v0 + v1 + v2) * here
        if x + 1 < size_x:
            image = image - corr[x + 1]
        if x > 0:
            image = image - (1.0 + v0) * corr[x - 1]
        image = image - jnp.where(rows < size_y - 1, pltpu.roll(here, size_y - 1, 0), 0.0)
        image = image - (1.0 + v1) * jnp.where(rows > 0, pltpu.roll(here, 1, 0), 0.0)
        image = image - shift_z(here, True) - (1.0 + v2) * shift_z(here, False)
        out[x] = field[x] - image


def write_y_message(out, field, corr, high):
    size_x, size_y, _ = corr.shape
    start = size_y - WIDE if high else 0
    edge = size_y - 1 if high else 0
    for x in range(size_x):
        out[x] = field[x, start : start + WIDE, :]
        out[size_x + x // WIDE, x % WIDE : x % WIDE + 1, :] = corr[x, edge : edge + 1, :]
    last = size_x + size_x // WIDE
    out[last] = corr[0, start : start + WIDE, :]
    out[last + 1] = corr[size_x - 1, start : start + WIDE, :]


def by_parity(odd, write, even_out, odd_out):
    @pl.when(odd == 0)
    def _():
        write(even_out, True)
        write(odd_out, False)

    @pl.when(odd != 0)
    def _():
        write(even_out, False)
        write(odd_out, True)


def first_kernel(
    flags, field, vectors, velocity, inverse, out, held_field, held_vectors, held_velocity, held_inverse, stage, sems
):
    parts = sems.shape[0] - 3
    step = vectors.shape[0] // parts
    chunks = [pl.ds(part * step, step) for part in range(parts)]
    pairs = [(field, held_field)] + [(vectors.at[chunk], held_vectors.at[chunk]) for chunk in chunks]
    pairs += [(velocity, held_velocity), (inverse, held_inverse)]
    copies = [pltpu.make_async_copy(here, there, sems.at[k]) for k, (here, there) in enumerate(pairs)]
    for copy in copies:
        copy.start()
    copies[0].wait()
    rounded = [held_field[x].astype(jnp.bfloat16).astype(F32) for x in range(field.shape[0])]
    restrict(held_vectors, [rounded, held_field], [], flags, (out, stage), copies[1 : 1 + parts])
    for copy in copies[1 + parts :]:
        copy.wait()


def by_side(odd, use, *pairs):
    evens, odds = [pair[0] for pair in pairs], [pair[1] for pair in pairs]

    @pl.when(odd == 0)
    def _():
        use(odds, evens)

    @pl.when(odd != 0)
    def _():
        use(evens, odds)


def velocity_y_kernel(flags, velocity, even_out, odd_out):
    _, size_x, size_y, _ = velocity.shape

    def write_y(out, high):
        start = size_y - WIDE if high else 0
        for d in range(3):
            for x in range(size_x):
                out[d, x] = velocity[d, x, start : start + WIDE, :]

    by_parity(flags[ODD_Y], write_y, even_out, odd_out)


def write_x_early(flags, planes, rest, corr, velocity, even_out, odd_out):
    size_x = rest.shape[0]

    def write(out, high):
        start = size_x - WIDE if high else 0
        out[0] = corr[size_x - 1 if high else 0]
        for k in range(planes):
            out[1 + k] = rest[start + k]
        if velocity is not None:
            for d in range(3):
                for k in range(WIDE):
                    out[1 + planes + d * WIDE + k] = velocity[d, start + k]

    by_parity(flags[ODD_X], write, even_out, odd_out)


def coefficients(x, v0, v1, v2, kept, outs):
    inverse, b0, b1, b2 = outs
    total = 6.0 + v0 + v1 + v2
    value = jnp.where(kept, 1.0 / total, 0.0)
    inverse[x] = value
    b0[x] = value * (1.0 + v0)
    b1[x] = value * (1.0 + v1)
    b2[x] = value * (1.0 + v2)
    return total


def rows_in_grid(flags, shape):
    row = lax.broadcasted_iota(jnp.int32, shape, 0)
    first_row = jnp.where(flags[LOW_Y] != 0, 0, WIDE)
    end_row = jnp.where(flags[HIGH_Y] != 0, shape[0], shape[0] - WIDE)
    return (row >= first_row) & (row < end_row)


def coefficients_kernel(flags, velocity, even_in, odd_in, diagonal, inverse, b0, b1, b2, wide):
    _, size_x, size_y, size_z = velocity.shape
    rows = size_y + 2 * WIDE

    def place(low, high):
        for d in range(3):
            for x in range(size_x):
                wide[d, x, 0:WIDE, :] = low[d, x]
                wide[d, x, WIDE : WIDE + size_y, :] = velocity[d, x]
                wide[d, x, WIDE + size_y : rows, :] = high[d, x]

    @pl.when(flags[ODD_Y] == 0)
    def _():
        place(odd_in, even_in)

    @pl.when(flags[ODD_Y] != 0)
    def _():
        place(even_in, odd_in)

    kept = rows_in_grid(flags, (rows, size_z))
    for x in range(size_x):
        diagonal[x] = coefficients(x, wide[0, x], wide[1, x], wide[2, x], kept, (inverse, b0, b1, b2))


def halo_coefficients(flags, early, late, outs, wide):
    size_y, size_z = early[0].shape[1:]
    rows = size_y + 2 * WIDE
    kept = rows_in_grid(flags, (rows, size_z))

    def side(start, message, corners, present):
        for k in range(WIDE):
            for d in range(3):
                tile = WIDE + 2 + d * WIDE + k
                wide[d, 0:WIDE, :] = corners[tile, 0:WIDE, :]
                wide[d, WIDE : WIDE + size_y, :] = message[1 + EARLY_FIRST + d * WIDE + k]
                wide[d, WIDE + size_y : rows, :] = corners[tile, WIDE : 2 * WIDE, :]
            coefficients(start + k, wide[0], wide[1], wide[2], kept & (flags[present] != 0), outs)

    by_side(flags[ODD_X], lambda low, high: (side(0, *low, LOW_X), side(WIDE, *high, HIGH_X)), early, late)


class Region:
    def __init__(self, own, halo):
        self.own, self.halo = own, halo

    def __getitem__(self, index):
        x, tile = index if isinstance(index, tuple) else (index, slice(None))
        size_x = self.own.shape[0]
        if x < WIDE:
            return self.halo[x, tile]
        return self.own[x - WIDE, tile] if x < WIDE + size_x else self.halo[x - size_x, tile]


def coarse_kernel(
    flags, received, inverse, vectors, field, velocity, after, corr, rest, even_out, odd_out, even_x, odd_x
):
    prolong(solve(gathered(received, vectors), inverse), vectors, corr)
    subtract_own(field, corr, velocity, rest)
    by_parity(flags[ODD_Y], lambda out, high: write_y_message(out, rest, corr, high), even_out, odd_out)
    write_x_early(flags, EARLY_FIRST, rest, corr, velocity, even_x, odd_x)


def second_coarse_kernel(
    flags, received, second, inverse, vectors, field, image, velocity, corr, rest, middle, alpha, even_out, odd_out,
    even_x, odd_x
):
    products = summed(second)
    step = jnp.broadcast_to(products[:, 0:1] / products[:, 1:2], alpha.shape)
    alpha[...] = step
    step = step[0:1, 0:1]
    for x in range(field.shape[0]):
        middle[x] = field[x] - step * image[x]
    pairs = zip(gathered(received, vectors, 1), gathered(second, vectors))
    prolong(solve([coarse - step * of_image for coarse, of_image in pairs], inverse), vectors, corr)
    subtract_own(middle, corr, velocity, rest)
    by_parity(flags[ODD_Y], lambda out, high: write_y_message(out, rest, corr, high), even_out, odd_out)
    write_x_early(flags, WIDE, rest, corr, None, even_x, odd_x)


def extend_kernel(
    flags, rest, corr, odd_in, even_in, velocity, even_vel, odd_vel, wide, sides, past, even_out, odd_out, corners, early_planes
):
    size_x, size_y, size_z = rest.shape
    rows = size_y + 2 * WIDE
    end = WIDE + size_y

    def place(low, high, high_vel):
        has_low, has_high = flags[LOW_Y] != 0, flags[HIGH_Y] != 0
        for x in range(size_x):
            at, line = size_x + x // WIDE, slice(x % WIDE, x % WIDE + 1)
            past_low = jnp.where(has_low, low[at, line, :], 0.0)
            past_high = jnp.where(has_high, high[at, line, :], 0.0)
            past[0, x : x + 1, :] = past_low
            past[1, x : x + 1, :] = past_high
            wide[x, 0 : WIDE - 1, :] = low[x, 0 : WIDE - 1, :]
            wide[x, WIDE - 1 : WIDE, :] = low[x, WIDE - 1 : WIDE, :] + corr[x, 0:1, :]
            wide[x, WIDE:end, :] = rest[x]
            wide[x, WIDE : WIDE + 1, :] = rest[x, 0:1, :] + (1.0 + velocity[1, x, 0:1, :]) * past_low
            wide[x, end - 1 : end, :] = rest[x, size_y - 1 : size_y, :] + past_high
            weight = 1.0 + high_vel[1, x, 0:1, :]
            wide[x, end : end + 1, :] = high[x, 0:1, :] + weight * corr[x, size_y - 1 : size_y, :]
            wide[x, end + 1 : rows, :] = high[x, 1:WIDE, :]
        last = size_x + size_x // WIDE
        for side, x in enumerate((0, size_x - 1)):
            sides[side, 0:WIDE, :] = low[last + side]
            sides[side, WIDE:end, :] = corr[x]
            sides[side, end:rows, :] = high[last + side]

    @pl.when(flags[ODD_Y] == 0)
    def _():
        place(odd_in, even_in, even_vel)

    @pl.when(flags[ODD_Y] != 0)
    def _():
        place(even_in, odd_in, odd_vel)

    def write(out, high):
        start = size_x - WIDE if high else 0
        for k in range(WIDE):
            out[k, 0:WIDE, :] = wide[start + k, 0:WIDE, :]
            out[k, WIDE : 2 * WIDE, :] = wide[start + k, end:rows, :]
        side = 1 if high else 0
        out[WIDE, 0:WIDE, :] = sides[side, 0:WIDE, :]
        out[WIDE, WIDE : 2 * WIDE, :] = sides[side, end:rows, :]
        out[WIDE + 1, 0:WIDE, :] = past[0, start : start + WIDE, :]
        out[WIDE + 1, WIDE : 2 * WIDE, :] = past[1, start : start + WIDE, :]

        tile = WIDE + 2 + (3 * WIDE if corners else 0)
        for k in range(early_planes, WIDE):
            for row in range(0, size_y, 8):
                out[tile] = rest[start + k, row : row + 8, :]
                tile += 1

    by_parity(flags[ODD_X], write, even_out, odd_out)
    if not corners:
        return

    def write_corners(low, high):
        def write(out, upper):
            start = size_x - WIDE if upper else 0
            for d in range(3):
                for k in range(WIDE):
                    tile = WIDE + 2 + d * WIDE + k
                    out[tile, 0:WIDE, :] = low[0][d, start + k]
                    out[tile, WIDE : 2 * WIDE, :] = high[0][d, start + k]

        by_parity(flags[ODD_X], write, even_out, odd_out)

    by_side(flags[ODD_Y], write_corners, (even_vel, odd_vel))


def beside_terms(before, here, after, x, tile, coefs):
    inverse, b0, b1, b2 = coefs
    rows = here.shape[0]
    ahead = pltpu.roll(here, rows - 1, 0) + shift_z(here, True)
    if after is not None:
        ahead = ahead + after
    total = inverse[x, tile] * ahead + b1[x, tile] * pltpu.roll(here, 1, 0) + b2[x, tile] * shift_z(here, False)
    if before is not None:
        total = total + b0[x, tile] * before
    return total


def chebyshev(planes, tile, inside, source, left, update, coefs, wanted):
    sigma = cheb_center / cheb_radius
    rho = 1.0 / sigma
    first, last = planes[0], planes[-1]
    for x in planes:
        update[0, x, tile] = jnp.where(inside, source(x), 0.0)
    estimate = {}
    for sweep in range(1, CHEB):
        rest = CHEB - 1 - sweep
        low, high = max(first, wanted[0] - rest), min(last, wanted[-1] + rest)
        rho_next = 1.0 / (2.0 * sigma - rho)
        for x in range(low, high + 1):
            here = update[sweep - 1, x, tile]
            before = update[sweep - 1, x - 1, tile] if x > first else None
            after = update[sweep - 1, x + 1, tile] if x < last else None
            remainder = beside_terms(before, here, after, x, tile, coefs)
            if sweep > 1:
                remainder = remainder + (left[x, tile] - here)
            if rest:
                left[x, tile] = remainder
            value = rho_next * rho * here + (2.0 * rho_next / cheb_radius) * jnp.where(inside, remainder, 0.0)
            if rest:
                update[sweep, x, tile] = value
            else:
                for k in range(CHEB - 1):
                    value = value + update[k, x, tile]
                estimate[x] = value
        rho = rho_next
    return estimate


def smooth(
    flags, early_planes, wide, sides, past, early, late, diagonal, coefs, corr, field_out, image_out, scratch
):
    source, left, update, whole = scratch
    inverse, b0, b1, _ = coefs
    size_x, size_y, size_z = corr.shape
    rows = size_y + 2 * WIDE
    span = size_x + 2 * WIDE
    row = lax.broadcasted_iota(jnp.int32, (rows, size_z), 0)
    has_low_x, has_high_x = flags[LOW_X] != 0, flags[HIGH_X] != 0
    has_low_y, has_high_y = flags[LOW_Y] != 0, flags[HIGH_Y] != 0
    lowest, highest = slice(0, 8), slice(rows - 8, rows)
    tile_row = lax.broadcasted_iota(jnp.int32, (8, size_z), 0)
    end = WIDE + size_y

    def put(out, x, middle, ends):
        out[x, 0:WIDE, :] = ends[0:WIDE, :]
        for row_ in range(0, size_y, 8):
            out[x, WIDE + row_ : WIDE + row_ + 8, :] = middle(row_)
        out[x, end:rows, :] = ends[WIDE : 2 * WIDE, :]

    def halo(side, first, edge, present):
        message, ends = side
        for k in range(WIDE):
            x = first + k
            if k < early_planes:
                middle = lambda row_: message[1 + k, row_ : row_ + 8, :]
            else:
                tile = ends.shape[0] - (WIDE - k) * (size_y // 8)
                middle = lambda row_: ends[tile + row_ // 8]
            put(source, x, middle, ends.at[k])
            source[x] = inverse[x] * source[x]
            for row_, weight, line in ((WIDE, b1, k), (end - 1, inverse, WIDE + k)):
                at = slice(row_, row_ + 1)
                source[x, at] = source[x, at] + weight[x, at] * ends[WIDE + 1, line : line + 1, :]
        put(whole, edge, lambda row_: message[0, row_ : row_ + 8, :], ends.at[WIDE])
        whole[edge] = jnp.where(present, whole[edge], 0.0)

    def halos(low, high):
        halo(low, 0, 0, has_low_x)
        halo(high, WIDE + size_x, size_x + 1, has_high_x)

    by_side(flags[ODD_X], halos, early, late)

    for k in range(size_x):
        source[WIDE + k] = inverse[WIDE + k] * wide[k]

    low_in, high_in = WIDE, WIDE + size_x - 1
    source[low_in - 1] = source[low_in - 1] + inverse[low_in - 1] * sides[0]
    source[low_in] = source[low_in] + b0[low_in] * whole[0]
    source[high_in] = source[high_in] + inverse[high_in] * whole[size_x + 1]
    source[high_in + 1] = source[high_in + 1] + b0[high_in + 1] * sides[1]

    def run(planes, tile, inside, wanted):
        return chebyshev(
            planes,
            tile,
            inside,
            lambda x: source[x, tile],
            left,
            update,
            coefs,
            wanted,
        )

    everything = slice(0, rows)
    box_rows = (row >= WIDE - DEPTH) & (row < WIDE + size_y + DEPTH)
    box_planes = range(WIDE - DEPTH, WIDE + size_x + DEPTH)
    own_planes = range(WIDE, WIDE + size_x)
    inner = (row >= WIDE) & (row < WIDE + size_y)

    beside = run(range(0, WIDE + DEPTH), everything, box_rows, (WIDE - 1,))[WIDE - 1]
    whole[0] = jnp.where(has_low_x & inner, whole[0] + beside, 0.0)
    x = WIDE + size_x
    beside = run(range(span - WIDE - DEPTH, span), everything, box_rows, (x,))[x]
    whole[size_x + 1] = jnp.where(has_high_x & inner, whole[size_x + 1] + beside, 0.0)

    own = run(box_planes, everything, box_rows, tuple(own_planes))
    zeros = jnp.zeros((rows - size_y, size_z), F32)
    for k in range(size_x):
        placed = pltpu.roll(jnp.concatenate([corr[k], zeros], axis=0), WIDE, 0)
        whole[k + 1] = jnp.where(inner, placed + own[WIDE + k], 0.0)

    beside = run(box_planes, lowest, tile_row < WIDE + DEPTH, tuple(own_planes))
    for k in range(size_x):
        line = past[0, k : k + 1, :] + beside[WIDE + k]
        here = has_low_y & (tile_row == WIDE - 1)
        whole[k + 1, lowest] = jnp.where(here, line, whole[k + 1, lowest])
    beside = run(box_planes, highest, tile_row >= 8 - WIDE - DEPTH, tuple(own_planes))
    for k in range(size_x):
        line = past[1, k : k + 1, :] + beside[WIDE + k]
        here = has_high_y & (tile_row == 8 - WIDE)
        whole[k + 1, highest] = jnp.where(here, line, whole[k + 1, highest])

    for k in range(size_x):
        x = WIDE + k
        terms = beside_terms(whole[k], whole[k + 1], whole[k + 2], x, everything, coefs)
        image = diagonal[k] * (whole[k + 1] - terms)
        image_out[k] = pltpu.roll(image, rows - WIDE, 0)[0:size_y]
        field_out[k] = pltpu.roll(whole[k + 1], rows - WIDE, 0)[0:size_y]


def dot_planes(left, right):
    total = left[0] * right[0]
    for x in range(1, left.shape[0]):
        total = total + left[x] * right[x]
    return total


def search_kernel(
    flags, wide, sides, past, odd_late, even_late, diagonal, own0, own1, own2, own3, corr, odd_early, even_early, vectors,
    right_side, search, image, out, halo0, halo1, halo2, halo3, stage, wide_vel, *scratch
):
    halos = (halo0, halo1, halo2, halo3)
    early, late = (even_early, odd_early), (even_late, odd_late)
    halo_coefficients(flags, early, late, halos, wide_vel)
    coefs = [Region(*pair) for pair in zip((own0, own1, own2, own3), halos)]
    smooth(flags, EARLY_FIRST, wide, sides, past, early, late, diagonal, coefs, corr, search, image, scratch)
    products = [dot_planes(right_side, right_side), dot_planes(right_side, image)]
    restrict(vectors, [image], products, flags, (out, stage))


def smoothed_kernel(
    flags, wide, sides, past, odd_late, even_late, diagonal, own0, own1, own2, own3, corr, odd_early, even_early, halo0,
    halo1, halo2, halo3, middle, smoothed, turned, out, *scratch
):
    early, late = (even_early, odd_early), (even_late, odd_late)
    coefs = [Region(*pair) for pair in zip((own0, own1, own2, own3), (halo0, halo1, halo2, halo3))]
    smooth(flags, WIDE, wide, sides, past, early, late, diagonal, coefs, corr, smoothed, turned, scratch)
    lane = lax.broadcasted_iota(jnp.int32, (1, LANES), 1)
    sums = jnp.zeros((1, LANES), F32)
    for k, total in enumerate((dot_planes(turned, middle), dot_planes(turned, turned))):
        total = jnp.sum(jnp.sum(total, axis=0, keepdims=True), axis=1, keepdims=True)
        sums = jnp.where(lane == k, total, sums)
    row = jnp.concatenate([jnp.zeros((1, LANES), F32), sums], axis=1)
    for k in range(out.shape[0]):
        out[k] = row


def last_kernel(flags, received, alpha, search, smoothed, middle, turned, solution_field, residual):
    sums = summed(received)
    omega = sums[:, 0:1] / sums[:, 1:2]
    step = alpha[0:1, 0:1]
    for x in range(search.shape[0]):
        solution_field[x] = step * search[x] + omega * smoothed[x]
        residual[x] = middle[x] - omega * turned[x]


def local(right_side, velocity, deflation, inverse_rows):
    size_x, size_y, size_z = right_side.shape
    vectors_count = deflation.shape[0]
    count_x, count_y = lax.axis_size("gx"), lax.axis_size("gy")
    count = count_x * count_y
    at_x, at_y = lax.axis_index("gx"), lax.axis_index("gy")
    kernel_call = functools.partial(call, vectors_count)
    x_pairs, y_pairs = pair_permutations(count_x, count_y)

    def swap(messages, pairs):
        odd = lax.ppermute(messages[1], AXES, pairs[1])
        return [lax.ppermute(messages[0], AXES, pairs[0]), odd]

    def share(row):
        return lax.all_to_all(row, AXES, 0, 0)

    rows = size_y + 2 * WIDE
    span = size_x + 2 * WIDE
    block = (size_x, size_y, size_z)
    row = pltpu.VMEM((count, 1, 2 * LANES), F32)
    stage = (2 * LANES, LANES)
    y_message = (size_x + size_x // WIDE + 2, WIDE, size_z)
    region = (span, rows, size_z)
    smooth_scratch = [region, region, (CHEB - 1,) + region, (size_x + 2, rows, size_z)]

    chunks = 8
    arguments = (right_side, deflation, velocity, inverse_rows)
    first_row, right_side, deflation, velocity, inverse_rows = kernel_call(
        first_kernel,
        [row] + [pltpu.VMEM(argument.shape, argument.dtype) for argument in arguments],
        [stage, pltpu.SemaphoreType.DMA((chunks + 3,))],
        *[pltpu.with_memory_space_constraint(argument, pltpu.HBM) for argument in arguments],
        micros=2.0,
        streamed=True,
    )
    first = share(first_row)
    faces_y = (3, size_x, WIDE, size_z)
    x_early = (WIDE + 1, size_y, size_z)
    x_early_first = (1 + EARLY_FIRST + 3 * WIDE, size_y, size_z)
    velocity_y = kernel_call(velocity_y_kernel, [faces_y] * 2, [], velocity, micros=0.01)
    after = velocity_y[0]
    velocity_y = swap(velocity_y, y_pairs)

    wide_own, wide_halo = (size_x, rows, size_z), (2 * WIDE, rows, size_z)

    def exchange(corr, rest, messages, corners, early_planes):
        tiles = WIDE + 2 + (3 * WIDE if corners else 0) + (WIDE - early_planes) * (size_y // 8)
        message = (tiles, 2 * WIDE, size_z)
        y_messages, early = swap(messages[:2], y_pairs), swap(messages[2:], x_pairs)
        *own, even, odd = kernel_call(
            functools.partial(extend_kernel, corners=corners, early_planes=early_planes),
            [wide_own, (2, rows, size_z), (2, size_x, size_z), message, message],
            [],
            rest,
            corr,
            *y_messages[::-1],
            velocity,
            *velocity_y,
            micros=0.01,
        )
        return (*own, *swap((even, odd), x_pairs)[::-1], *coefs, corr, *early[::-1])

    corr, rest, *messages = kernel_call(
        coarse_kernel,
        [block, block, y_message, y_message, x_early_first, x_early_first],
        [],
        first,
        inverse_rows,
        deflation,
        right_side,
        velocity,
        after,
        micros=1.4,
    )
    coefs = kernel_call(
        coefficients_kernel,
        [wide_own] * 5,
        [(3, size_x, rows, size_z)],
        velocity,
        *velocity_y,
        micros=0.01,
    )
    search, image, second_row, *halo_coefs = kernel_call(
        search_kernel,
        [block, block, row] + [wide_halo] * 4,
        [stage, (3, rows, size_z)] + smooth_scratch,
        *exchange(corr, rest, messages, True, EARLY_FIRST),
        deflation,
        right_side,
        micros=3.0,
    )
    second = share(second_row)
    corr, rest, middle, alpha, *messages = kernel_call(
        second_coarse_kernel,
        [block, block, block, (8, LANES), y_message, y_message, x_early, x_early],
        [],
        first,
        second,
        inverse_rows,
        deflation,
        right_side,
        image,
        velocity,
        micros=1.4,
    )
    smoothed, turned, third_row = kernel_call(
        smoothed_kernel,
        [block, block, row],
        smooth_scratch,
        *exchange(corr, rest, messages, False, WIDE),
        *halo_coefs,
        middle,
        micros=2.5,
    )
    third = share(third_row)
    return tuple(
        kernel_call(last_kernel, [block, block], [], third, alpha, search, smoothed, middle, turned, micros=1.4)
    )


def solution(mesh):
    return jax.shard_map(
        local,
        mesh=mesh,
        in_specs=(
            P("gx", "gy", None),
            P(None, "gx", "gy", None),
            P(None, "gx", "gy", None),
            P(("gx", "gy"), None),
        ),
        out_specs=(P("gx", "gy", None), P("gx", "gy", None)),
        check_vma=False,
    )
```

```python
import functools

import jax
import jax.numpy as jnp
from jax import lax
from jax.experimental import pallas as pl
from jax.experimental.pallas import tpu as pltpu
from jax.sharding import PartitionSpec as P

DEPTH = 2
CHEB = 4
WIDE = 4
EARLY_FIRST = 0
LANES = 128
AXES = ("gx", "gy")
F32 = jnp.float32
HIGHEST = lax.Precision.HIGHEST

cheb_center = 1.0
cheb_radius = 0.9

ODD_X, ODD_Y, LOW_X, HIGH_X, LOW_Y, HIGH_Y, SLOT = range(7)

def pair_permutations(count_x, count_y):
    def number(i, j):
        return i * count_y + j

    even_x, odd_x, even_y, odd_y = [], [], [], []
    for i in range(count_x):
        for j in range(count_y):
            here = number(i, j)
            even_x.append((here, number(i ^ 1, j)))
            even_y.append((here, number(i, j ^ 1)))
            other = ((i - 1) ^ 1) + 1
            odd_x.append((here, number(other, j) if 0 <= other < count_x else number(i, j ^ 1)))
            other = ((j - 1) ^ 1) + 1
            odd_y.append((here, number(i, other) if 0 <= other < count_y else number(i ^ 1, j)))
    return (even_x, odd_x), (even_y, odd_y)


def place_flags(vectors_count):
    count_x, count_y = lax.axis_size("gx"), lax.axis_size("gy")
    at_x, at_y = lax.axis_index("gx"), lax.axis_index("gy")
    return (
        lax.rem(at_x, 2),
        lax.rem(at_y, 2),
        (at_x > 0).astype(jnp.int32),
        (at_x < count_x - 1).astype(jnp.int32),
        (at_y > 0).astype(jnp.int32),
        (at_y < count_y - 1).astype(jnp.int32),
        lax.rem(at_x * count_y + at_y, LANES // vectors_count),
    )


def call(vectors, body, outs, scratch, *args, micros, streamed=False):
    def kernel(*refs):
        body(place_flags(vectors), *refs)

    return pl.pallas_call(
        kernel,
        out_shape=[jax.ShapeDtypeStruct(kind, F32) if isinstance(kind, tuple) else kind for kind in outs],
        in_specs=[pl.BlockSpec(memory_space=pltpu.HBM if streamed else pltpu.VMEM)] * len(args),
        out_specs=[pl.BlockSpec(memory_space=pltpu.VMEM)] * len(outs),
        scratch_shapes=[pltpu.VMEM(kind, F32) if isinstance(kind, tuple) else kind for kind in scratch],
        compiler_params=pltpu.CompilerParams(vmem_limit_bytes=24 * 1024 * 1024),
        cost_estimate=pl.CostEstimate(flops=0, bytes_accessed=int(micros * 3.6e6), transcendentals=0),
    )(*args)


def shift_z(plane, ahead):
    width = plane.shape[1]
    lane = lax.broadcasted_iota(jnp.int32, (plane.shape[0], LANES), 1)
    edge = LANES - 1 if ahead else 0
    turned = [pltpu.roll(plane[:, i : i + LANES], LANES - 1 if ahead else 1, 1) for i in range(0, width, LANES)]
    beside = turned[1:] + [0.0] if ahead else [0.0] + turned[:-1]
    return jnp.concatenate([jnp.where(lane == edge, far, near) for near, far in zip(turned, beside)], axis=1)


def restrict(vectors, fields, sums, flags, send, copies=()):
    count, size_x, size_y, size_z = vectors.shape
    out, stage = send
    stage[...] = jnp.zeros_like(stage)

    def lanes_of(total):
        total = jnp.sum(total, axis=0, keepdims=True)
        return functools.reduce(jnp.add, [total[:, k : k + LANES] for k in range(0, size_z, LANES)])

    offset = pl.multiple_of(flags[SLOT] * count, count)
    for j in range(count):
        if copies and j % (count // len(copies)) == 0:
            copies[j // (count // len(copies))].wait()
        totals = [0.0] * len(fields)
        for x in range(size_x):
            plane = vectors[j, x].astype(F32)
            totals = [total + plane * field[x] for total, field in zip(totals, fields)]
        for k, total in enumerate(totals):
            stage[pl.ds(k * LANES + offset + j, 1), :] = lanes_of(total)
    for k, total in enumerate(sums):
        stage[LANES + k : LANES + k + 1, :] = lanes_of(total)
    write_row(stage, out)


def write_row(stage, out):
    row = lax.dot_general(
        jnp.ones((8, LANES), F32), stage[...], (((1,), (1,)), ((), ())), precision=HIGHEST, preferred_element_type=F32
    )
    for k in range(out.shape[0]):
        out[k] = row[0:1]


def gathered(received, vectors, part=0):
    share = LANES // vectors.shape[0]
    return [
        functools.reduce(jnp.add, [received[k + i, :, part * LANES : (part + 1) * LANES] for i in range(share)])
        for k in range(0, received.shape[0], share)
    ]


def summed(received):
    return functools.reduce(jnp.add, [received[k, :, LANES:] for k in range(received.shape[0])])


def solve(coarse, inverse):
    total = inverse[:, :LANES] * coarse[0]
    for k in range(1, len(coarse)):
        total = total + inverse[:, k * LANES : (k + 1) * LANES] * coarse[k]
    return jnp.sum(total, axis=1, keepdims=True).astype(jnp.bfloat16).astype(F32)


def prolong(solved, vectors, corr):
    count, size_x, size_y, size_z = vectors.shape
    totals = [jnp.zeros((size_y, size_z), F32) for _ in range(size_x)]
    for j in range(count):
        weight = jnp.broadcast_to(solved[j : j + 1], (size_y, size_z))
        for x in range(size_x):
            totals[x] = totals[x] + vectors[j, x].astype(F32) * weight
    for x in range(size_x):
        corr[x] = totals[x]


def subtract_own(field, corr, velocity, out):
    size_x, size_y, size_z = corr.shape
    rows = lax.broadcasted_iota(jnp.int32, (size_y, size_z), 0)
    for x in range(size_x):
        v0, v1, v2 = velocity[0, x], velocity[1, x], velocity[2, x]
        here = corr[x]
        image = (6.0 + v0 + v1 + v2) * here
        if x + 1 < size_x:
            image = image - corr[x + 1]
        if x > 0:
            image = image - (1.0 + v0) * corr[x - 1]
        image = image - jnp.where(rows < size_y - 1, pltpu.roll(here, size_y - 1, 0), 0.0)
        image = image - (1.0 + v1) * jnp.where(rows > 0, pltpu.roll(here, 1, 0), 0.0)
        image = image - shift_z(here, True) - (1.0 + v2) * shift_z(here, False)
        out[x] = field[x] - image


def write_y_message(out, field, corr, high):
    size_x, size_y, _ = corr.shape
    start = size_y - WIDE if high else 0
    edge = size_y - 1 if high else 0
    for x in range(size_x):
        out[x] = field[x, start : start + WIDE, :]
        out[size_x + x // WIDE, x % WIDE : x % WIDE + 1, :] = corr[x, edge : edge + 1, :]
    last = size_x + size_x // WIDE
    out[last] = corr[0, start : start + WIDE, :]
    out[last + 1] = corr[size_x - 1, start : start + WIDE, :]


def by_parity(odd, write, even_out, odd_out):
    @pl.when(odd == 0)
    def _():
        write(even_out, True)
        write(odd_out, False)

    @pl.when(odd != 0)
    def _():
        write(even_out, False)
        write(odd_out, True)


def first_kernel(
    flags, field, vectors, velocity, inverse, out, held_field, held_vectors, held_velocity, held_inverse, stage, sems
):
    parts = sems.shape[0] - 3
    step = vectors.shape[0] // parts
    chunks = [pl.ds(part * step, step) for part in range(parts)]
    pairs = [(field, held_field)] + [(vectors.at[chunk], held_vectors.at[chunk]) for chunk in chunks]
    pairs += [(velocity, held_velocity), (inverse, held_inverse)]
    copies = [pltpu.make_async_copy(here, there, sems.at[k]) for k, (here, there) in enumerate(pairs)]
    for copy in copies:
        copy.start()
    copies[0].wait()
    rounded = [held_field[x].astype(jnp.bfloat16).astype(F32) for x in range(field.shape[0])]
    restrict(held_vectors, [rounded, held_field], [], flags, (out, stage), copies[1 : 1 + parts])
    for copy in copies[1 + parts :]:
        copy.wait()


def by_side(odd, use, *pairs):
    evens, odds = [pair[0] for pair in pairs], [pair[1] for pair in pairs]

    @pl.when(odd == 0)
    def _():
        use(odds, evens)

    @pl.when(odd != 0)
    def _():
        use(evens, odds)


def velocity_y_kernel(flags, velocity, even_out, odd_out):
    _, size_x, size_y, _ = velocity.shape

    def write_y(out, high):
        start = size_y - WIDE if high else 0
        for d in range(3):
            for x in range(size_x):
                out[d, x] = velocity[d, x, start : start + WIDE, :]

    by_parity(flags[ODD_Y], write_y, even_out, odd_out)


def write_x_early(flags, planes, rest, corr, velocity, even_out, odd_out):
    size_x = rest.shape[0]

    def write(out, high):
        start = size_x - WIDE if high else 0
        out[0] = corr[size_x - 1 if high else 0]
        for k in range(planes):
            out[1 + k] = rest[start + k]
        if velocity is not None:
            for d in range(3):
                for k in range(WIDE):
                    out[1 + planes + d * WIDE + k] = velocity[d, start + k]

    by_parity(flags[ODD_X], write, even_out, odd_out)


def coefficients(x, v0, v1, v2, kept, outs):
    inverse, b0, b1, b2 = outs
    total = 6.0 + v0 + v1 + v2
    value = jnp.where(kept, 1.0 / total, 0.0)
    inverse[x] = value
    b0[x] = value * (1.0 + v0)
    b1[x] = value * (1.0 + v1)
    b2[x] = value * (1.0 + v2)
    return total


def rows_in_grid(flags, shape):
    row = lax.broadcasted_iota(jnp.int32, shape, 0)
    first_row = jnp.where(flags[LOW_Y] != 0, 0, WIDE)
    end_row = jnp.where(flags[HIGH_Y] != 0, shape[0], shape[0] - WIDE)
    return (row >= first_row) & (row < end_row)


def coefficients_kernel(flags, velocity, even_in, odd_in, diagonal, inverse, b0, b1, b2, wide):
    _, size_x, size_y, size_z = velocity.shape
    rows = size_y + 2 * WIDE

    def place(low, high):
        for d in range(3):
            for x in range(size_x):
                wide[d, x, 0:WIDE, :] = low[d, x]
                wide[d, x, WIDE : WIDE + size_y, :] = velocity[d, x]
                wide[d, x, WIDE + size_y : rows, :] = high[d, x]

    @pl.when(flags[ODD_Y] == 0)
    def _():
        place(odd_in, even_in)

    @pl.when(flags[ODD_Y] != 0)
    def _():
        place(even_in, odd_in)

    kept = rows_in_grid(flags, (rows, size_z))
    for x in range(size_x):
        diagonal[x] = coefficients(x, wide[0, x], wide[1, x], wide[2, x], kept, (inverse, b0, b1, b2))


def halo_coefficients(flags, early, late, outs, wide):
    size_y, size_z = early[0].shape[1:]
    rows = size_y + 2 * WIDE
    kept = rows_in_grid(flags, (rows, size_z))

    def side(start, message, corners, present):
        for k in range(WIDE):
            for d in range(3):
                tile = WIDE + 2 + d * WIDE + k
                wide[d, 0:WIDE, :] = corners[tile, 0:WIDE, :]
                wide[d, WIDE : WIDE + size_y, :] = message[1 + EARLY_FIRST + d * WIDE + k]
                wide[d, WIDE + size_y : rows, :] = corners[tile, WIDE : 2 * WIDE, :]
            coefficients(start + k, wide[0], wide[1], wide[2], kept & (flags[present] != 0), outs)

    by_side(flags[ODD_X], lambda low, high: (side(0, *low, LOW_X), side(WIDE, *high, HIGH_X)), early, late)


class Region:
    def __init__(self, own, halo):
        self.own, self.halo = own, halo

    def __getitem__(self, index):
        x, tile = index if isinstance(index, tuple) else (index, slice(None))
        size_x = self.own.shape[0]
        if x < WIDE:
            return self.halo[x, tile]
        return self.own[x - WIDE, tile] if x < WIDE + size_x else self.halo[x - size_x, tile]


def coarse_kernel(
    flags, received, inverse, vectors, field, velocity, after, corr, rest, even_out, odd_out, even_x, odd_x
):
    prolong(solve(gathered(received, vectors), inverse), vectors, corr)
    subtract_own(field, corr, velocity, rest)
    by_parity(flags[ODD_Y], lambda out, high: write_y_message(out, rest, corr, high), even_out, odd_out)
    write_x_early(flags, EARLY_FIRST, rest, corr, velocity, even_x, odd_x)


def second_coarse_kernel(
    flags, received, second, inverse, vectors, field, image, velocity, corr, rest, middle, alpha, even_out, odd_out,
    even_x, odd_x
):
    products = summed(second)
    step = jnp.broadcast_to(products[:, 0:1] / products[:, 1:2], alpha.shape)
    alpha[...] = step
    step = step[0:1, 0:1]
    for x in range(field.shape[0]):
        middle[x] = field[x] - step * image[x]
    pairs = zip(gathered(received, vectors, 1), gathered(second, vectors))
    prolong(solve([coarse - step * of_image for coarse, of_image in pairs], inverse), vectors, corr)
    subtract_own(middle, corr, velocity, rest)
    by_parity(flags[ODD_Y], lambda out, high: write_y_message(out, rest, corr, high), even_out, odd_out)
    write_x_early(flags, WIDE, rest, corr, None, even_x, odd_x)


def extend_kernel(
    flags, rest, corr, odd_in, even_in, velocity, even_vel, odd_vel, wide, sides, past, even_out, odd_out, corners, early_planes
):
    size_x, size_y, size_z = rest.shape
    rows = size_y + 2 * WIDE
    end = WIDE + size_y

    def place(low, high, high_vel):
        has_low, has_high = flags[LOW_Y] != 0, flags[HIGH_Y] != 0
        for x in range(size_x):
            at, line = size_x + x // WIDE, slice(x % WIDE, x % WIDE + 1)
            past_low = jnp.where(has_low, low[at, line, :], 0.0)
            past_high = jnp.where(has_high, high[at, line, :], 0.0)
            past[0, x : x + 1, :] = past_low
            past[1, x : x + 1, :] = past_high
            wide[x, 0 : WIDE - 1, :] = low[x, 0 : WIDE - 1, :]
            wide[x, WIDE - 1 : WIDE, :] = low[x, WIDE - 1 : WIDE, :] + corr[x, 0:1, :]
            wide[x, WIDE:end, :] = rest[x]
            wide[x, WIDE : WIDE + 1, :] = rest[x, 0:1, :] + (1.0 + velocity[1, x, 0:1, :]) * past_low
            wide[x, end - 1 : end, :] = rest[x, size_y - 1 : size_y, :] + past_high
            weight = 1.0 + high_vel[1, x, 0:1, :]
            wide[x, end : end + 1, :] = high[x, 0:1, :] + weight * corr[x, size_y - 1 : size_y, :]
            wide[x, end + 1 : rows, :] = high[x, 1:WIDE, :]
        last = size_x + size_x // WIDE
        for side, x in enumerate((0, size_x - 1)):
            sides[side, 0:WIDE, :] = low[last + side]
            sides[side, WIDE:end, :] = corr[x]
            sides[side, end:rows, :] = high[last + side]

    @pl.when(flags[ODD_Y] == 0)
    def _():
        place(odd_in, even_in, even_vel)

    @pl.when(flags[ODD_Y] != 0)
    def _():
        place(even_in, odd_in, odd_vel)

    def write(out, high):
        start = size_x - WIDE if high else 0
        for k in range(WIDE):
            out[k, 0:WIDE, :] = wide[start + k, 0:WIDE, :]
            out[k, WIDE : 2 * WIDE, :] = wide[start + k, end:rows, :]
        side = 1 if high else 0
        out[WIDE, 0:WIDE, :] = sides[side, 0:WIDE, :]
        out[WIDE, WIDE : 2 * WIDE, :] = sides[side, end:rows, :]
        out[WIDE + 1, 0:WIDE, :] = past[0, start : start + WIDE, :]
        out[WIDE + 1, WIDE : 2 * WIDE, :] = past[1, start : start + WIDE, :]

        tile = WIDE + 2 + (3 * WIDE if corners else 0)
        for k in range(early_planes, WIDE):
            for row in range(0, size_y, 8):
                out[tile] = rest[start + k, row : row + 8, :]
                tile += 1

    by_parity(flags[ODD_X], write, even_out, odd_out)
    if not corners:
        return

    def write_corners(low, high):
        def write(out, upper):
            start = size_x - WIDE if upper else 0
            for d in range(3):
                for k in range(WIDE):
                    tile = WIDE + 2 + d * WIDE + k
                    out[tile, 0:WIDE, :] = low[0][d, start + k]
                    out[tile, WIDE : 2 * WIDE, :] = high[0][d, start + k]

        by_parity(flags[ODD_X], write, even_out, odd_out)

    by_side(flags[ODD_Y], write_corners, (even_vel, odd_vel))


def ready_kernel(flags, wide, inverse, corr, source, placed):
    size_x, size_y, size_z = corr.shape
    for k in range(size_x):
        source[k] = inverse[k] * wide[k]
        placed[k] = jnp.zeros(placed.shape[1:], F32)
        placed[k, WIDE : WIDE + size_y, :] = corr[k]


def beside_terms(before, here, after, x, tile, coefs):
    inverse, b0, b1, b2 = coefs
    rows = here.shape[0]
    ahead = pltpu.roll(here, rows - 1, 0) + shift_z(here, True)
    if after is not None:
        ahead = ahead + after
    total = inverse[x, tile] * ahead + b1[x, tile] * pltpu.roll(here, 1, 0) + b2[x, tile] * shift_z(here, False)
    if before is not None:
        total = total + b0[x, tile] * before
    return total


def chebyshev(planes, tile, inside, source, left, update, coefs, wanted):
    sigma = cheb_center / cheb_radius
    rho = 1.0 / sigma
    first, last = planes[0], planes[-1]
    for x in planes:
        update[0, x, tile] = jnp.where(inside, source(x), 0.0)
    estimate = {}
    for sweep in range(1, CHEB):
        rest = CHEB - 1 - sweep
        low, high = max(first, wanted[0] - rest), min(last, wanted[-1] + rest)
        rho_next = 1.0 / (2.0 * sigma - rho)
        for x in range(low, high + 1):
            here = update[sweep - 1, x, tile]
            before = update[sweep - 1, x - 1, tile] if x > first else None
            after = update[sweep - 1, x + 1, tile] if x < last else None
            remainder = beside_terms(before, here, after, x, tile, coefs)
            if sweep > 1:
                remainder = remainder + (left[x, tile] - here)
            if rest:
                left[x, tile] = remainder
            value = rho_next * rho * here + (2.0 * rho_next / cheb_radius) * jnp.where(inside, remainder, 0.0)
            if rest:
                update[sweep, x, tile] = value
            else:
                for k in range(CHEB - 1):
                    value = value + update[k, x, tile]
                estimate[x] = value
        rho = rho_next
    return estimate


def smooth(
    flags, early_planes, wide, sides, past, early, late, diagonal, coefs, corr, field_out, image_out, scratch
):
    source, left, update, whole = scratch
    inverse, b0, b1, _ = coefs
    size_x, rows, size_z = corr.shape
    size_y = rows - 2 * WIDE
    span = size_x + 2 * WIDE
    row = lax.broadcasted_iota(jnp.int32, (rows, size_z), 0)
    has_low_x, has_high_x = flags[LOW_X] != 0, flags[HIGH_X] != 0
    has_low_y, has_high_y = flags[LOW_Y] != 0, flags[HIGH_Y] != 0
    lowest, highest = slice(0, 8), slice(rows - 8, rows)
    tile_row = lax.broadcasted_iota(jnp.int32, (8, size_z), 0)
    end = WIDE + size_y

    def put(out, x, middle, ends):
        out[x, 0:WIDE, :] = ends[0:WIDE, :]
        for row_ in range(0, size_y, 8):
            out[x, WIDE + row_ : WIDE + row_ + 8, :] = middle(row_)
        out[x, end:rows, :] = ends[WIDE : 2 * WIDE, :]

    def halo(side, first, edge, present):
        message, ends = side
        for k in range(WIDE):
            x = first + k
            if k < early_planes:
                middle = lambda row_: message[1 + k, row_ : row_ + 8, :]
            else:
                tile = ends.shape[0] - (WIDE - k) * (size_y // 8)
                middle = lambda row_: ends[tile + row_ // 8]
            put(source, x, middle, ends.at[k])
            source[x] = inverse[x] * source[x]
            for row_, weight, line in ((WIDE, b1, k), (end - 1, inverse, WIDE + k)):
                at = slice(row_, row_ + 1)
                source[x, at] = source[x, at] + weight[x, at] * ends[WIDE + 1, line : line + 1, :]
        put(whole, edge, lambda row_: message[0, row_ : row_ + 8, :], ends.at[WIDE])
        whole[edge] = jnp.where(present, whole[edge], 0.0)

    def halos(low, high):
        halo(low, 0, 0, has_low_x)
        halo(high, WIDE + size_x, size_x + 1, has_high_x)

    by_side(flags[ODD_X], halos, early, late)

    for k in range(size_x):
        source[WIDE + k] = wide[k]

    low_in, high_in = WIDE, WIDE + size_x - 1
    source[low_in - 1] = source[low_in - 1] + inverse[low_in - 1] * sides[0]
    source[low_in] = source[low_in] + b0[low_in] * whole[0]
    source[high_in] = source[high_in] + inverse[high_in] * whole[size_x + 1]
    source[high_in + 1] = source[high_in + 1] + b0[high_in + 1] * sides[1]

    def run(planes, tile, inside, wanted):
        return chebyshev(
            planes,
            tile,
            inside,
            lambda x: source[x, tile],
            left,
            update,
            coefs,
            wanted,
        )

    everything = slice(0, rows)
    box_rows = (row >= WIDE - DEPTH) & (row < WIDE + size_y + DEPTH)
    box_planes = range(WIDE - DEPTH, WIDE + size_x + DEPTH)
    own_planes = range(WIDE, WIDE + size_x)
    inner = (row >= WIDE) & (row < WIDE + size_y)

    beside = run(range(0, WIDE + DEPTH), everything, box_rows, (WIDE - 1,))[WIDE - 1]
    whole[0] = jnp.where(has_low_x & inner, whole[0] + beside, 0.0)
    x = WIDE + size_x
    beside = run(range(span - WIDE - DEPTH, span), everything, box_rows, (x,))[x]
    whole[size_x + 1] = jnp.where(has_high_x & inner, whole[size_x + 1] + beside, 0.0)

    own = run(box_planes, everything, box_rows, tuple(own_planes))
    for k in range(size_x):
        whole[k + 1] = jnp.where(inner, corr[k] + own[WIDE + k], 0.0)

    beside = run(box_planes, lowest, tile_row < WIDE + DEPTH, tuple(own_planes))
    for k in range(size_x):
        line = past[0, k : k + 1, :] + beside[WIDE + k]
        here = has_low_y & (tile_row == WIDE - 1)
        whole[k + 1, lowest] = jnp.where(here, line, whole[k + 1, lowest])
    beside = run(box_planes, highest, tile_row >= 8 - WIDE - DEPTH, tuple(own_planes))
    for k in range(size_x):
        line = past[1, k : k + 1, :] + beside[WIDE + k]
        here = has_high_y & (tile_row == 8 - WIDE)
        whole[k + 1, highest] = jnp.where(here, line, whole[k + 1, highest])

    for k in range(size_x):
        x = WIDE + k
        terms = beside_terms(whole[k], whole[k + 1], whole[k + 2], x, everything, coefs)
        image = diagonal[k] * (whole[k + 1] - terms)
        image_out[k] = pltpu.roll(image, rows - WIDE, 0)[0:size_y]
        field_out[k] = pltpu.roll(whole[k + 1], rows - WIDE, 0)[0:size_y]


def dot_planes(left, right):
    total = left[0] * right[0]
    for x in range(1, left.shape[0]):
        total = total + left[x] * right[x]
    return total


def search_kernel(
    flags, wide, sides, past, odd_late, even_late, diagonal, own0, own1, own2, own3, corr, odd_early, even_early, vectors,
    right_side, search, image, out, halo0, halo1, halo2, halo3, stage, wide_vel, *scratch
):
    halos = (halo0, halo1, halo2, halo3)
    early, late = (even_early, odd_early), (even_late, odd_late)
    halo_coefficients(flags, early, late, halos, wide_vel)
    coefs = [Region(*pair) for pair in zip((own0, own1, own2, own3), halos)]
    smooth(flags, EARLY_FIRST, wide, sides, past, early, late, diagonal, coefs, corr, search, image, scratch)
    products = [dot_planes(right_side, right_side), dot_planes(right_side, image)]
    restrict(vectors, [image], products, flags, (out, stage))


def smoothed_kernel(
    flags, wide, sides, past, odd_late, even_late, diagonal, own0, own1, own2, own3, corr, odd_early, even_early, halo0,
    halo1, halo2, halo3, middle, smoothed, turned, out, *scratch
):
    early, late = (even_early, odd_early), (even_late, odd_late)
    coefs = [Region(*pair) for pair in zip((own0, own1, own2, own3), (halo0, halo1, halo2, halo3))]
    smooth(flags, WIDE, wide, sides, past, early, late, diagonal, coefs, corr, smoothed, turned, scratch)
    lane = lax.broadcasted_iota(jnp.int32, (1, LANES), 1)
    sums = jnp.zeros((1, LANES), F32)
    for k, total in enumerate((dot_planes(turned, middle), dot_planes(turned, turned))):
        total = jnp.sum(jnp.sum(total, axis=0, keepdims=True), axis=1, keepdims=True)
        sums = jnp.where(lane == k, total, sums)
    row = jnp.concatenate([jnp.zeros((1, LANES), F32), sums], axis=1)
    for k in range(out.shape[0]):
        out[k] = row


def last_kernel(flags, received, alpha, search, smoothed, middle, turned, solution_field, residual):
    sums = summed(received)
    omega = sums[:, 0:1] / sums[:, 1:2]
    step = alpha[0:1, 0:1]
    for x in range(search.shape[0]):
        solution_field[x] = step * search[x] + omega * smoothed[x]
        residual[x] = middle[x] - omega * turned[x]


def local(right_side, velocity, deflation, inverse_rows):
    size_x, size_y, size_z = right_side.shape
    vectors_count = deflation.shape[0]
    count_x, count_y = lax.axis_size("gx"), lax.axis_size("gy")
    count = count_x * count_y
    at_x, at_y = lax.axis_index("gx"), lax.axis_index("gy")
    kernel_call = functools.partial(call, vectors_count)
    x_pairs, y_pairs = pair_permutations(count_x, count_y)

    def swap(messages, pairs):
        odd = lax.ppermute(messages[1], AXES, pairs[1])
        return [lax.ppermute(messages[0], AXES, pairs[0]), odd]

    def share(row):
        return lax.all_to_all(row, AXES, 0, 0)

    rows = size_y + 2 * WIDE
    span = size_x + 2 * WIDE
    block = (size_x, size_y, size_z)
    row = pltpu.VMEM((count, 1, 2 * LANES), F32)
    stage = (2 * LANES, LANES)
    y_message = (size_x + size_x // WIDE + 2, WIDE, size_z)
    region = (span, rows, size_z)
    smooth_scratch = [region, region, (CHEB - 1,) + region, (size_x + 2, rows, size_z)]

    chunks = 8
    arguments = (right_side, deflation, velocity, inverse_rows)
    first_row, right_side, deflation, velocity, inverse_rows = kernel_call(
        first_kernel,
        [row] + [pltpu.VMEM(argument.shape, argument.dtype) for argument in arguments],
        [stage, pltpu.SemaphoreType.DMA((chunks + 3,))],
        *[pltpu.with_memory_space_constraint(argument, pltpu.HBM) for argument in arguments],
        micros=2.0,
        streamed=True,
    )
    first = share(first_row)
    faces_y = (3, size_x, WIDE, size_z)
    x_early = (WIDE + 1, size_y, size_z)
    x_early_first = (1 + EARLY_FIRST + 3 * WIDE, size_y, size_z)
    velocity_y = kernel_call(velocity_y_kernel, [faces_y] * 2, [], velocity, micros=0.01)
    after = velocity_y[0]
    velocity_y = swap(velocity_y, y_pairs)

    wide_own, wide_halo = (size_x, rows, size_z), (2 * WIDE, rows, size_z)

    def exchange(corr, rest, messages, corners, early_planes):
        tiles = WIDE + 2 + (3 * WIDE if corners else 0) + (WIDE - early_planes) * (size_y // 8)
        message = (tiles, 2 * WIDE, size_z)
        y_messages, early = swap(messages[:2], y_pairs), swap(messages[2:], x_pairs)
        *own, even, odd = kernel_call(
            functools.partial(extend_kernel, corners=corners, early_planes=early_planes),
            [wide_own, (2, rows, size_z), (2, size_x, size_z), message, message],
            [],
            rest,
            corr,
            *y_messages[::-1],
            velocity,
            *velocity_y,
            micros=0.01,
        )
        wide, *rest_own = own
        source, placed = kernel_call(ready_kernel, [wide_own] * 2, [], wide, coefs[1], corr, micros=0.01)
        return (source, *rest_own, *swap((even, odd), x_pairs)[::-1], *coefs, placed, *early[::-1])

    corr, rest, *messages = kernel_call(
        coarse_kernel,
        [block, block, y_message, y_message, x_early_first, x_early_first],
        [],
        first,
        inverse_rows,
        deflation,
        right_side,
        velocity,
        after,
        micros=1.4,
    )
    coefs = kernel_call(
        coefficients_kernel,
        [wide_own] * 5,
        [(3, size_x, rows, size_z)],
        velocity,
        *velocity_y,
        micros=0.01,
    )
    search, image, second_row, *halo_coefs = kernel_call(
        search_kernel,
        [block, block, row] + [wide_halo] * 4,
        [stage, (3, rows, size_z)] + smooth_scratch,
        *exchange(corr, rest, messages, True, EARLY_FIRST),
        deflation,
        right_side,
        micros=3.0,
    )
    second = share(second_row)
    corr, rest, middle, alpha, *messages = kernel_call(
        second_coarse_kernel,
        [block, block, block, (8, LANES), y_message, y_message, x_early, x_early],
        [],
        first,
        second,
        inverse_rows,
        deflation,
        right_side,
        image,
        velocity,
        micros=1.4,
    )
    smoothed, turned, third_row = kernel_call(
        smoothed_kernel,
        [block, block, row],
        smooth_scratch,
        *exchange(corr, rest, messages, False, WIDE),
        *halo_coefs,
        middle,
        micros=2.5,
    )
    third = share(third_row)
    return tuple(
        kernel_call(last_kernel, [block, block], [], third, alpha, search, smoothed, middle, turned, micros=1.4)
    )


def solution(mesh):
    return jax.shard_map(
        local,
        mesh=mesh,
        in_specs=(
            P("gx", "gy", None),
            P(None, "gx", "gy", None),
            P(None, "gx", "gy", None),
            P(("gx", "gy"), None),
        ),
        out_specs=(P("gx", "gy", None), P("gx", "gy", None)),
        check_vma=False,
    )
```

```python
import functools

import jax
import jax.numpy as jnp
from jax import lax
from jax.experimental import pallas as pl
from jax.experimental.pallas import tpu as pltpu
from jax.sharding import PartitionSpec as P

DEPTH = 2
CHEB = 4
WIDE = 4
EARLY_FIRST = 0
LANES = 128
AXES = ("gx", "gy")
F32 = jnp.float32
HIGHEST = lax.Precision.HIGHEST

cheb_center = 1.0
cheb_radius = 0.9

ODD_X, ODD_Y, LOW_X, HIGH_X, LOW_Y, HIGH_Y, SLOT = range(7)

def pair_permutations(count_x, count_y):
    def number(i, j):
        return i * count_y + j

    even_x, odd_x, even_y, odd_y = [], [], [], []
    for i in range(count_x):
        for j in range(count_y):
            here = number(i, j)
            even_x.append((here, number(i ^ 1, j)))
            even_y.append((here, number(i, j ^ 1)))
            other = ((i - 1) ^ 1) + 1
            odd_x.append((here, number(other, j) if 0 <= other < count_x else number(i, j ^ 1)))
            other = ((j - 1) ^ 1) + 1
            odd_y.append((here, number(i, other) if 0 <= other < count_y else number(i ^ 1, j)))
    return (even_x, odd_x), (even_y, odd_y)


def place_flags(vectors_count):
    count_x, count_y = lax.axis_size("gx"), lax.axis_size("gy")
    at_x, at_y = lax.axis_index("gx"), lax.axis_index("gy")
    return (
        lax.rem(at_x, 2),
        lax.rem(at_y, 2),
        (at_x > 0).astype(jnp.int32),
        (at_x < count_x - 1).astype(jnp.int32),
        (at_y > 0).astype(jnp.int32),
        (at_y < count_y - 1).astype(jnp.int32),
        lax.rem(at_x * count_y + at_y, LANES // vectors_count),
    )


def call(vectors, body, outs, scratch, *args, micros, streamed=False):
    def kernel(*refs):
        body(place_flags(vectors), *refs)

    return pl.pallas_call(
        kernel,
        out_shape=[jax.ShapeDtypeStruct(kind, F32) if isinstance(kind, tuple) else kind for kind in outs],
        in_specs=[pl.BlockSpec(memory_space=pltpu.HBM if streamed else pltpu.VMEM)] * len(args),
        out_specs=[pl.BlockSpec(memory_space=pltpu.VMEM)] * len(outs),
        scratch_shapes=[pltpu.VMEM(kind, F32) if isinstance(kind, tuple) else kind for kind in scratch],
        compiler_params=pltpu.CompilerParams(vmem_limit_bytes=24 * 1024 * 1024),
        cost_estimate=pl.CostEstimate(flops=0, bytes_accessed=int(micros * 3.6e6), transcendentals=0),
    )(*args)


def shift_z(plane, ahead):
    width = plane.shape[1]
    lane = lax.broadcasted_iota(jnp.int32, (plane.shape[0], LANES), 1)
    edge = LANES - 1 if ahead else 0
    turned = [pltpu.roll(plane[:, i : i + LANES], LANES - 1 if ahead else 1, 1) for i in range(0, width, LANES)]
    beside = turned[1:] + [0.0] if ahead else [0.0] + turned[:-1]
    return jnp.concatenate([jnp.where(lane == edge, far, near) for near, far in zip(turned, beside)], axis=1)


def restrict(vectors, fields, sums, flags, send, copies=()):
    count, size_x, size_y, size_z = vectors.shape
    out, stage = send
    stage[...] = jnp.zeros_like(stage)

    def lanes_of(total):
        total = jnp.sum(total, axis=0, keepdims=True)
        return functools.reduce(jnp.add, [total[:, k : k + LANES] for k in range(0, size_z, LANES)])

    offset = pl.multiple_of(flags[SLOT] * count, count)
    for j in range(count):
        if copies and j % (count // len(copies)) == 0:
            copies[j // (count // len(copies))].wait()
        totals = [0.0] * len(fields)
        for x in range(size_x):
            plane = vectors[j, x].astype(F32)
            totals = [total + plane * field[x] for total, field in zip(totals, fields)]
        for k, total in enumerate(totals):
            stage[pl.ds(k * LANES + offset + j, 1), :] = lanes_of(total)
    for k, total in enumerate(sums):
        stage[LANES + k : LANES + k + 1, :] = lanes_of(total)
    write_row(stage, out)


def write_row(stage, out):
    row = lax.dot_general(
        jnp.ones((8, LANES), F32), stage[...], (((1,), (1,)), ((), ())), precision=HIGHEST, preferred_element_type=F32
    )
    for k in range(out.shape[0]):
        out[k] = row[0:1]


def gathered(received, vectors, part=0):
    share = LANES // vectors.shape[0]
    return [
        functools.reduce(jnp.add, [received[k + i, :, part * LANES : (part + 1) * LANES] for i in range(share)])
        for k in range(0, received.shape[0], share)
    ]


def summed(received):
    return functools.reduce(jnp.add, [received[k, :, LANES:] for k in range(received.shape[0])])


def solve(coarse, inverse):
    total = inverse[:, :LANES] * coarse[0]
    for k in range(1, len(coarse)):
        total = total + inverse[:, k * LANES : (k + 1) * LANES] * coarse[k]
    return jnp.sum(total, axis=1, keepdims=True).astype(jnp.bfloat16).astype(F32)


def prolong(solved, vectors, corr):
    count, size_x, size_y, size_z = vectors.shape
    totals = [jnp.zeros((size_y, size_z), F32) for _ in range(size_x)]
    for j in range(count):
        weight = jnp.broadcast_to(solved[j : j + 1], (size_y, size_z))
        for x in range(size_x):
            totals[x] = totals[x] + vectors[j, x].astype(F32) * weight
    for x in range(size_x):
        corr[x] = totals[x]


def subtract_own(field, corr, velocity, out):
    size_x, size_y, size_z = corr.shape
    rows = lax.broadcasted_iota(jnp.int32, (size_y, size_z), 0)
    for x in range(size_x):
        v0, v1, v2 = velocity[0, x], velocity[1, x], velocity[2, x]
        here = corr[x]
        image = (6.0 + v0 + v1 + v2) * here
        if x + 1 < size_x:
            image = image - corr[x + 1]
        if x > 0:
            image = image - (1.0 + v0) * corr[x - 1]
        image = image - jnp.where(rows < size_y - 1, pltpu.roll(here, size_y - 1, 0), 0.0)
        image = image - (1.0 + v1) * jnp.where(rows > 0, pltpu.roll(here, 1, 0), 0.0)
        image = image - shift_z(here, True) - (1.0 + v2) * shift_z(here, False)
        out[x] = field[x] - image


def write_y_message(out, field, corr, high):
    size_x, size_y, _ = corr.shape
    start = size_y - WIDE if high else 0
    edge = size_y - 1 if high else 0
    for x in range(size_x):
        out[x] = field[x, start : start + WIDE, :]
        out[size_x + x // WIDE, x % WIDE : x % WIDE + 1, :] = corr[x, edge : edge + 1, :]
    last = size_x + size_x // WIDE
    out[last] = corr[0, start : start + WIDE, :]
    out[last + 1] = corr[size_x - 1, start : start + WIDE, :]


def by_parity(odd, write, even_out, odd_out):
    @pl.when(odd == 0)
    def _():
        write(even_out, True)
        write(odd_out, False)

    @pl.when(odd != 0)
    def _():
        write(even_out, False)
        write(odd_out, True)


def first_kernel(
    flags, field, vectors, velocity, inverse, out, held_field, held_vectors, held_velocity, held_inverse, stage, sems
):
    parts = sems.shape[0] - 3
    step = vectors.shape[0] // parts
    chunks = [pl.ds(part * step, step) for part in range(parts)]
    pairs = [(field, held_field)] + [(vectors.at[chunk], held_vectors.at[chunk]) for chunk in chunks]
    pairs += [(velocity, held_velocity), (inverse, held_inverse)]
    copies = [pltpu.make_async_copy(here, there, sems.at[k]) for k, (here, there) in enumerate(pairs)]
    for copy in copies:
        copy.start()
    copies[0].wait()
    rounded = [held_field[x].astype(jnp.bfloat16).astype(F32) for x in range(field.shape[0])]
    restrict(held_vectors, [rounded, held_field], [], flags, (out, stage), copies[1 : 1 + parts])
    for copy in copies[1 + parts :]:
        copy.wait()


def by_side(odd, use, *pairs):
    evens, odds = [pair[0] for pair in pairs], [pair[1] for pair in pairs]

    @pl.when(odd == 0)
    def _():
        use(odds, evens)

    @pl.when(odd != 0)
    def _():
        use(evens, odds)


def velocity_y_kernel(flags, velocity, even_out, odd_out):
    _, size_x, size_y, _ = velocity.shape

    def write_y(out, high):
        start = size_y - WIDE if high else 0
        for d in range(3):
            for x in range(size_x):
                out[d, x] = velocity[d, x, start : start + WIDE, :]

    by_parity(flags[ODD_Y], write_y, even_out, odd_out)


def write_x_early(flags, planes, rest, corr, velocity, even_out, odd_out):
    size_x = rest.shape[0]

    def write(out, high):
        start = size_x - WIDE if high else 0
        out[0] = corr[size_x - 1 if high else 0]
        for k in range(planes):
            out[1 + k] = rest[start + k]
        if velocity is not None:
            for d in range(3):
                for k in range(WIDE):
                    out[1 + planes + d * WIDE + k] = velocity[d, start + k]

    by_parity(flags[ODD_X], write, even_out, odd_out)


def coefficients(x, v0, v1, v2, kept, outs):
    inverse, b0, b1, b2 = outs
    total = 6.0 + v0 + v1 + v2
    value = jnp.where(kept, 1.0 / total, 0.0)
    inverse[x] = value
    b0[x] = value * (1.0 + v0)
    b1[x] = value * (1.0 + v1)
    b2[x] = value * (1.0 + v2)
    return total


def rows_in_grid(flags, shape):
    row = lax.broadcasted_iota(jnp.int32, shape, 0)
    first_row = jnp.where(flags[LOW_Y] != 0, 0, WIDE)
    end_row = jnp.where(flags[HIGH_Y] != 0, shape[0], shape[0] - WIDE)
    return (row >= first_row) & (row < end_row)


def coefficients_kernel(flags, velocity, even_in, odd_in, diagonal, inverse, b0, b1, b2, wide):
    _, size_x, size_y, size_z = velocity.shape
    rows = size_y + 2 * WIDE

    def place(low, high):
        for d in range(3):
            for x in range(size_x):
                wide[d, x, 0:WIDE, :] = low[d, x]
                wide[d, x, WIDE : WIDE + size_y, :] = velocity[d, x]
                wide[d, x, WIDE + size_y : rows, :] = high[d, x]

    @pl.when(flags[ODD_Y] == 0)
    def _():
        place(odd_in, even_in)

    @pl.when(flags[ODD_Y] != 0)
    def _():
        place(even_in, odd_in)

    kept = rows_in_grid(flags, (rows, size_z))
    for x in range(size_x):
        diagonal[x] = coefficients(x, wide[0, x], wide[1, x], wide[2, x], kept, (inverse, b0, b1, b2))


def halo_coefficients(flags, early, late, outs, wide):
    size_y, size_z = early[0].shape[1:]
    rows = size_y + 2 * WIDE
    kept = rows_in_grid(flags, (rows, size_z))

    def side(start, message, corners, present):
        for k in range(WIDE):
            for d in range(3):
                tile = WIDE + 2 + d * WIDE + k
                wide[d, 0:WIDE, :] = corners[tile, 0:WIDE, :]
                wide[d, WIDE : WIDE + size_y, :] = message[1 + EARLY_FIRST + d * WIDE + k]
                wide[d, WIDE + size_y : rows, :] = corners[tile, WIDE : 2 * WIDE, :]
            coefficients(start + k, wide[0], wide[1], wide[2], kept & (flags[present] != 0), outs)

    by_side(flags[ODD_X], lambda low, high: (side(0, *low, LOW_X), side(WIDE, *high, HIGH_X)), early, late)


class Region:
    def __init__(self, own, halo):
        self.own, self.halo = own, halo

    def __getitem__(self, index):
        x, tile = index if isinstance(index, tuple) else (index, slice(None))
        size_x = self.own.shape[0]
        if x < WIDE:
            return self.halo[x, tile]
        return self.own[x - WIDE, tile] if x < WIDE + size_x else self.halo[x - size_x, tile]


def coarse_kernel(
    flags, received, inverse, vectors, field, velocity, after, corr, rest, even_out, odd_out, even_x, odd_x
):
    prolong(solve(gathered(received, vectors), inverse), vectors, corr)
    subtract_own(field, corr, velocity, rest)
    by_parity(flags[ODD_Y], lambda out, high: write_y_message(out, rest, corr, high), even_out, odd_out)
    write_x_early(flags, EARLY_FIRST, rest, corr, velocity, even_x, odd_x)


def second_coarse_kernel(
    flags, received, second, inverse, vectors, field, image, velocity, corr, rest, middle, alpha, even_out, odd_out,
    even_x, odd_x
):
    products = summed(second)
    step = jnp.broadcast_to(products[:, 0:1] / products[:, 1:2], alpha.shape)
    alpha[...] = step
    step = step[0:1, 0:1]
    for x in range(field.shape[0]):
        middle[x] = field[x] - step * image[x]
    pairs = zip(gathered(received, vectors, 1), gathered(second, vectors))
    prolong(solve([coarse - step * of_image for coarse, of_image in pairs], inverse), vectors, corr)
    subtract_own(middle, corr, velocity, rest)
    by_parity(flags[ODD_Y], lambda out, high: write_y_message(out, rest, corr, high), even_out, odd_out)
    write_x_early(flags, WIDE, rest, corr, None, even_x, odd_x)


def extend_kernel(
    flags, rest, corr, odd_in, even_in, velocity, even_vel, odd_vel, wide, sides, past, even_out, odd_out, corners, early_planes
):
    size_x, size_y, size_z = rest.shape
    rows = size_y + 2 * WIDE
    end = WIDE + size_y

    def place(low, high, high_vel):
        has_low, has_high = flags[LOW_Y] != 0, flags[HIGH_Y] != 0
        for x in range(size_x):
            at, line = size_x + x // WIDE, slice(x % WIDE, x % WIDE + 1)
            past_low = jnp.where(has_low, low[at, line, :], 0.0)
            past_high = jnp.where(has_high, high[at, line, :], 0.0)
            past[0, x : x + 1, :] = past_low
            past[1, x : x + 1, :] = past_high
            wide[x, 0 : WIDE - 1, :] = low[x, 0 : WIDE - 1, :]
            wide[x, WIDE - 1 : WIDE, :] = low[x, WIDE - 1 : WIDE, :] + corr[x, 0:1, :]
            wide[x, WIDE:end, :] = rest[x]
            wide[x, WIDE : WIDE + 1, :] = rest[x, 0:1, :] + (1.0 + velocity[1, x, 0:1, :]) * past_low
            wide[x, end - 1 : end, :] = rest[x, size_y - 1 : size_y, :] + past_high
            weight = 1.0 + high_vel[1, x, 0:1, :]
            wide[x, end : end + 1, :] = high[x, 0:1, :] + weight * corr[x, size_y - 1 : size_y, :]
            wide[x, end + 1 : rows, :] = high[x, 1:WIDE, :]
        last = size_x + size_x // WIDE
        for side, x in enumerate((0, size_x - 1)):
            sides[side, 0:WIDE, :] = low[last + side]
            sides[side, WIDE:end, :] = corr[x]
            sides[side, end:rows, :] = high[last + side]

    @pl.when(flags[ODD_Y] == 0)
    def _():
        place(odd_in, even_in, even_vel)

    @pl.when(flags[ODD_Y] != 0)
    def _():
        place(even_in, odd_in, odd_vel)

    def write(out, high):
        start = size_x - WIDE if high else 0
        for k in range(WIDE):
            out[k, 0:WIDE, :] = wide[start + k, 0:WIDE, :]
            out[k, WIDE : 2 * WIDE, :] = wide[start + k, end:rows, :]
        side = 1 if high else 0
        out[WIDE, 0:WIDE, :] = sides[side, 0:WIDE, :]
        out[WIDE, WIDE : 2 * WIDE, :] = sides[side, end:rows, :]
        out[WIDE + 1, 0:WIDE, :] = past[0, start : start + WIDE, :]
        out[WIDE + 1, WIDE : 2 * WIDE, :] = past[1, start : start + WIDE, :]

        tile = WIDE + 2 + (3 * WIDE if corners else 0)
        for k in range(early_planes, WIDE):
            for row in range(0, size_y, 8):
                out[tile] = rest[start + k, row : row + 8, :]
                tile += 1

    by_parity(flags[ODD_X], write, even_out, odd_out)
    if not corners:
        return

    def write_corners(low, high):
        def write(out, upper):
            start = size_x - WIDE if upper else 0
            for d in range(3):
                for k in range(WIDE):
                    tile = WIDE + 2 + d * WIDE + k
                    out[tile, 0:WIDE, :] = low[0][d, start + k]
                    out[tile, WIDE : 2 * WIDE, :] = high[0][d, start + k]

        by_parity(flags[ODD_X], write, even_out, odd_out)

    by_side(flags[ODD_Y], write_corners, (even_vel, odd_vel))


def ready_kernel(flags, wide, inverse, corr, source, placed):
    size_x, size_y, size_z = corr.shape
    for k in range(size_x):
        source[k] = inverse[k] * wide[k]
        placed[k] = jnp.zeros(placed.shape[1:], F32)
        placed[k, WIDE : WIDE + size_y, :] = corr[k]


def beside_terms(before, here, after, x, tile, coefs):
    inverse, b0, b1, b2 = coefs
    rows = here.shape[0]
    ahead = pltpu.roll(here, rows - 1, 0) + shift_z(here, True)
    if after is not None:
        ahead = ahead + after
    total = inverse[x, tile] * ahead + b1[x, tile] * pltpu.roll(here, 1, 0) + b2[x, tile] * shift_z(here, False)
    if before is not None:
        total = total + b0[x, tile] * before
    return total


def chebyshev(planes, tile, inside, source, left, update, coefs, wanted):
    sigma = cheb_center / cheb_radius
    rho = 1.0 / sigma
    first, last = planes[0], planes[-1]
    for x in planes:
        update[0, x, tile] = jnp.where(inside, source(x), 0.0)
    estimate = {}
    for sweep in range(1, CHEB):
        rest = CHEB - 1 - sweep
        low, high = max(first, wanted[0] - rest), min(last, wanted[-1] + rest)
        rho_next = 1.0 / (2.0 * sigma - rho)
        for x in range(low, high + 1):
            here = update[sweep - 1, x, tile]
            before = update[sweep - 1, x - 1, tile] if x > first else None
            after = update[sweep - 1, x + 1, tile] if x < last else None
            remainder = beside_terms(before, here, after, x, tile, coefs)
            if sweep > 1:
                remainder = remainder + (left[x, tile] - here)
            if rest:
                left[x, tile] = remainder
            value = rho_next * rho * here + (2.0 * rho_next / cheb_radius) * jnp.where(inside, remainder, 0.0)
            if rest:
                update[sweep, x, tile] = value
            else:
                for k in range(CHEB - 1):
                    value = value + update[k, x, tile]
                estimate[x] = value
        rho = rho_next
    return estimate


def smooth(
    flags, early_planes, wide, sides, past, early, late, diagonal, coefs, corr, field_out, image_out, scratch
):
    source, left, update, whole = scratch
    inverse, b0, b1, _ = coefs
    size_x, rows, size_z = corr.shape
    size_y = rows - 2 * WIDE
    span = size_x + 2 * WIDE
    row = lax.broadcasted_iota(jnp.int32, (rows, size_z), 0)
    has_low_x, has_high_x = flags[LOW_X] != 0, flags[HIGH_X] != 0
    has_low_y, has_high_y = flags[LOW_Y] != 0, flags[HIGH_Y] != 0
    lowest, highest = slice(0, 8), slice(rows - 8, rows)
    tile_row = lax.broadcasted_iota(jnp.int32, (8, size_z), 0)
    end = WIDE + size_y

    def put(out, x, middle, ends):
        out[x, 0:WIDE, :] = ends[0:WIDE, :]
        for row_ in range(0, size_y, 8):
            out[x, WIDE + row_ : WIDE + row_ + 8, :] = middle(row_)
        out[x, end:rows, :] = ends[WIDE : 2 * WIDE, :]

    def halo(side, first, edge, present):
        message, ends = side
        for k in range(WIDE):
            x = first + k
            if k < early_planes:
                middle = lambda row_: message[1 + k, row_ : row_ + 8, :]
            else:
                tile = ends.shape[0] - (WIDE - k) * (size_y // 8)
                middle = lambda row_: ends[tile + row_ // 8]
            put(source, x, middle, ends.at[k])
            source[x] = inverse[x] * source[x]
            for row_, weight, line in ((WIDE, b1, k), (end - 1, inverse, WIDE + k)):
                at = slice(row_, row_ + 1)
                source[x, at] = source[x, at] + weight[x, at] * ends[WIDE + 1, line : line + 1, :]
        put(whole, edge, lambda row_: message[0, row_ : row_ + 8, :], ends.at[WIDE])
        whole[edge] = jnp.where(present, whole[edge], 0.0)

    def halos(low, high):
        halo(low, 0, 0, has_low_x)
        halo(high, WIDE + size_x, size_x + 1, has_high_x)

    by_side(flags[ODD_X], halos, early, late)

    for k in range(size_x):
        source[WIDE + k] = wide[k]

    low_in, high_in = WIDE, WIDE + size_x - 1
    source[low_in - 1] = source[low_in - 1] + inverse[low_in - 1] * sides[0]
    source[low_in] = source[low_in] + b0[low_in] * whole[0]
    source[high_in] = source[high_in] + inverse[high_in] * whole[size_x + 1]
    source[high_in + 1] = source[high_in + 1] + b0[high_in + 1] * sides[1]

    def run(planes, tile, inside, wanted):
        return chebyshev(
            planes,
            tile,
            inside,
            lambda x: source[x, tile],
            left,
            update,
            coefs,
            wanted,
        )

    everything = slice(0, rows)
    box_rows = (row >= WIDE - DEPTH) & (row < WIDE + size_y + DEPTH)
    box_planes = range(WIDE - DEPTH, WIDE + size_x + DEPTH)
    own_planes = range(WIDE, WIDE + size_x)
    inner = (row >= WIDE) & (row < WIDE + size_y)

    beside = run(range(0, WIDE + DEPTH), everything, box_rows, (WIDE - 1,))[WIDE - 1]
    whole[0] = jnp.where(has_low_x & inner, whole[0] + beside, 0.0)
    x = WIDE + size_x
    beside = run(range(span - WIDE - DEPTH, span), everything, box_rows, (x,))[x]
    whole[size_x + 1] = jnp.where(has_high_x & inner, whole[size_x + 1] + beside, 0.0)

    own = run(box_planes, everything, box_rows, tuple(own_planes))
    for k in range(size_x):
        whole[k + 1] = jnp.where(inner, corr[k] + own[WIDE + k], 0.0)

    beside = run(box_planes, lowest, tile_row < WIDE + DEPTH, tuple(own_planes))
    for k in range(size_x):
        line = past[0, k : k + 1, :] + beside[WIDE + k]
        here = has_low_y & (tile_row == WIDE - 1)
        whole[k + 1, lowest] = jnp.where(here, line, whole[k + 1, lowest])
    beside = run(box_planes, highest, tile_row >= 8 - WIDE - DEPTH, tuple(own_planes))
    for k in range(size_x):
        line = past[1, k : k + 1, :] + beside[WIDE + k]
        here = has_high_y & (tile_row == 8 - WIDE)
        whole[k + 1, highest] = jnp.where(here, line, whole[k + 1, highest])

    for k in range(size_x):
        x = WIDE + k
        terms = beside_terms(whole[k], whole[k + 1], whole[k + 2], x, everything, coefs)
        image = diagonal[k] * (whole[k + 1] - terms)
        image_out[k] = pltpu.roll(image, rows - WIDE, 0)[0:size_y]
        field_out[k] = pltpu.roll(whole[k + 1], rows - WIDE, 0)[0:size_y]


def dot_planes(left, right):
    total = left[0] * right[0]
    for x in range(1, left.shape[0]):
        total = total + left[x] * right[x]
    return total


def search_kernel(
    flags, wide, sides, past, odd_late, even_late, diagonal, own0, own1, own2, own3, corr, even_early, odd_early, vectors,
    right_side, search, image, out, halo0, halo1, halo2, halo3, stage, wide_vel, *scratch
):
    halos = (halo0, halo1, halo2, halo3)
    early, late = (even_early, odd_early), (even_late, odd_late)
    halo_coefficients(flags, early, late, halos, wide_vel)
    coefs = [Region(*pair) for pair in zip((own0, own1, own2, own3), halos)]
    smooth(flags, EARLY_FIRST, wide, sides, past, early, late, diagonal, coefs, corr, search, image, scratch)
    products = [dot_planes(right_side, right_side), dot_planes(right_side, image)]
    restrict(vectors, [image], products, flags, (out, stage))


def smoothed_kernel(
    flags, wide, sides, past, odd_late, even_late, diagonal, own0, own1, own2, own3, corr, even_early, odd_early, halo0,
    halo1, halo2, halo3, middle, smoothed, turned, out, *scratch
):
    early, late = (even_early, odd_early), (even_late, odd_late)
    coefs = [Region(*pair) for pair in zip((own0, own1, own2, own3), (halo0, halo1, halo2, halo3))]
    smooth(flags, WIDE, wide, sides, past, early, late, diagonal, coefs, corr, smoothed, turned, scratch)
    lane = lax.broadcasted_iota(jnp.int32, (1, LANES), 1)
    sums = jnp.zeros((1, LANES), F32)
    for k, total in enumerate((dot_planes(turned, middle), dot_planes(turned, turned))):
        total = jnp.sum(jnp.sum(total, axis=0, keepdims=True), axis=1, keepdims=True)
        sums = jnp.where(lane == k, total, sums)
    row = jnp.concatenate([jnp.zeros((1, LANES), F32), sums], axis=1)
    for k in range(out.shape[0]):
        out[k] = row


def last_kernel(flags, received, alpha, search, smoothed, middle, turned, solution_field, residual):
    sums = summed(received)
    omega = sums[:, 0:1] / sums[:, 1:2]
    step = alpha[0:1, 0:1]
    for x in range(search.shape[0]):
        solution_field[x] = step * search[x] + omega * smoothed[x]
        residual[x] = middle[x] - omega * turned[x]


def local(right_side, velocity, deflation, inverse_rows):
    size_x, size_y, size_z = right_side.shape
    vectors_count = deflation.shape[0]
    count_x, count_y = lax.axis_size("gx"), lax.axis_size("gy")
    count = count_x * count_y
    at_x, at_y = lax.axis_index("gx"), lax.axis_index("gy")
    kernel_call = functools.partial(call, vectors_count)
    x_pairs, y_pairs = pair_permutations(count_x, count_y)

    def swap(messages, pairs):
        odd = lax.ppermute(messages[1], AXES, pairs[1])
        return [lax.ppermute(messages[0], AXES, pairs[0]), odd]

    def share(row):
        return lax.all_to_all(row, AXES, 0, 0)

    rows = size_y + 2 * WIDE
    span = size_x + 2 * WIDE
    block = (size_x, size_y, size_z)
    row = pltpu.VMEM((count, 1, 2 * LANES), F32)
    stage = (2 * LANES, LANES)
    y_message = (size_x + size_x // WIDE + 2, WIDE, size_z)
    region = (span, rows, size_z)
    smooth_scratch = [region, region, (CHEB - 1,) + region, (size_x + 2, rows, size_z)]

    chunks = 8
    arguments = (right_side, deflation, velocity, inverse_rows)
    first_row, right_side, deflation, velocity, inverse_rows = kernel_call(
        first_kernel,
        [row] + [pltpu.VMEM(argument.shape, argument.dtype) for argument in arguments],
        [stage, pltpu.SemaphoreType.DMA((chunks + 3,))],
        *[pltpu.with_memory_space_constraint(argument, pltpu.HBM) for argument in arguments],
        micros=2.0,
        streamed=True,
    )
    first = share(first_row)
    faces_y = (3, size_x, WIDE, size_z)
    x_early = (WIDE + 1, size_y, size_z)
    x_early_first = (1 + EARLY_FIRST + 3 * WIDE, size_y, size_z)
    velocity_y = kernel_call(velocity_y_kernel, [faces_y] * 2, [], velocity, micros=0.01)
    after = velocity_y[0]
    velocity_y = swap(velocity_y, y_pairs)

    wide_own, wide_halo = (size_x, rows, size_z), (2 * WIDE, rows, size_z)

    def exchange(corr, rest, messages, corners, early_planes):
        tiles = WIDE + 2 + (3 * WIDE if corners else 0) + (WIDE - early_planes) * (size_y // 8)
        message = (tiles, 2 * WIDE, size_z)
        y_messages, early = swap(messages[:2], y_pairs), swap(messages[2:], x_pairs)
        *own, even, odd = kernel_call(
            functools.partial(extend_kernel, corners=corners, early_planes=early_planes),
            [wide_own, (2, rows, size_z), (2, size_x, size_z), message, message],
            [],
            rest,
            corr,
            *y_messages[::-1],
            velocity,
            *velocity_y,
            micros=0.01,
        )
        wide, *rest_own = own
        source, placed = kernel_call(ready_kernel, [wide_own] * 2, [], wide, coefs[1], corr, micros=0.01)
        return (source, *rest_own, *swap((even, odd), x_pairs)[::-1], *coefs, placed, *early)

    corr, rest, *messages = kernel_call(
        coarse_kernel,
        [block, block, y_message, y_message, x_early_first, x_early_first],
        [],
        first,
        inverse_rows,
        deflation,
        right_side,
        velocity,
        after,
        micros=1.4,
    )
    coefs = kernel_call(
        coefficients_kernel,
        [wide_own] * 5,
        [(3, size_x, rows, size_z)],
        velocity,
        *velocity_y,
        micros=0.01,
    )
    search, image, second_row, *halo_coefs = kernel_call(
        search_kernel,
        [block, block, row] + [wide_halo] * 4,
        [stage, (3, rows, size_z)] + smooth_scratch,
        *exchange(corr, rest, messages, True, EARLY_FIRST),
        deflation,
        right_side,
        micros=3.0,
    )
    second = share(second_row)
    corr, rest, middle, alpha, *messages = kernel_call(
        second_coarse_kernel,
        [block, block, block, (8, LANES), y_message, y_message, x_early, x_early],
        [],
        first,
        second,
        inverse_rows,
        deflation,
        right_side,
        image,
        velocity,
        micros=1.4,
    )
    smoothed, turned, third_row = kernel_call(
        smoothed_kernel,
        [block, block, row],
        smooth_scratch,
        *exchange(corr, rest, messages, False, WIDE),
        *halo_coefs,
        middle,
        micros=2.5,
    )
    third = share(third_row)
    return tuple(
        kernel_call(last_kernel, [block, block], [], third, alpha, search, smoothed, middle, turned, micros=1.4)
    )


def solution(mesh):
    return jax.shard_map(
        local,
        mesh=mesh,
        in_specs=(
            P("gx", "gy", None),
            P(None, "gx", "gy", None),
            P(None, "gx", "gy", None),
            P(("gx", "gy"), None),
        ),
        out_specs=(P("gx", "gy", None), P("gx", "gy", None)),
        check_vma=False,
    )
```
